32 devices in a mesh: pipe: 2 (over x), dp: 16 (over z, y, core).
Axes of the slice: x: 2, y: 2, z: 4, core: 2. Of those that a mesh axis runs over, the one named last changes fastest.
Arguments:
- embeddings: bfloat16 [2, 32768, 512], P('pipe', 'dp'), may hold values from -6 to 6
- cotangent: bfloat16 [32768, 512], P('dp'), may hold values from -6 to 6
- lengths: int32 [32, 17], P('dp'), may hold values from 20 to 100, as said below
- copy_index: int32 [32768], P('dp'), may hold values from 0 to 1023, as said below
- priority: int32 [32768], P('dp'), may hold values from 0 to 99, as said below
- hamming: int32 [32, 17], P('dp'), may hold values from 0 to 100, as said below
- self_in: bfloat16 [2, 512, 1536], P('pipe'), may hold values from -0.25 to 0.25
- self_out: bfloat16 [2, 512, 512], P('pipe'), may hold values from -0.75 to 0.75
- cross_weight: bfloat16 [2, 512, 1024], P('pipe'), may hold values from -0.375 to 0.375
- expand: bfloat16 [2, 512, 2048], P('pipe'), may hold values from -0.25 to 0.25
- contract: bfloat16 [2, 2048, 512], P('pipe'), may hold values from -0.125 to 0.125
- expand_bias: float32 [2, 2048], P('pipe'), may hold values from -1.75 to 1.75
- branch_bias: float32 [2, 3, 512], P('pipe'), may hold values from -1.75 to 1.75
- norm_gain: float32 [2, 3, 512], P('pipe'), may hold values from 0.5 to 1.5
- norm_shift: float32 [2, 3, 512], P('pipe'), may hold values from -0.625 to 0.625
Outputs:
- layer_out: float32 [2, 32768, 512], P('pipe', 'dp')
- embedding_grad: float32 [2, 32768, 512], P('pipe', 'dp')
- self_in_grad: float32 [2, 512, 1536], P('pipe')
- self_out_grad: float32 [2, 512, 512], P('pipe')
- cross_grad: float32 [2, 512, 1024], P('pipe')
- expand_grad: float32 [2, 512, 2048], P('pipe')
- contract_grad: float32 [2, 2048, 512], P('pipe')
- expand_bias_grad: float32 [2, 2048], P('pipe')
- branch_bias_grad: float32 [2, 3, 512], P('pipe')
- norm_gain_grad: float32 [2, 3, 512], P('pipe')
- norm_shift_grad: float32 [2, 3, 512], P('pipe')
The draws below stay inside these ranges and needn't reach their ends.
Inputs may be any that keep to these rules, and one draw needn't show every extreme that they name: Each row holds 17 sentences whose lengths sum to 1024; every row has a sentence of 100 tokens. `copy_index`: A position of a token of the same sentence, counted from the row's start; the first and last positions of each row copy themselves. `priority`: within each sentence the entries are 0 to its length minus 1, each once. `hamming`: entry j belongs to sentence j of the row and is at most that sentence's length; a sentence of 100 tokens has the count 100.
All inputs are finite; a program needn't handle non-finite values.
Results may differ from the reference program's by a relative error of at most 0.025.
Values may be sent and summed in bfloat16 or wider, within the bound.
No kernel may reach another device: no remote copies, remote signals or barrier semaphores. Data moves between devices by JAX's collectives and lax.ppermute only.
A program may use at most 384 MiB of HBM per device.

```python
import jax
import jax.numpy as jnp
from jax import lax

D = 512
HEADS = 8
FF = 2048
ROW_LEN = 1024
LEN_MIN = 20
LEN_MAX = 100
PAIRS = 8
REST = 64
SENTS = 17
ROWS = 32
TOKENS = 32768


def row_lengths(key):
    pair_key, order_key = jax.random.split(key)
    picks = jax.random.randint(pair_key, (ROWS, PAIRS), LEN_MIN, LEN_MAX + 1, dtype=jnp.int32)
    picks = picks.at[:, 0].set(LEN_MAX)
    partners = LEN_MIN + LEN_MAX - picks
    remainder = jnp.full((ROWS, 1), REST, dtype=jnp.int32)
    table = jnp.concatenate([picks, partners, remainder], axis=1)
    orders = jax.vmap(lambda single: jax.random.permutation(single, SENTS))(jax.random.split(order_key, ROWS))
    return jnp.take_along_axis(table, orders.astype(jnp.int32), axis=1).astype(jnp.int32)


def sentence_layout(lengths):
    ends = jnp.cumsum(lengths, axis=1, dtype=jnp.int32)
    places = jnp.arange(ROW_LEN, dtype=jnp.int32)
    segments = jnp.sum((places[None, :, None] >= ends[:, None, :]).astype(jnp.int32), axis=2, dtype=jnp.int32)
    starts = jnp.take_along_axis(ends - lengths, segments, axis=1)
    spans = jnp.take_along_axis(lengths, segments, axis=1)
    return (segments, starts, spans)


def draw_lengths(key, part):
    return row_lengths(key)


def draw_copy_index(key, part):
    lengths = row_lengths(key)
    key = jax.random.fold_in(key, 5)
    segments, starts, spans = sentence_layout(lengths)
    noise = jax.random.randint(key, (ROWS, ROW_LEN), 0, 1 << 20, dtype=jnp.int32)
    chosen = starts + noise % spans
    places = jnp.arange(ROW_LEN, dtype=jnp.int32)
    ends_mask = (places == 0) | (places == ROW_LEN - 1)
    chosen = jnp.where(ends_mask[None, :], places[None, :], chosen)
    return chosen.reshape(TOKENS).astype(jnp.int32)


def draw_priority(key, part):
    lengths = row_lengths(key)
    key = jax.random.fold_in(key, 7)
    segments, starts, spans = sentence_layout(lengths)
    places = jnp.arange(ROW_LEN, dtype=jnp.int32)
    noise = jax.random.randint(key, (ROWS, ROW_LEN), 0, 1024, dtype=jnp.int32)
    scores = segments * (1 << 20) + noise * 1024 + places[None, :]
    orders = jnp.argsort(scores, axis=1, stable=True).astype(jnp.int32)
    within = places[None, :] - starts

    def place_row(order_row, within_row):
        return jnp.zeros((ROW_LEN,), jnp.int32).at[order_row].set(within_row)
    return jax.vmap(place_row)(orders, within).reshape(TOKENS).astype(jnp.int32)


def draw_hamming(key, part):
    lengths = row_lengths(key)
    key = jax.random.fold_in(key, 9)
    noise = jax.random.randint(key, (ROWS, SENTS), 0, 1 << 20, dtype=jnp.int32)
    counts = noise % (lengths + 1)
    return jnp.where(lengths == LEN_MAX, lengths, counts).astype(jnp.int32)


def block_scale(key, extent, cuts, low, high):
    def one(axis_at, shards_of):
        steps = jax.random.uniform(jax.random.fold_in(jax.random.fold_in(key, 6), axis_at), (shards_of,), jnp.float32, low / len(cuts), high / len(cuts))
        return jnp.repeat(jnp.exp(steps), extent[axis_at] // shards_of).reshape((-1,) + (1,) * (len(extent) - axis_at - 1))

    factor_of = one(*cuts[0])
    for cut in cuts[1:]:
        factor_of = factor_of * one(*cut)
    return factor_of


def scatter_about(own_key, extent, scale, most, pieces=(), kind=jnp.bfloat16):
    level = block_scale(own_key, extent, pieces, -0.22, 0.18) if pieces else 1.0
    drawn = jax.random.normal(own_key, extent, jnp.float32) * scale * level
    return jnp.minimum(jnp.maximum(drawn, -most), most).astype(kind)


def setup_inputs(seed: int = 0) -> dict:
    seeds = jax.random.split(jax.random.key(seed), 16)
    return {
        "embeddings": scatter_about(seeds[0], (2, TOKENS, D), 1.0, 6.0, ((0, 2), (1, 16))),
        "cotangent": scatter_about(seeds[1], (TOKENS, D), 1.0, 6.0, ((0, 16),)),
        "lengths": draw_lengths(jax.random.fold_in(seeds[15], 71), 0),
        "copy_index": draw_copy_index(jax.random.fold_in(seeds[15], 71), 0),
        "priority": draw_priority(jax.random.fold_in(seeds[15], 71), 0),
        "hamming": draw_hamming(jax.random.fold_in(seeds[15], 71), 0),
        "self_in": scatter_about(seeds[6], (2, D, 3 * D), D ** -0.5, 0.25, ((0, 2),)),
        "self_out": scatter_about(seeds[7], (2, D, D), (D // 8) ** -0.5, 0.75, ((0, 2),)),
        "cross_weight": scatter_about(seeds[8], (2, D, 2 * D), (D // 2) ** -0.5, 0.375, ((0, 2),)),
        "expand": scatter_about(seeds[9], (2, D, FF), D ** -0.5, 0.25, ((0, 2),)),
        "contract": scatter_about(seeds[10], (2, FF, D), FF ** -0.5, 0.125, ((0, 2),)),
        "expand_bias": scatter_about(seeds[11], (2, FF), 0.3, 1.75, ((0, 2),), jnp.float32),
        "branch_bias": scatter_about(seeds[12], (2, 3, D), 0.3, 1.75, ((0, 2),), jnp.float32),
        "norm_gain": jnp.clip(1.0 + 0.1 * jax.random.normal(seeds[13], (2, 3, D), jnp.float32), 0.5, 1.5),
        "norm_shift": scatter_about(seeds[14], (2, 3, D), 0.1, 0.625, ((0, 2),), jnp.float32),
    }


PRECISION = lax.Precision.HIGHEST
EPSILON = 1e-05

@jax.custom_vjp
def low(v):
    return lax.optimization_barrier(v.astype(jnp.bfloat16)).astype(jnp.float32)

@jax.custom_vjp
def low_back(v):
    return v

def low_keep(v):
    return (low(v), None)

def low_pass(kept, grad):
    return (grad,)

def back_keep(v):
    return (v, None)

def back_low(kept, grad):
    return (low(grad),)
low.defvjp(low_keep, low_pass)
low_back.defvjp(back_keep, back_low)

def product(left, right):
    return jnp.dot(left, right, precision=PRECISION)

def layer_norm(value, gain, shift):
    center = lax.optimization_barrier(jnp.mean(value, axis=-1, keepdims=True))
    centered = value - center
    spread = lax.optimization_barrier(jnp.mean(centered * centered, axis=-1, keepdims=True))
    return centered * lax.rsqrt(spread + EPSILON) * gain + shift

def segment_of(length_row, width):
    ends = jnp.cumsum(length_row, dtype=jnp.int32)
    places = jnp.arange(width, dtype=jnp.int32)
    return lax.optimization_barrier(jnp.sum((places[:, None] >= ends[None, :]).astype(jnp.int32), axis=1, dtype=jnp.int32))

def attend(queries, keys, values, segments):
    length, width = queries.shape
    size = width // HEADS
    block = min(512, length)
    scale = size ** (-0.5)
    key_heads = keys.reshape(length, HEADS, size)
    value_heads = values.reshape(length, HEADS, size)
    query_blocks = queries.reshape(length // block, block, HEADS, size)
    segment_blocks = segments.reshape(length // block, block)

    def one_block(record):
        query_part, segment_part = record
        scores = low_back(jnp.einsum('qhd,khd->hqk', query_part, key_heads, precision=PRECISION) * scale)
        allowed = segment_part[:, None] == segments[None, :]
        scores = jnp.where(allowed[None], scores, -1e+30)
        highest = lax.optimization_barrier(jnp.max(scores, axis=-1, keepdims=True))
        raised = jnp.exp(scores - highest)
        shares = raised / lax.optimization_barrier(jnp.sum(raised, axis=-1, keepdims=True))
        mixed = jnp.einsum('hqk,khd->qhd', low(shares), value_heads, precision=PRECISION)
        return mixed.reshape(block, width)
    mixed = lax.map(jax.checkpoint(one_block), (query_blocks, segment_blocks))
    return low(low_back(mixed.reshape(length, width)))

def self_block(inputs, weight_in, weight_out, bias_out, segments):
    width = inputs.shape[1]
    joined = low(low_back(product(low(inputs), weight_in)))
    mixed = attend(joined[:, :width], joined[:, width:2 * width], joined[:, 2 * width:], segments)
    return low_back(product(mixed, weight_out)) + bias_out

def feed_forward(inputs, weight_in, bias_in, weight_out, bias_out):
    inner = low_back(product(low(inputs), weight_in) + bias_in)
    active = low(jax.nn.gelu(inner, approximate=True))
    return low_back(product(active, weight_out)) + bias_out

def encoder_row(params, source, length_row, copy_row):
    self_in, self_out, cross_weight, expand, contract, expand_bias, branch_bias, norm_gain, norm_shift = params
    width = source.shape[1]
    segments = segment_of(length_row, source.shape[0])
    entry = layer_norm(source, norm_gain[2], norm_shift[2])
    hidden = entry + self_block(entry, self_in, self_out, branch_bias[0], segments)
    hidden = layer_norm(hidden, norm_gain[0], norm_shift[0])
    hidden = hidden + feed_forward(hidden, expand, expand_bias, contract, branch_bias[1])
    memory = layer_norm(hidden, norm_gain[1], norm_shift[1])
    value_bias = jnp.concatenate([jnp.zeros((width,), jnp.float32), branch_bias[2]])
    states = low(low_back(product(low(memory), cross_weight) + value_bias))
    copied = low_back(jnp.take(source, copy_row, axis=0))
    return (memory, states, copied)

def decoder_row(params, target, states, copied, length_row, rank_row, count_row):
    self_in, self_out, cross_weight, expand, contract, expand_bias, branch_bias, norm_gain, norm_shift = params
    width = target.shape[1]
    segments = segment_of(length_row, target.shape[0])
    wanted = (count_row + 1) // 2
    picks = segments[:, None] == jnp.arange(count_row.shape[0], dtype=jnp.int32)[None, :]
    quota = lax.optimization_barrier(jnp.sum(jnp.where(picks, wanted[None, :], 0), axis=1, dtype=jnp.int32))
    glance = rank_row < quota
    start = jnp.where(glance[:, None], target, copied)
    hidden = start + self_block(start, self_in, self_out, branch_bias[0], segments)
    hidden = layer_norm(hidden, norm_gain[0], norm_shift[0])
    query = low(low_back(product(low(hidden), cross_weight[:, :width])))
    mixed = attend(query, states[:, :width], states[:, width:], segments)
    cross = low_back(product(mixed, cross_weight[:, width:])) + branch_bias[2]
    hidden = layer_norm(hidden + cross, norm_gain[1], norm_shift[1])
    hidden = hidden + feed_forward(hidden, expand, expand_bias, contract, branch_bias[1])
    return layer_norm(hidden, norm_gain[2], norm_shift[2])

def reference(embeddings, cotangent, lengths, copy_index, priority, hamming, self_in, self_out, cross_weight, expand, contract, expand_bias, branch_bias, norm_gain, norm_shift):
    stacked = tuple((weight.astype(jnp.float32) for weight in (self_in, self_out, cross_weight, expand, contract, expand_bias, branch_bias, norm_gain, norm_shift)))
    encoder_params = tuple((weight[0] for weight in stacked))
    decoder_params = tuple((weight[1] for weight in stacked))
    source = embeddings[0].astype(jnp.float32).reshape(ROWS, ROW_LEN, D)
    target = embeddings[1].astype(jnp.float32).reshape(ROWS, ROW_LEN, D)
    copies = copy_index.reshape(ROWS, ROW_LEN)
    ranks = priority.reshape(ROWS, ROW_LEN)

    def forward(first_params, second_params, source_rows, target_rows):

        def per_row(record):
            source_row, target_row, length_row, copy_row, rank_row, count_row = record
            memory, states, copied = encoder_row(first_params, source_row, length_row, copy_row)
            decoded = decoder_row(second_params, target_row, states, copied, length_row, rank_row, count_row)
            return (memory, decoded)
        return lax.map(jax.checkpoint(per_row), (source_rows, target_rows, lengths, copies, ranks, hamming))
    (memory, decoded), pullback = jax.vjp(forward, encoder_params, decoder_params, source, target)
    wanted = cotangent.astype(jnp.float32).reshape(ROWS, ROW_LEN, D)
    first_grads, second_grads, source_grad, target_grad = pullback((jnp.zeros_like(memory), wanted))
    layer_out = jnp.stack([memory.reshape(TOKENS, D), decoded.reshape(TOKENS, D)])
    embedding_grad = jnp.stack([source_grad.reshape(TOKENS, D), target_grad.reshape(TOKENS, D)])
    joined = tuple((jnp.stack([first, second]) for first, second in zip(first_grads, second_grads)))
    return (layer_out, embedding_grad, joined[0], joined[1], joined[2], joined[3], joined[4], joined[5], joined[6], joined[7], joined[8])
```

```python
import functools

import jax
import jax.numpy as jnp
from jax import lax
from jax.experimental import pallas as pl
from jax.experimental.pallas import tpu as pltpu
from jax.sharding import PartitionSpec as P

HEADS = 8
D = 512
FF = 2048
T = 1024
SENTS = 17
WIN = 128
EPSILON = 1e-05
NEG = -1e30
BF = jnp.bfloat16
F32 = jnp.float32
VMEM = pl.BlockSpec(memory_space=pltpu.VMEM)
SMEM = pl.BlockSpec(memory_space=pltpu.SMEM)
BLOCK = 256
STEPS = T // BLOCK


def nn(a, b):
    return jnp.dot(a, b, preferred_element_type=F32)


def nt(a, b):
    return lax.dot_general(a, b, (((1,), (1,)), ((), ())), preferred_element_type=F32)


def tn(a, b):
    return lax.dot_general(a, b, (((0,), (0,)), ((), ())), preferred_element_type=F32)


def normalized(value):
    center = jnp.mean(value, axis=-1, keepdims=True)
    centered = value - center
    spread = jnp.mean(centered * centered, axis=-1, keepdims=True)
    scale = lax.rsqrt(spread + EPSILON)
    return centered * scale, scale


def normalized_back(grad, unit, scale):
    first = jnp.mean(grad, axis=-1, keepdims=True)
    second = jnp.mean(grad * unit, axis=-1, keepdims=True)
    return scale * (grad - first - unit * second)


def folded(value):
    return jnp.sum(value.reshape(value.shape[0] // 8, 8, value.shape[1]), axis=0)


def column_sum(value):
    return jnp.sum(value, axis=0, keepdims=True)


def each_block(body):
    def step(index, carry):
        body(pl.ds(pl.multiple_of(index * BLOCK, BLOCK), BLOCK))
        return carry

    lax.fori_loop(0, STEPS, step, 0)


def each_chunk(count, size, body):
    def step(index, carry):
        body(pl.multiple_of(index * size, size))
        return carry

    lax.fori_loop(0, count, step, 0)


def kernel_call(body, outs, operands, scalars=0, scratch=(), out_specs=None, flops=0):
    size = sum(x.size * x.dtype.itemsize for x in operands)
    size += sum(x.size * x.dtype.itemsize for x in outs)
    return pl.pallas_call(
        body,
        out_shape=tuple(outs),
        in_specs=[SMEM] * scalars + [VMEM] * (len(operands) - scalars),
        out_specs=tuple(out_specs) if out_specs else (VMEM,) * len(outs),
        scratch_shapes=list(scratch),
        compiler_params=pltpu.CompilerParams(vmem_limit_bytes=56 << 20),
        cost_estimate=pl.CostEstimate(flops=flops, bytes_accessed=size, transcendentals=0),
    )(*operands)


def shaped(rows, columns, kind):
    return jax.ShapeDtypeStruct((rows, columns), kind)


def layout_kernel(lengths, hamming, priority, copies, table, bias, glance, places):
    ends = []
    total = jnp.int32(0)
    for j in range(SENTS):
        total = total + lengths[0, j]
        ends.append(total)
    count = jnp.int32(0)
    first = jnp.int32(0)

    def origin(start):
        return jnp.minimum((start // 16) * 16, T - WIN)

    starts_at = []
    for j in range(SENTS):
        begin = jnp.int32(0) if j == 0 else ends[j - 1]
        opens = (ends[j] - origin(first)) > WIN
        if j == 0:
            opens = jnp.bool_(False)
        first = jnp.where(opens, begin, first)
        count = jnp.where(opens, count + 1, count)
        table[0, 1 + count] = origin(first)
        table[0, 32 + count] = first
        table[0, 64 + count] = ends[j]
    table[0, 0] = count + 1

    lanes = lax.broadcasted_iota(jnp.int32, (8, WIN), 1)
    rows = lax.broadcasted_iota(jnp.int32, (8, WIN), 0)
    place = rows * WIN + lanes
    quota = jnp.zeros((8, WIN), jnp.int32) + (hamming[0, 0] + 1) // 2
    for j in range(SENTS - 1):
        change = (hamming[0, j + 1] + 1) // 2 - (hamming[0, j] + 1) // 2
        quota = quota + jnp.where(place >= ends[j], change, 0)
    chosen = jnp.where(priority[...] < quota, 1.0, 0.0)
    copy = copies[...].astype(F32)
    for i in range(T // WIN):
        part = pl.ds(i * WIN, WIN)
        glance[part, :] = jnp.broadcast_to(chosen[i : i + 1, :], (WIN, WIN)).T
        places[part, :] = jnp.broadcast_to(copy[i : i + 1, :], (WIN, WIN)).T.astype(jnp.int32)

    def window(w, carry):
        at = table[0, 1 + w]
        here = lanes + at
        segment = jnp.zeros((8, WIN), F32)
        for j in range(SENTS):
            segment = segment + jnp.where(here >= ends[j], 1.0, 0.0)
        inside = (here >= table[0, 32 + w]) & (here < table[0, 64 + w])
        segment = jnp.where(inside, segment, -1.0)
        across = jnp.broadcast_to(segment[0:1, :], (WIN, WIN))
        down = across.T
        bias[w] = jnp.where((across == down) & (across >= 0.0), 0.0, NEG)
        return carry

    lax.fori_loop(0, count + 1, window, 0)


def row_layout(lengths, hamming, priority, copies):
    outs = (
        shaped(1, 128, jnp.int32),
        jax.ShapeDtypeStruct((SENTS, WIN, WIN), F32),
        shaped(T, WIN, F32),
        shaped(T, WIN, jnp.int32),
    )
    return kernel_call(
        layout_kernel,
        outs,
        (lengths, hamming, priority, copies),
        scalars=2,
        out_specs=(SMEM, VMEM, VMEM, VMEM),
    )


def pair_halves(part):
    low = lax.broadcasted_iota(jnp.int32, (WIN, WIN), 1) < 64
    zero = jnp.zeros_like(part)
    return jnp.concatenate([jnp.where(low, part, zero), jnp.where(low, zero, part)], axis=0)


def pair_join(both):
    low = lax.broadcasted_iota(jnp.int32, (WIN, WIN), 1) < 64
    return jnp.where(low, both[:WIN], both[WIN:])


def attend(table, bias, queries, keys, values, mixed, stats):
    def window(w, carry):
        at = pl.ds(pl.multiple_of(table[0, 1 + w], 16), WIN)
        masked = bias[w]
        masked = jnp.concatenate([masked, masked], axis=1)
        for pair in range(HEADS // 2):
            lanes = slice(pair * 128, pair * 128 + 128)
            query = pair_halves(queries[at, lanes])
            scores = nt(keys[at, lanes], query) + masked
            highest = jnp.maximum(jnp.max(scores, axis=0, keepdims=True), -1e29)
            raised = jnp.exp(scores - highest)
            inverse = 1.0 / jnp.maximum(jnp.sum(raised, axis=0, keepdims=True), 1e-30)
            shares = (raised * inverse).astype(BF)
            stats[w * 4 + pair, 0:1, :] = highest
            stats[w * 4 + pair, 1:2, :] = inverse
            out = pair_join(tn(shares, values[at, lanes])).astype(BF)
            mixed[at, lanes] = mixed[at, lanes] + out
        return carry

    mixed[...] = jnp.zeros_like(mixed)
    lax.fori_loop(0, table[0, 0], window, 0)


def attend_back(table, bias, queries, keys, values, stats, grad, grad_q, grad_k, grad_v):
    def window(w, carry):
        at = pl.ds(pl.multiple_of(table[0, 1 + w], 16), WIN)
        masked = bias[w]
        masked = jnp.concatenate([masked, masked], axis=1)
        for pair in range(HEADS // 2):
            lanes = slice(pair * 128, pair * 128 + 128)
            query = pair_halves(queries[at, lanes])
            key = keys[at, lanes]
            scores = nt(key, query) + masked
            shares = jnp.exp(scores - stats[w * 4 + pair, 0:1, :]) * stats[w * 4 + pair, 1:2, :]
            out = pair_halves(grad[at, lanes])
            back = nt(values[at, lanes], out)
            grad_v[at, lanes] = grad_v[at, lanes] + nn(shares.astype(BF), out).astype(BF)
            total = jnp.sum(shares * back, axis=0, keepdims=True)
            scored = (shares * (back - total)).astype(BF)
            grad_k[at, lanes] = grad_k[at, lanes] + nn(scored, query).astype(BF)
            asked = pair_join(tn(scored, key)) * 0.125
            grad_q[at, lanes] = grad_q[at, lanes] + asked.astype(BF)
        return carry

    for ref in (grad_q, grad_k, grad_v):
        ref[...] = jnp.zeros_like(ref)
    lax.fori_loop(0, table[0, 0], window, 0)


STATS = jax.ShapeDtypeStruct((SENTS * 4, 2, 2 * WIN), F32)


def thirds(ref):
    return tuple(ref.at[:, i * D : (i + 1) * D] for i in range(ref.shape[1] // D))


def self_tail(x, weight_out, bias, mixed, z):
    def after(at):
        z[at, :] = x[at, :].astype(F32) + nn(mixed[at, :], weight_out[...]) + bias[0:1, :]

    each_block(after)


def project(x, weight_in, joined, at):
    got = nn(x, weight_in[...])
    joined[at, :D] = (got[:, :D] * 0.125).astype(BF)
    joined[at, D:] = got[:, D:].astype(BF)


def encoder_self_kernel(
    table, bias, source, weight_in, weight_out, branch, gain, shift, joined, mixed, stats, z, x
):
    def before(at):
        unit, _ = normalized(source[at, :].astype(F32))
        value = unit * gain[2:3, :] + shift[2:3, :]
        x[at, :] = value
        project(value.astype(BF), weight_in, joined, at)

    each_block(before)
    attend(table, bias, *thirds(joined), mixed, stats)
    self_tail(x, weight_out, branch, mixed, z)


def decoder_self_kernel(
    table, bias, source, target, glance, places, weight_in, weight_out, branch, x, joined, mixed, stats, z, copied
):
    copied[...] = jnp.zeros_like(copied)

    def window(w, carry):
        start = pl.multiple_of(table[0, 1 + w], 16)
        at = pl.ds(start, WIN)
        lanes = lax.broadcasted_iota(jnp.int32, (WIN, WIN), 1) + start
        allowed = jnp.min(bias[w], axis=1, keepdims=True)
        inside = jnp.max(bias[w], axis=1, keepdims=True) == 0.0
        hit = jnp.where((places[at, :] == lanes) & inside, 1.0, 0.0).astype(BF)
        copied[at, :] = copied[at, :] + nn(hit, source[at, :]).astype(BF)
        return carry

    lax.fori_loop(0, table[0, 0], window, 0)

    def before(at):
        kept = jnp.concatenate([glance[at, :]] * 4, axis=1) > 0.5
        value = jnp.where(kept, target[at, :].astype(F32), copied[at, :].astype(F32)).astype(BF)
        x[at, :] = value
        project(value, weight_in, joined, at)

    each_block(before)
    attend(table, bias, *thirds(joined), mixed, stats)
    self_tail(x, weight_out, branch, mixed, z)


FLOP_UNIT = 2 * T * D * D


def encoder_self(table, bias, source, weights, small):
    outs = (shaped(T, 3 * D, BF), shaped(T, D, BF), STATS, shaped(T, D, F32))
    return kernel_call(
        encoder_self_kernel,
        outs,
        (table, bias, source, weights["self_in"], weights["self_out"], small["branch_bias"], small["norm_gain"], small["norm_shift"]),
        scalars=1,
        scratch=[pltpu.VMEM((T, D), F32)],
        flops=8 * FLOP_UNIT,
    )


def decoder_self(table, bias, source, target, glance, places, weights, small):
    outs = (shaped(T, D, BF), shaped(T, 3 * D, BF), shaped(T, D, BF), STATS, shaped(T, D, F32))
    return kernel_call(
        decoder_self_kernel,
        outs,
        (table, bias, source, target, glance, places, weights["self_in"], weights["self_out"], small["branch_bias"]),
        scalars=1,
        scratch=[pltpu.VMEM((T, D), BF)],
        flops=8 * FLOP_UNIT,
    )


ROOT = 0.7978845608028654
CUBE = 0.044715


def gelu_parts(u):
    square = u * u
    bent = jnp.tanh(u * (ROOT + ROOT * CUBE * square))
    half = 0.5 + 0.5 * bent
    slope = half + (0.5 * u) * (1.0 - bent * bent) * (ROOT + 3.0 * ROOT * CUBE * square)
    return u * half, slope


def expand_block(value, expand, expand_bias, active, slope, at):
    for j in range(FF // D):
        cols = slice(j * D, (j + 1) * D)
        act, bend = gelu_parts(nn(value, expand[:, cols]) + expand_bias[0:1, cols])
        active[at, cols] = act.astype(BF)
        slope[at, cols] = bend.astype(BF)


def encoder_ff_kernel(z1, expand, expand_bias, contract, cross, branch, gain, shift, active, slope, z2, memory, states):
    def block(at):
        unit, _ = normalized(z1[at, :])
        value = unit * gain[0:1, :] + shift[0:1, :]
        expand_block(value.astype(BF), expand, expand_bias, active, slope, at)
        total = value + nn(active[at, :], contract[...]) + branch[1:2, :]
        z2[at, :] = total
        unit, _ = normalized(total)
        out = unit * gain[1:2, :] + shift[1:2, :]
        memory[at, :] = out
        got = nn(out.astype(BF), cross[...])
        states[at, :D] = got[:, :D].astype(BF)
        states[at, D:] = (got[:, D:] + branch[2:3, :]).astype(BF)

    each_block(block)


def encoder_ff(z1, weights, small):
    outs = (shaped(T, FF, BF), shaped(T, FF, BF), shaped(T, D, F32), shaped(T, D, F32), shaped(T, 2 * D, BF))
    return kernel_call(
        encoder_ff_kernel,
        outs,
        (z1, weights["expand"], small["expand_bias"], weights["contract"], weights["cross_weight"], small["branch_bias"], small["norm_gain"], small["norm_shift"]),
        flops=10 * FLOP_UNIT,
    )


def weight_grads(x, y, out, row, columns):
    for c in range(columns):
        out[row + c * D : row + (c + 1) * D, :] = tn(x[...], y[:, c * D : (c + 1) * D]).astype(BF)


def ff_back(dzb, value_b, active, slope, expand, contract, inner, grads):
    def block(at):
        for j in range(FF // D):
            cols = slice(j * D, (j + 1) * D)
            back = nt(dzb[at, :], contract[cols, :])
            inner[at, cols] = (back * slope[at, cols].astype(F32)).astype(BF)

    each_block(block)
    for c in range(FF // D):
        cols = slice(c * D, (c + 1) * D)
        grads[FF + c * D : FF + (c + 1) * D, :] = tn(active[:, cols], dzb[...]).astype(BF)
        grads[c * D : (c + 1) * D, :] = tn(value_b[...], inner[:, cols]).astype(BF)


def decoder_ff_kernel(
    z2, expand, expand_bias, contract, branch, gain, shift, cotangent,
    decoded, grads, bias_grads, ff_bias_grad, dz2,
    active, slope, inner, value_b, dz, dzb,
):
    bias_grads[...] = jnp.zeros_like(bias_grads)

    def block(at):
        unit, _ = normalized(z2[at, :])
        value = unit * gain[1:2, :] + shift[1:2, :]
        value_b[at, :] = value.astype(BF)
        expand_block(value.astype(BF), expand, expand_bias, active, slope, at)
        total = value + nn(active[at, :], contract[...]) + branch[1:2, :]
        unit, scale = normalized(total)
        decoded[at, :] = unit * gain[2:3, :] + shift[2:3, :]
        wanted = cotangent[at, :].astype(F32)
        bias_grads[0:1, :] += column_sum(wanted * unit)
        bias_grads[1:2, :] += column_sum(wanted)
        back = normalized_back(wanted * gain[2:3, :], unit, scale)
        bias_grads[2:3, :] += column_sum(back)
        dz[at, :] = back
        dzb[at, :] = back.astype(BF)

    each_block(block)
    ff_back(dzb, value_b, active, slope, expand, contract, inner, grads)
    ff_bias_grad[...] = jnp.zeros_like(ff_bias_grad)

    def last(at):
        ff_bias_grad[0:1, :] += column_sum(inner[at, :].astype(F32))
        back = dz[at, :] + nt(inner[at, :], expand[...])
        unit, scale = normalized(z2[at, :])
        bias_grads[3:4, :] += column_sum(back * unit)
        bias_grads[4:5, :] += column_sum(back)
        dz2[at, :] = normalized_back(back * gain[1:2, :], unit, scale)

    each_block(last)


def decoder_ff(z2, cotangent, weights, small):
    outs = (shaped(T, D, F32), shaped(2 * FF, D, BF), shaped(8, D, F32), shaped(8, FF, F32), shaped(T, D, F32))
    return kernel_call(
        decoder_ff_kernel,
        outs,
        (z2, weights["expand"], small["expand_bias"], weights["contract"], small["branch_bias"], small["norm_gain"], small["norm_shift"], cotangent),
        scratch=[
            pltpu.VMEM((T, FF), BF),
            pltpu.VMEM((T, FF), BF),
            pltpu.VMEM((T, FF), BF),
            pltpu.VMEM((T, D), BF),
            pltpu.VMEM((T, D), F32),
            pltpu.VMEM((T, D), BF),
        ],
        flops=24 * FLOP_UNIT,
    )


def encoder_ff_back_kernel(
    dstates, z1, z2, active, slope, expand, contract, cross, gain, shift,
    cross_grads, grads, bias_grads, ff_bias_grad, dz1,
    inner, value_b, memory_b, dz, dzb,
):
    bias_grads[...] = jnp.zeros_like(bias_grads)

    def block(at):
        unit, scale = normalized(z2[at, :])
        memory_b[at, :] = (unit * gain[1:2, :] + shift[1:2, :]).astype(BF)
        back = nt(dstates[at, :], cross[...])
        bias_grads[0:1, :] += column_sum(dstates[at, D:].astype(F32))
        bias_grads[1:2, :] += column_sum(back * unit)
        bias_grads[2:3, :] += column_sum(back)
        back = normalized_back(back * gain[1:2, :], unit, scale)
        bias_grads[3:4, :] += column_sum(back)
        dz[at, :] = back
        dzb[at, :] = back.astype(BF)
        unit, _ = normalized(z1[at, :])
        value_b[at, :] = (unit * gain[0:1, :] + shift[0:1, :]).astype(BF)

    each_block(block)
    weight_grads(memory_b, dstates, cross_grads, 0, 2)
    ff_back(dzb, value_b, active, slope, expand, contract, inner, grads)
    ff_bias_grad[...] = jnp.zeros_like(ff_bias_grad)

    def last(at):
        ff_bias_grad[0:1, :] += column_sum(inner[at, :].astype(F32))
        back = dz[at, :] + nt(inner[at, :], expand[...])
        unit, scale = normalized(z1[at, :])
        bias_grads[4:5, :] += column_sum(back * unit)
        bias_grads[5:6, :] += column_sum(back)
        dz1[at, :] = normalized_back(back * gain[0:1, :], unit, scale)

    each_block(last)


def encoder_ff_back(dstates, z1, z2, active, slope, weights, small):
    outs = (shaped(2 * D, D, BF), shaped(2 * FF, D, BF), shaped(8, D, F32), shaped(8, FF, F32), shaped(T, D, F32))
    return kernel_call(
        encoder_ff_back_kernel,
        outs,
        (dstates, z1, z2, active, slope, weights["expand"], weights["contract"], weights["cross_weight"], small["norm_gain"], small["norm_shift"]),
        scratch=[
            pltpu.VMEM((T, FF), BF),
            pltpu.VMEM((T, D), BF),
            pltpu.VMEM((T, D), BF),
            pltpu.VMEM((T, D), F32),
            pltpu.VMEM((T, D), BF),
        ],
        flops=20 * FLOP_UNIT,
    )


def decoder_cross_kernel(table, bias, z1, states, weight, branch, gain, shift, queries, mixed, stats, z2, x):
    def before(at):
        unit, _ = normalized(z1[at, :])
        value = unit * gain[0:1, :] + shift[0:1, :]
        x[at, :] = value
        queries[at, :] = (nn(value.astype(BF), weight[:, :D]) * 0.125).astype(BF)

    each_block(before)
    attend(table, bias, queries, *thirds(states), mixed, stats)

    def after(at):
        z2[at, :] = x[at, :] + nn(mixed[at, :], weight[:, D:]) + branch[2:3, :]

    each_block(after)


def decoder_cross(table, bias, z1, states, weights, small):
    outs = (shaped(T, D, BF), shaped(T, D, BF), STATS, shaped(T, D, F32))
    return kernel_call(
        decoder_cross_kernel,
        outs,
        (table, bias, z1, states, weights["cross_weight"], small["branch_bias"], small["norm_gain"], small["norm_shift"]),
        scalars=1,
        scratch=[pltpu.VMEM((T, D), F32)],
        flops=6 * FLOP_UNIT,
    )


def decoder_cross_back_kernel(
    table, bias, dz2, z1, queries, states, mixed, stats, weight, gain, shift,
    grads, bias_grads, dstates, dz1,
    value_b, dzb, out, dq,
):
    bias_grads[...] = jnp.zeros_like(bias_grads)

    def before(at):
        bias_grads[0:1, :] += column_sum(dz2[at, :])
        low = dz2[at, :].astype(BF)
        dzb[at, :] = low
        out[at, :] = nt(low, weight[:, D:]).astype(BF)
        unit, _ = normalized(z1[at, :])
        value_b[at, :] = (unit * gain[0:1, :] + shift[0:1, :]).astype(BF)

    each_block(before)
    attend_back(table, bias, queries, *thirds(states), stats, out, dq, *thirds(dstates))
    grads[:D, :] = tn(value_b[...], dq[...]).astype(BF)
    grads[D:, :] = tn(mixed[...], dzb[...]).astype(BF)

    def after(at):
        back = dz2[at, :] + nt(dq[at, :], weight[:, :D])
        unit, scale = normalized(z1[at, :])
        bias_grads[1:2, :] += column_sum(back * unit)
        bias_grads[2:3, :] += column_sum(back)
        dz1[at, :] = normalized_back(back * gain[0:1, :], unit, scale)

    each_block(after)


def decoder_cross_back(table, bias, dz2, z1, queries, states, mixed, stats, weights, small):
    outs = (shaped(2 * D, D, BF), shaped(8, D, F32), shaped(T, 2 * D, BF), shaped(T, D, F32))
    return kernel_call(
        decoder_cross_back_kernel,
        outs,
        (table, bias, dz2, z1, queries, states, mixed, stats, weights["cross_weight"], small["norm_gain"], small["norm_shift"]),
        scalars=1,
        scratch=[pltpu.VMEM((T, D), BF)] * 4,
        flops=12 * FLOP_UNIT,
    )


def self_back(table, bias, dz, x, joined, mixed, stats, weight_in, weight_out, grads, bias_grads, dzb, out, djoined):
    def before(at):
        bias_grads[0:1, :] += column_sum(dz[at, :])
        low = dz[at, :].astype(BF)
        dzb[at, :] = low
        out[at, :] = nt(low, weight_out[...]).astype(BF)

    each_block(before)
    attend_back(table, bias, *thirds(joined), stats, out, *thirds(djoined))
    weight_grads(x, djoined, grads, 0, 3)
    grads[3 * D :, :] = tn(mixed[...], dzb[...]).astype(BF)


def decoder_self_back_kernel(
    table, bias, dz, x, joined, mixed, stats, glance, places, weight_in, weight_out,
    grads, bias_grads, target_grad, source_grad,
    dzb, out, djoined, dcopied,
):
    bias_grads[...] = jnp.zeros_like(bias_grads)
    self_back(table, bias, dz, x, joined, mixed, stats, weight_in, weight_out, grads, bias_grads, dzb, out, djoined)

    def after(at):
        back = dz[at, :] + nt(djoined[at, :], weight_in[...])
        kept = jnp.concatenate([glance[at, :]] * 4, axis=1) > 0.5
        target_grad[at, :] = jnp.where(kept, back, 0.0)
        dcopied[at, :] = jnp.where(kept, 0.0, back).astype(BF)

    each_block(after)
    source_grad[...] = jnp.zeros_like(source_grad)

    def window(w, carry):
        start = pl.multiple_of(table[0, 1 + w], 16)
        at = pl.ds(start, WIN)
        lanes = lax.broadcasted_iota(jnp.int32, (WIN, WIN), 1) + start
        inside = jnp.max(bias[w], axis=1, keepdims=True) == 0.0
        hit = jnp.where((places[at, :] == lanes) & inside, 1.0, 0.0).astype(BF)
        source_grad[at, :] = source_grad[at, :] + tn(hit, dcopied[at, :])
        return carry

    lax.fori_loop(0, table[0, 0], window, 0)


def decoder_self_back(table, bias, dz, x, joined, mixed, stats, glance, places, weights):
    outs = (shaped(4 * D, D, BF), shaped(8, D, F32), shaped(T, D, F32), shaped(T, D, F32))
    return kernel_call(
        decoder_self_back_kernel,
        outs,
        (table, bias, dz, x, joined, mixed, stats, glance, places, weights["self_in"], weights["self_out"]),
        scalars=1,
        scratch=[pltpu.VMEM((T, D), BF), pltpu.VMEM((T, D), BF), pltpu.VMEM((T, 3 * D), BF), pltpu.VMEM((T, D), BF)],
        flops=16 * FLOP_UNIT,
    )


def encoder_self_back_kernel(
    table, bias, dz, source, joined, mixed, stats, copies_grad, weight_in, weight_out, gain, shift,
    grads, bias_grads, source_grad,
    x, dzb, out, djoined,
):
    bias_grads[...] = jnp.zeros_like(bias_grads)

    def first(at):
        unit, _ = normalized(source[at, :].astype(F32))
        x[at, :] = (unit * gain[2:3, :] + shift[2:3, :]).astype(BF)

    each_block(first)
    self_back(table, bias, dz, x, joined, mixed, stats, weight_in, weight_out, grads, bias_grads, dzb, out, djoined)

    def after(at):
        back = dz[at, :] + nt(djoined[at, :], weight_in[...])
        unit, scale = normalized(source[at, :].astype(F32))
        bias_grads[1:2, :] += column_sum(back * unit)
        bias_grads[2:3, :] += column_sum(back)
        source_grad[at, :] = normalized_back(back * gain[2:3, :], unit, scale) + copies_grad[at, :]

    each_block(after)


def encoder_self_back(table, bias, dz, source, joined, mixed, stats, copies_grad, weights, small):
    outs = (shaped(4 * D, D, BF), shaped(8, D, F32), shaped(T, D, F32))
    return kernel_call(
        encoder_self_back_kernel,
        outs,
        (table, bias, dz, source, joined, mixed, stats, copies_grad, weights["self_in"], weights["self_out"], small["norm_gain"], small["norm_shift"]),
        scalars=1,
        scratch=[pltpu.VMEM((T, D), BF), pltpu.VMEM((T, D), BF), pltpu.VMEM((T, D), BF), pltpu.VMEM((T, 3 * D), BF)],
        flops=16 * FLOP_UNIT,
    )


def row_pass(source, target, cotangent, lengths, hamming, priority, copies, encoder, decoder, enc_small, dec_small):
    table, bias, glance, places = row_layout(lengths, hamming, priority, copies)
    e_joined, e_mixed, e_stats, e_z1 = encoder_self(table, bias, source, encoder, enc_small)
    x, d_joined, d_mixed, d_stats, d_z1 = decoder_self(table, bias, source, target, glance, places, decoder, dec_small)
    active, slope, e_z2, memory, states = encoder_ff(e_z1, encoder, enc_small)
    queries, c_mixed, c_stats, d_z2 = decoder_cross(table, bias, d_z1, states, decoder, dec_small)
    decoded, d_ff, d_ff_bias, d_ex_bias, dz2 = decoder_ff(d_z2, cotangent, decoder, dec_small)
    d_cross, d_cross_bias, dstates, dz1 = decoder_cross_back(table, bias, dz2, d_z1, queries, states, c_mixed, c_stats, decoder, dec_small)
    d_self, d_self_bias, target_grad, copies_grad = decoder_self_back(table, bias, dz1, x, d_joined, d_mixed, d_stats, glance, places, decoder)
    e_cross, e_ff, e_ff_bias, e_ex_bias, e_dz1 = encoder_ff_back(dstates, e_z1, e_z2, active, slope, encoder, enc_small)
    e_self, e_self_bias, source_grad = encoder_self_back(table, bias, e_dz1, source, e_joined, e_mixed, e_stats, copies_grad, encoder, enc_small)
    enc_rows = jnp.concatenate(
        [
            e_ex_bias[0:1].reshape(4, D),
            e_self_bias[0:1], e_ff_bias[3:4], e_ff_bias[0:1],
            e_ff_bias[4:5], e_ff_bias[1:2], e_self_bias[1:2],
            e_ff_bias[5:6], e_ff_bias[2:3], e_self_bias[2:3],
            jnp.zeros((3, D), F32),
        ],
        axis=0,
    )
    dec_rows = jnp.concatenate(
        [
            d_ex_bias[0:1].reshape(4, D),
            d_self_bias[0:1], d_ff_bias[2:3], d_cross_bias[0:1],
            d_cross_bias[1:2], d_ff_bias[3:4], d_ff_bias[0:1],
            d_cross_bias[2:3], d_ff_bias[4:5], d_ff_bias[1:2],
            jnp.zeros((3, D), F32),
        ],
        axis=0,
    )
    enc_grads = (e_ff, e_cross, e_self, enc_rows)
    dec_grads = (d_ff, d_cross, d_self, dec_rows)
    return memory, decoded, source_grad, target_grad, enc_grads, dec_grads


def swapped(value, axis, bit):
    count = lax.axis_size(axis)
    return lax.ppermute(value, axis, [(i, i ^ (1 << bit)) for i in range(count)])


def parted(value, bit):
    half = value.shape[0] // 2
    kept = lax.dynamic_slice_in_dim(value, bit * half, half, 0)
    sent = lax.dynamic_slice_in_dim(value, (1 - bit) * half, half, 0)
    return kept, sent


def joined_halves(own, other, bit):
    return jnp.where(bit == 0, jnp.concatenate([own, other], 0), jnp.concatenate([other, own], 0))


def summed(enc, dec, leading):
    index = lax.axis_index("dp")
    bits = (lax.axis_size("dp") - 1).bit_length()
    for b in range(bits):
        bit = (index >> b) & 1
        out = []
        for value in (enc, dec):
            kept, sent = parted(value, bit)
            got = swapped(sent, "dp", b)
            out.append((kept.astype(F32) + got.astype(F32)).astype(BF))
        enc, dec = out
    kept = jnp.where(leading, enc, dec)
    sent = jnp.where(leading, dec, enc)
    got = swapped(sent, "pipe", 0)
    total = (kept.astype(F32) + got.astype(F32)).astype(BF)
    for b in reversed(range(bits)):
        bit = (index >> b) & 1
        total = joined_halves(total, swapped(total, "dp", b), bit)
    return total


NAMES = ("self_in", "self_out", "expand", "contract", "cross_weight")


def per_device(
    embeddings, cotangent, lengths, copy_index, priority, hamming,
    self_in, self_out, cross_weight, expand, contract,
    expand_bias, branch_bias, norm_gain, norm_shift,
):
    pipe = lax.axis_index("pipe")
    leading = pipe == 0
    core = lax.axis_index("dp") & 1
    own_rows = embeddings[0]
    mine, theirs = parted(own_rows, pipe)
    got = swapped(theirs, "pipe", 0)
    source = jnp.where(leading, mine, got)
    target = jnp.where(leading, got, mine)

    big = {
        "self_in": self_in[0], "self_out": self_out[0], "cross_weight": cross_weight[0],
        "expand": expand[0], "contract": contract[0],
    }
    small = {
        "expand_bias": expand_bias, "branch_bias": branch_bias[0],
        "norm_gain": norm_gain[0], "norm_shift": norm_shift[0],
    }
    encoder, decoder = {}, {}
    for name in NAMES:
        own = big[name]
        kept, _ = parted(own, core)
        half = swapped(kept, "pipe", 0)
        other = joined_halves(half, swapped(half, "dp", 0), core)
        encoder[name] = jnp.where(leading, own, other)
        decoder[name] = jnp.where(leading, other, own)
    packed = jnp.concatenate([small["expand_bias"].reshape(4, D), small["branch_bias"], small["norm_gain"], small["norm_shift"]], 0)
    packed_other = swapped(packed, "pipe", 0)
    enc_packed = jnp.where(leading, packed, packed_other)
    dec_packed = jnp.where(leading, packed_other, packed)

    def unpacked(rows):
        return {
            "expand_bias": rows[:4].reshape(1, FF), "branch_bias": rows[4:7],
            "norm_gain": rows[7:10], "norm_shift": rows[10:13],
        }

    def own_half(value):
        return parted(value, pipe)[0]

    memory, decoded, source_grad, target_grad, enc_grads, dec_grads = row_pass(
        source, target, own_half(cotangent),
        own_half(lengths), own_half(hamming),
        own_half(priority).reshape(T // WIN, WIN), own_half(copy_index).reshape(T // WIN, WIN),
        encoder, decoder, unpacked(enc_packed), unpacked(dec_packed),
    )

    def rows_out(first, second):
        sent = jnp.where(leading, second, first).astype(BF)
        kept = jnp.where(leading, first, second)
        got = swapped(sent, "pipe", 0).astype(F32)
        return joined_halves(kept, got, pipe)[None]

    layer_out = rows_out(memory, decoded)
    embedding_grad = rows_out(source_grad, target_grad)

    ff = summed(enc_grads[0], dec_grads[0], leading)
    rest_enc = jnp.concatenate([enc_grads[1], enc_grads[2]], 0)
    rest_dec = jnp.concatenate([dec_grads[1], dec_grads[2]], 0)
    rest = summed(rest_enc, rest_dec, leading)
    rows = jnp.where(leading, enc_grads[3], dec_grads[3])
    rows_sent = jnp.where(leading, dec_grads[3], enc_grads[3])
    rows = rows + swapped(rows_sent, "pipe", 0)
    rows = lax.psum(rows, "dp")

    def wide(part, count):
        return jnp.concatenate([part[i * D : (i + 1) * D] for i in range(count)], axis=1).astype(F32)[None]

    return (
        layer_out,
        embedding_grad,
        wide(rest[2 * D : 5 * D], 3),
        rest[5 * D :].astype(F32)[None],
        wide(rest[: 2 * D], 2),
        wide(ff[:FF], 4),
        ff[FF:].astype(F32)[None],
        rows[:4].reshape(1, FF),
        rows[4:7][None],
        rows[7:10][None],
        rows[10:13][None],
    )


def solution(mesh):
    return jax.shard_map(
        per_device,
        mesh=mesh,
        in_specs=(
            P("pipe", "dp", None),
            P("dp", None),
            P("dp", None),
            P("dp"),
            P("dp"),
            P("dp", None),
            P("pipe", None, None),
            P("pipe", None, None),
            P("pipe", None, None),
            P("pipe", None, None),
            P("pipe", None, None),
            P("pipe", None),
            P("pipe", None, None),
            P("pipe", None, None),
            P("pipe", None, None),
        ),
        out_specs=(
            P("pipe", "dp", None),
            P("pipe", "dp", None),
            P("pipe", None, None),
            P("pipe", None, None),
            P("pipe", None, None),
            P("pipe", None, None),
            P("pipe", None, None),
            P("pipe", None),
            P("pipe", None, None),
            P("pipe", None, None),
            P("pipe", None, None),
        ),
        check_vma=False,
    )
```

```python
import functools
import math

import jax
import jax.numpy as jnp
from jax import lax
from jax.experimental import pallas as pl
from jax.experimental.pallas import tpu as pltpu
from jax.sharding import PartitionSpec as P

HEADS = 8
D = 512
FF = 2048
T = 1024
SENTS = 17
WIN = 128
EPSILON = 1e-05
NEG = -1e30
BF = jnp.bfloat16
F32 = jnp.float32
VMEM = pl.BlockSpec(memory_space=pltpu.VMEM)
SMEM = pl.BlockSpec(memory_space=pltpu.SMEM)
BLOCK = 512
STEPS = T // BLOCK


def nn(a, b):
    return jnp.dot(a, b, preferred_element_type=F32)


def nt(a, b):
    return lax.dot_general(a, b, (((1,), (1,)), ((), ())), preferred_element_type=F32)


def tn(a, b):
    return lax.dot_general(a, b, (((0,), (0,)), ((), ())), preferred_element_type=F32)


def normalized(value):
    center = jnp.mean(value, axis=-1, keepdims=True)
    centered = value - center
    spread = jnp.mean(centered * centered, axis=-1, keepdims=True)
    scale = lax.rsqrt(spread + EPSILON)
    return centered * scale, scale


def normalized_back(grad, unit, scale):
    first = jnp.mean(grad, axis=-1, keepdims=True)
    second = jnp.mean(grad * unit, axis=-1, keepdims=True)
    return scale * (grad - first - unit * second)


def folded(value):
    return jnp.sum(value.reshape(value.shape[0] // 8, 8, value.shape[1]), axis=0)


def column_sum(value):
    return jnp.sum(value, axis=0, keepdims=True)


def each_block(body):
    for index in range(STEPS):
        body(pl.ds(index * BLOCK, BLOCK))


def each_chunk(count, size, body):
    def step(index, carry):
        body(pl.multiple_of(index * size, size))
        return carry

    lax.fori_loop(0, count, step, 0)


class Held:
    def __init__(self, ref, copy):
        self.ref, self.copy = ref, copy

    def ready(self):
        if self.copy is not None:
            self.copy.wait()
            self.copy = None
        return self.ref

    def __getitem__(self, index):
        return self.ready()[index]

    @property
    def at(self):
        return self.ready().at

    @property
    def shape(self):
        return self.ref.shape


def ready(value):
    return value.ready() if isinstance(value, (Held, Landing)) else value


LEAVING = {}


def leave(*refs):
    for ref in refs:
        copy, started = LEAVING.get(id(ref), (None, True))
        if not started:
            copy.start()
            LEAVING[id(ref)] = (copy, True)


class Landing:
    def __init__(self, ref, sem):
        self.ref, self.sem = ref, sem

    def ready(self):
        if self.sem is not None:
            pltpu.make_async_copy(self.ref, self.ref, self.sem).wait()
            self.sem = None
        return self.ref

    def __getitem__(self, index):
        return self.ready()[index]

    @property
    def at(self):
        return self.ready().at

    @property
    def shape(self):
        return self.ref.shape


class Raw:
    def __init__(self, value):
        self.value, self.shape, self.dtype = value, value.shape, value.dtype


def bytes_of(x):
    return math.prod(x.shape) * jnp.dtype(x.dtype).itemsize


LARGE = 256 << 10


def kernel_call(body, outs, operands, scalars=0, scratch=(), out_specs=None, flops=0, after=(), direct=False):
    size = sum(bytes_of(x) for x in (*operands, *outs))
    held = size + (sum(bytes_of(x) for x in scratch) if direct else 0)
    count, many, extra = len(operands), len(outs), len(scratch)
    raw = [isinstance(x, Raw) for x in operands]
    comes = [not (direct or r) and i >= scalars and bytes_of(x) >= LARGE for i, (x, r) in enumerate(zip(operands, raw))]
    goes = [not direct and bytes_of(x) >= LARGE for x in outs]
    anywhere = pl.BlockSpec(memory_space=pl.ANY)
    in_specs = [SMEM] * scalars + [anywhere if c or r else VMEM for c, r in zip(comes[scalars:], raw[scalars:])] + [anywhere] * len(after)
    specs = list(out_specs) if out_specs else [VMEM] * many
    specs = [anywhere if g else spec for g, spec in zip(goes, specs)]
    room = [pltpu.VMEM(x.shape, x.dtype) for x, c in zip((*operands, *outs), comes + goes) if c]
    sems = [pltpu.SemaphoreType.DMA((len(room),))] if room else []

    def run(*refs):
        ins, rest = list(refs[:count]), refs[count + len(after) :]
        results, rest = list(rest[:many]), rest[many:]
        own, rest = rest[:extra], rest[extra:]
        buffers, slot = rest[: len(room)], 0
        for i, c in enumerate(comes):
            if c:
                copy = pltpu.make_async_copy(ins[i], buffers[slot], rest[-1].at[slot])
                copy.start()
                ins[i] = Held(buffers[slot], copy)
                slot += 1
        LEAVING.clear()
        for i, g in enumerate(goes):
            if g:
                copy = pltpu.make_async_copy(buffers[slot], results[i], rest[-1].at[slot])
                results[i] = buffers[slot]
                LEAVING[id(results[i])] = (copy, False)
                slot += 1
        body(*ins, *results, *own)
        for value in ins:
            ready(value)
        for i, g in enumerate(goes):
            if g:
                leave(results[i])
        for i, g in enumerate(goes):
            if g:
                LEAVING[id(results[i])][0].wait()
        LEAVING.clear()

    return pl.pallas_call(
        run,
        out_shape=tuple(outs),
        in_specs=in_specs,
        out_specs=tuple(specs),
        scratch_shapes=list(scratch) + room + sems,
        compiler_params=pltpu.CompilerParams(vmem_limit_bytes=held + (3 << 20) if direct else 62 << 20),
        cost_estimate=pl.CostEstimate(flops=flops, bytes_accessed=size, transcendentals=0),
    )(*(x.value if isinstance(x, Raw) else x for x in operands), *after)


def shaped(rows, columns, kind):
    return jax.ShapeDtypeStruct((rows, columns), kind)


def layout_kernel(flags, lengths, hamming, priority, copies, table, bias, glance, places):
    row = flags[0, 0]
    ends = []
    total = jnp.int32(0)
    for j in range(SENTS):
        total = total + lengths[row, j]
        ends.append(total)
    count = jnp.int32(0)
    first = jnp.int32(0)

    def origin(start):
        return jnp.minimum((start // 16) * 16, T - WIN)

    for j in range(SENTS):
        begin = jnp.int32(0) if j == 0 else ends[j - 1]
        opens = (ends[j] - origin(first)) > WIN
        if j == 0:
            opens = jnp.bool_(False)
        first = jnp.where(opens, begin, first)
        count = jnp.where(opens, count + 1, count)
        table[0, 1 + count] = origin(first)
        table[0, 32 + count] = first
        table[0, 64 + count] = ends[j]
    table[0, 0] = count + 1

    lanes = lax.broadcasted_iota(jnp.int32, (8, WIN), 1)
    rows = lax.broadcasted_iota(jnp.int32, (8, WIN), 0)
    place = rows * WIN + lanes
    quota = jnp.zeros((8, WIN), jnp.int32) + (hamming[row, 0] + 1) // 2
    for j in range(SENTS - 1):
        change = (hamming[row, j + 1] + 1) // 2 - (hamming[row, j] + 1) // 2
        quota = quota + jnp.where(place >= ends[j], change, 0)
    part = pl.ds(pl.multiple_of(row * (T // WIN), 8), T // WIN)
    chosen = jnp.where(priority[part, :] < quota, 1.0, 0.0)
    copy = copies[part, :].astype(F32)
    for i in range(T // WIN):
        part = pl.ds(i * WIN, WIN)
        glance[part, :] = jnp.broadcast_to(chosen[i : i + 1, :], (WIN, WIN)).T
        places[part, :] = jnp.broadcast_to(copy[i : i + 1, :], (WIN, WIN)).T.astype(jnp.int32)

    def window(w, carry):
        at = table[0, 1 + w]
        here = lanes + at
        segment = jnp.zeros((8, WIN), F32)
        for j in range(SENTS):
            segment = segment + jnp.where(here >= ends[j], 1.0, 0.0)
        inside = (here >= table[0, 32 + w]) & (here < table[0, 64 + w])
        segment = jnp.where(inside, segment, -1.0)
        across = jnp.broadcast_to(segment[0:1, :], (WIN, WIN))
        down = across.T
        bias[w] = jnp.where((across == down) & (across >= 0.0), 0.0, NEG)
        return carry

    lax.fori_loop(0, count + 1, window, 0)
    table[0, 2 + count] = 0
    bias[count + 1] = jnp.full((WIN, WIN), NEG, F32)


def row_layout(flags, lengths, hamming, priority, copies):
    outs = (
        shaped(1, 128, jnp.int32),
        jax.ShapeDtypeStruct((SENTS + 1, WIN, WIN), F32),
        shaped(T, WIN, F32),
        shaped(T, WIN, jnp.int32),
    )
    return kernel_call(
        layout_kernel,
        outs,
        (flags, lengths, hamming, priority, copies),
        scalars=3,
        out_specs=(SMEM, VMEM, VMEM, VMEM),
        direct=True,
    )


def pair_halves(part):
    low = lax.broadcasted_iota(jnp.int32, (WIN, WIN), 1) < 64
    zero = jnp.zeros_like(part)
    return jnp.concatenate([jnp.where(low, part, zero), jnp.where(low, zero, part)], axis=0)


def pair_join(both):
    low = lax.broadcasted_iota(jnp.int32, (WIN, WIN), 1) < 64
    return jnp.where(low, both[:WIN], both[WIN:])


PAIRS = [slice(i * 128, i * 128 + 128) for i in range(HEADS // 2)]


PAIRS = [slice(i * 128, i * 128 + 128) for i in range(HEADS // 2)]
GROUP = 2


def grouped(table, body):
    def step(index, carry):
        body([index * GROUP + i for i in range(GROUP)])
        return carry

    lax.fori_loop(0, (table[0, 0] + GROUP - 1) // GROUP, step, 0)


def spread(table, windows):
    ats = [pl.ds(pl.multiple_of(table[0, 1 + w], 16), WIN) for w in windows]
    return [(w, pair, at, lanes) for w, at in zip(windows, ats) for pair, lanes in enumerate(PAIRS)]


def masks(bias, windows):
    out = []
    for w in windows:
        masked = bias[w]
        out += [jnp.concatenate([masked, masked], axis=1)] * len(PAIRS)
    return out


def attend(table, bias, queries, keys, values, mixed, stats):
    bias, queries, keys, values = map(ready, (bias, queries, keys, values))

    def body(windows):
        parts = spread(table, windows)
        masked = masks(bias, windows)
        query = [pair_halves(queries[at, lanes]) for _, _, at, lanes in parts]
        key = [keys[at, lanes] for _, _, at, lanes in parts]
        value = [values[at, lanes] for _, _, at, lanes in parts]
        scores = [nt(k, q) + mask for k, q, mask in zip(key, query, masked)]
        highest = [jnp.maximum(jnp.max(s, axis=0, keepdims=True), -1e29) for s in scores]
        raised = [jnp.exp(s - h) for s, h in zip(scores, highest)]
        inverse = [1.0 / jnp.maximum(jnp.sum(r, axis=0, keepdims=True), 1e-30) for r in raised]
        shares = [(r * i).astype(BF) for r, i in zip(raised, inverse)]
        out = [pair_join(tn(s, v)).astype(BF) for s, v in zip(shares, value)]
        for (w, pair, at, lanes), o, h, i in zip(parts, out, highest, inverse):
            mixed[at, lanes] = mixed[at, lanes] + o
            stats[w * 4 + pair, 0:1, :] = h
            stats[w * 4 + pair, 1:2, :] = i

    mixed[...] = jnp.zeros_like(mixed)
    grouped(table, body)


def attend_back(table, bias, queries, keys, values, stats, grad, grad_q, grad_k, grad_v):
    bias, queries, keys, values, stats = map(ready, (bias, queries, keys, values, stats))

    def body(windows):
        parts = spread(table, windows)
        masked = masks(bias, windows)
        query = [pair_halves(queries[at, lanes]) for _, _, at, lanes in parts]
        key = [keys[at, lanes] for _, _, at, lanes in parts]
        value = [values[at, lanes] for _, _, at, lanes in parts]
        out = [pair_halves(grad[at, lanes]) for _, _, at, lanes in parts]
        top = [stats[w * 4 + pair, 0:1, :] for w, pair, _, _ in parts]
        inverse = [stats[w * 4 + pair, 1:2, :] for w, pair, _, _ in parts]
        scores = [nt(k, q) + mask for k, q, mask in zip(key, query, masked)]
        back = [nt(v, o) for v, o in zip(value, out)]
        shares = [jnp.exp(s - h) * i for s, h, i in zip(scores, top, inverse)]
        got_v = [nn(s.astype(BF), o).astype(BF) for s, o in zip(shares, out)]
        total = [jnp.sum(s * b, axis=0, keepdims=True) for s, b in zip(shares, back)]
        scored = [(s * (b - t)).astype(BF) for s, b, t in zip(shares, back, total)]
        got_k = [nn(s, q).astype(BF) for s, q in zip(scored, query)]
        got_q = [(pair_join(tn(s, k)) * 0.125).astype(BF) for s, k in zip(scored, key)]
        for ref, got in zip((grad_q, grad_k, grad_v), (got_q, got_k, got_v)):
            for (_, _, at, lanes), value_got in zip(parts, got):
                ref[at, lanes] = ref[at, lanes] + value_got

    for ref in (grad_q, grad_k, grad_v):
        ref[...] = jnp.zeros_like(ref)
    grouped(table, body)


STATS = jax.ShapeDtypeStruct(((SENTS + 1) * 4, 2, 2 * WIN), F32)


def thirds(ref):
    return tuple(ref.at[:, i * D : (i + 1) * D] for i in range(ref.shape[1] // D))


def put(flags, half, kept, sent, rows, value):
    @pl.when(flags[0, 1] == half)
    def _():
        kept[rows, :] = value

    @pl.when(flags[0, 1] != half)
    def _():
        sent[rows, :] = value


def rows_at(start, count=D):
    return slice(start, start + count)


def scaled(unit, small, slot):
    return unit * small[7 + slot : 8 + slot, :] + small[10 + slot : 11 + slot, :]


def project(x, weight_in, joined, at):
    got = nn(x, weight_in[...])
    joined[at, :D] = (got[:, :D] * 0.125).astype(BF)
    joined[at, D:] = got[:, D:].astype(BF)


def encoder_self_kernel(table, bias, source, weight_in, weight_out, small, joined, mixed, stats, z, x):
    def before(at):
        unit, _ = normalized(source[at, :].astype(F32))
        value = scaled(unit, small, 2)
        x[at, :] = value
        project(value.astype(BF), weight_in, joined, at)

    each_block(before)
    leave(joined)
    attend(table, bias, *thirds(joined), mixed, stats)
    leave(mixed, stats)

    def after(at):
        z[at, :] = x[at, :] + nn(mixed[at, :], weight_out[...]) + small[4:5, :]

    each_block(after)


def copy_hits(bias, places, w, start):
    at = pl.ds(start, WIN)
    lanes = lax.broadcasted_iota(jnp.int32, (WIN, WIN), 1) + start
    inside = jnp.max(bias[w], axis=1, keepdims=True) == 0.0
    return at, jnp.where((places[at, :] == lanes) & inside, 1.0, 0.0).astype(BF)


def kept_rows(glance, at):
    return jnp.concatenate([glance[at, :]] * (D // WIN), axis=1) > 0.5


def decoder_self_kernel(
    table, bias, source, target, glance, places, weight_in, weight_out, small, x, joined, mixed, stats, z, copied
):
    copied[...] = jnp.zeros_like(copied)
    bias, places, source = map(ready, (bias, places, source))

    def gather(windows):
        parts = [copy_hits(bias, places, w, pl.multiple_of(table[0, 1 + w], 16)) for w in windows]
        got = [nn(hit, source[at, :]).astype(BF) for at, hit in parts]
        for (at, _), value in zip(parts, got):
            copied[at, :] = copied[at, :] + value

    grouped(table, gather)

    def before(at):
        value = jnp.where(kept_rows(glance, at), target[at, :].astype(F32), copied[at, :].astype(F32)).astype(BF)
        x[at, :] = value
        project(value, weight_in, joined, at)

    each_block(before)
    leave(joined)
    attend(table, bias, *thirds(joined), mixed, stats)
    leave(mixed, stats)

    def after(at):
        z[at, :] = x[at, :].astype(F32) + nn(mixed[at, :], weight_out[...]) + small[4:5, :]

    each_block(after)


FLOP_UNIT = 2 * T * D * D


ROOT = 0.7978845608028654
CUBE = 0.044715


def gelu_parts(u):
    square = u * u
    bent = jnp.tanh(u * (ROOT + ROOT * CUBE * square))
    half = 0.5 + 0.5 * bent
    slope = half + (u - u * (bent * bent)) * (0.5 * ROOT + 1.5 * ROOT * CUBE * square)
    return u * half, slope


def expand_block(value, expand, small, active, slope, at):
    for j in range(FF // D):
        cols = rows_at(j * D)
        hidden = (nn(value, expand[:, cols]) + small[j : j + 1, :]).astype(BF)
        active[at, cols], slope[at, cols] = gelu_parts(hidden)


def encoder_ff_kernel(z1, expand, contract, cross, small, inner, z2, memory, states, active):
    def block(at):
        unit, _ = normalized(z1[at, :])
        value = scaled(unit, small, 0)
        for j in range(FF // D):
            cols = rows_at(j * D)
            hidden = (nn(value.astype(BF), expand[:, cols]) + small[j : j + 1, :]).astype(BF)
            inner[at, cols] = hidden
            active[at, cols], _ = gelu_parts(hidden)
        total = value + nn(active[at, :], contract[...]) + small[5:6, :]
        z2[at, :] = total
        unit, _ = normalized(total)
        out = scaled(unit, small, 1)
        memory[at, :] = out.astype(BF)
        got = nn(out.astype(BF), cross[...])
        states[at, :D] = got[:, :D].astype(BF)
        states[at, D:] = (got[:, D:] + small[6:7, :]).astype(BF)

    each_block(block)
    leave(inner, z2, memory)


def ff_back(flags, dzb, value_b, active, inner, expand, contract, kept, sent, bias_rows):
    def block(at):
        for j in range(FF // D):
            cols = rows_at(j * D)
            back = nt(dzb[at, :], contract[cols, :])
            inner[at, cols] = (back * inner[at, cols].astype(F32)).astype(BF)

    each_block(block)
    for c in range(FF // D):
        cols = rows_at(c * D)
        put(flags, 1, kept, sent, cols, tn(active[:, cols], dzb[...]).astype(BF))
        put(flags, 0, kept, sent, cols, tn(value_b[...], inner[:, cols]).astype(BF))
        bias_rows[c : c + 1, :] = column_sum(inner[:, cols].astype(F32))


def decoder_ff_kernel(
    flags, z2, expand, contract, small, cotangent,
    decoded, kept, sent, bias_grads, bias_rows, dz2,
    active, inner, value_b, dz, dzb,
):
    bias_grads[...] = jnp.zeros_like(bias_grads)
    offset = flags[0, 0] * T

    def block(at):
        unit, _ = normalized(z2[at, :])
        value = scaled(unit, small, 1)
        value_b[at, :] = value.astype(BF)
        expand_block(value.astype(BF), expand, small, active, inner, at)
        total = value + nn(active[at, :], contract[...]) + small[5:6, :]
        unit, scale = normalized(total)
        decoded[at, :] = scaled(unit, small, 2).astype(BF)
        wanted = cotangent[pl.ds(pl.multiple_of(offset + at.start, BLOCK), BLOCK), :].astype(F32)
        bias_grads[0:1, :] += column_sum(wanted * unit)
        bias_grads[1:2, :] += column_sum(wanted)
        back = normalized_back(wanted * small[9:10, :], unit, scale)
        bias_grads[2:3, :] += column_sum(back)
        dz[at, :] = back
        dzb[at, :] = back.astype(BF)

    each_block(block)
    leave(decoded)
    ff_back(flags, dzb, value_b, active, inner, expand, contract, kept, sent, bias_rows)
    leave(kept, sent)

    def last(at):
        back = dz[at, :] + nt(inner[at, :], expand[...])
        unit, scale = normalized(z2[at, :])
        bias_grads[3:4, :] += column_sum(back * unit)
        bias_grads[4:5, :] += column_sum(back)
        dz2[at, :] = normalized_back(back * small[8:9, :], unit, scale)

    each_block(last)


def encoder_ff_back_kernel(
    flags, z2, dstates, z1, hidden, own_cross, own_expand, own_contract, rest, half, last_half, small,
    cross_grads, kept, sent, bias_grads, bias_rows, dz1,
    cross, expand, contract, active, inner, value_b, memory_b, dz, dzb, sems,
):
    own = (own_cross, own_expand, own_contract, rest, half, last_half)
    cross, expand, contract = fetch_rest(0, flags, *own, cross, expand, contract, sems)
    bias_grads[...] = jnp.zeros_like(bias_grads)

    def block(at):
        unit, scale = normalized(z2[at, :])
        memory_b[at, :] = scaled(unit, small, 1).astype(BF)
        back = nt(dstates[at, :], cross[...])
        bias_grads[0:1, :] += column_sum(dstates[at, D:].astype(F32))
        bias_grads[1:2, :] += column_sum(back * unit)
        bias_grads[2:3, :] += column_sum(back)
        back = normalized_back(back * small[8:9, :], unit, scale)
        bias_grads[3:4, :] += column_sum(back)
        dz[at, :] = back
        dzb[at, :] = back.astype(BF)
        unit, _ = normalized(z1[at, :])
        value_b[at, :] = scaled(unit, small, 0).astype(BF)
        for j in range(FF // D):
            cols = rows_at(j * D)
            active[at, cols], inner[at, cols] = gelu_parts(hidden[at, cols])

    each_block(block)
    ff_back(flags, dzb, value_b, active, inner, expand, contract, kept, sent, bias_rows)
    for c in range(2):
        cross_grads[rows_at(c * D), :] = tn(memory_b[...], dstates[:, rows_at(c * D)]).astype(BF)
    leave(kept, sent, cross_grads)

    def last(at):
        back = dz[at, :] + nt(inner[at, :], expand[...])
        unit, scale = normalized(z1[at, :])
        bias_grads[4:5, :] += column_sum(back * unit)
        bias_grads[5:6, :] += column_sum(back)
        dz1[at, :] = normalized_back(back * small[7:8, :], unit, scale)

    each_block(last)


def encoder_ff_back(flags, dstates, z1, z2, hidden, weights, small, after=()):
    outs = (
        shaped(2 * D, D, BF), shaped(FF, D, BF), shaped(FF, D, BF),
        shaped(8, D, F32), shaped(8, D, F32), shaped(T, D, F32),
    )
    return kernel_call(
        encoder_ff_back_kernel,
        outs,
        (flags, z2, dstates, z1, hidden, *map(Raw, weights), small),
        scalars=1,
        scratch=[
            pltpu.VMEM((D, 2 * D), BF),
            pltpu.VMEM((D, FF), BF),
            pltpu.VMEM((FF, D), BF),
            pltpu.VMEM((T, FF), BF),
            pltpu.VMEM((T, FF), BF),
            pltpu.VMEM((T, D), BF),
            pltpu.VMEM((T, D), BF),
            pltpu.VMEM((T, D), F32),
            pltpu.VMEM((T, D), BF),
            pltpu.SemaphoreType.DMA((3,)),
        ],
        flops=22 * FLOP_UNIT,
        after=after,
    )


def decoder_cross_kernel(table, bias, z1, states, weight, small, queries, mixed, stats, z2, x):
    def before(at):
        unit, _ = normalized(z1[at, :])
        value = scaled(unit, small, 0)
        x[at, :] = value
        queries[at, :] = (nn(value.astype(BF), weight[:, :D]) * 0.125).astype(BF)

    each_block(before)
    attend(table, bias, queries, *thirds(states), mixed, stats)

    def after(at):
        z2[at, :] = x[at, :] + nn(mixed[at, :], weight[:, D:]) + small[6:7, :]

    each_block(after)


def decoder_cross_back_kernel(
    table, bias, dz2, z1, queries, states, mixed, stats, weight, small,
    grads, bias_grads, dstates, dz1,
    value_b, dzb, out, dq,
):
    bias_grads[...] = jnp.zeros_like(bias_grads)

    def before(at):
        bias_grads[0:1, :] += column_sum(dz2[at, :])
        low = dz2[at, :].astype(BF)
        dzb[at, :] = low
        out[at, :] = nt(low, weight[:, D:]).astype(BF)
        unit, _ = normalized(z1[at, :])
        value_b[at, :] = scaled(unit, small, 0).astype(BF)

    each_block(before)
    attend_back(table, bias, queries, *thirds(states), stats, out, dq, *thirds(dstates))
    leave(dstates)
    grads[:D, :] = tn(value_b[...], dq[...]).astype(BF)
    grads[D:, :] = tn(mixed[...], dzb[...]).astype(BF)
    leave(grads)

    def after(at):
        back = dz2[at, :] + nt(dq[at, :], weight[:, :D])
        unit, scale = normalized(z1[at, :])
        bias_grads[1:2, :] += column_sum(back * unit)
        bias_grads[2:3, :] += column_sum(back)
        dz1[at, :] = normalized_back(back * small[7:8, :], unit, scale)

    each_block(after)


def self_back(table, bias, flags, dz, x, joined, mixed, stats, weight_in, weight_out, cross, kept, sent, acc, dzb, out, djoined):
    acc[...] = jnp.zeros_like(acc)

    def before(at):
        acc[0:1, :] += column_sum(dz[at, :])
        low = dz[at, :].astype(BF)
        dzb[at, :] = low
        out[at, :] = nt(low, weight_out[...]).astype(BF)

    each_block(before)
    attend_back(table, bias, *thirds(joined), stats, out, *thirds(djoined))
    for half in range(2):
        put(flags, half, kept, sent, rows_at(0), cross[rows_at(half * D), :])
    for c in range(3):
        value = tn(x[...], djoined[:, rows_at(c * D)]).astype(BF)
        put(flags, c // 2, kept, sent, rows_at(D + c % 2 * D), value)
    put(flags, 1, kept, sent, rows_at(2 * D), tn(mixed[...], dzb[...]).astype(BF))


def put_small(flags, kept, sent, rows):
    count = kept.shape[0] - 3 * D
    at = rows_at(3 * D, count)
    filled = jnp.concatenate(rows + [jnp.zeros((count - 13, D), F32)], axis=0).astype(BF)
    put(flags, 0, kept, sent, at, filled)
    put(flags, 1, kept, sent, at, jnp.zeros((count, D), BF))


def decoder_self_back_kernel(
    table, flags, dz, own_in, own_out, half, rest, joined, bias, stats, x, mixed, glance, places,
    cross, ff_bias, ff_rows, cross_bias,
    kept, sent, target_grad, source_grad,
    weight_in, weight_out, acc, dzb, out, djoined, dcopied, sems,
):
    weight_in, weight_out = fetch_self(1, flags, own_in, own_out, half, rest, weight_in, weight_out, sems)
    self_back(table, bias, flags, dz, x, joined, mixed, stats, weight_in, weight_out, cross, kept, sent, acc, dzb, out, djoined)
    put_small(
        flags, kept, sent,
        [
            ff_rows[0:4, :], acc[0:1, :], ff_bias[2:3, :], cross_bias[0:1, :],
            cross_bias[1:2, :], ff_bias[3:4, :], ff_bias[0:1, :],
            cross_bias[2:3, :], ff_bias[4:5, :], ff_bias[1:2, :],
        ],
    )

    def after(at):
        back = dz[at, :] + nt(djoined[at, :], weight_in[...])
        kept_at = kept_rows(glance, at)
        target_grad[at, :] = jnp.where(kept_at, back, 0.0).astype(BF)
        dcopied[at, :] = jnp.where(kept_at, 0.0, back).astype(BF)

    each_block(after)
    leave(target_grad, kept, sent)
    source_grad[...] = jnp.zeros_like(source_grad)
    bias, places = ready(bias), ready(places)

    def scatter(windows):
        parts = [copy_hits(bias, places, w, pl.multiple_of(table[0, 1 + w], 16)) for w in windows]
        got = [tn(hit, dcopied[at, :]).astype(BF) for at, hit in parts]
        for (at, _), value in zip(parts, got):
            source_grad[at, :] = source_grad[at, :] + value

    grouped(table, scatter)


def half_rows(count):
    return 3 * D + 8 * count


def decoder_self_back(table, flags, bias, dz, x, joined, mixed, stats, glance, places, weights, cross, ff_bias, ff_rows, cross_bias, count, after=()):
    half = half_rows(count)
    outs = (shaped(half, D, BF), shaped(half, D, BF), shaped(T, D, BF), shaped(T, D, BF))
    return kernel_call(
        decoder_self_back_kernel,
        outs,
        (table, flags, dz, *map(Raw, weights), joined, bias, stats, x, mixed, glance, places, cross, ff_bias, ff_rows, cross_bias),
        scalars=2,
        scratch=[
            pltpu.VMEM((D, 3 * D), BF), pltpu.VMEM((D, D), BF),
            pltpu.VMEM((8, D), F32), pltpu.VMEM((T, D), BF), pltpu.VMEM((T, D), BF),
            pltpu.VMEM((T, 3 * D), BF), pltpu.VMEM((T, D), BF), pltpu.SemaphoreType.DMA((2,)),
        ],
        flops=18 * FLOP_UNIT,
        after=after,
    )


def encoder_self_back_kernel(
    table, flags, dz, rows, got, own_in, own_out, half, rest, joined, bias, stats, mixed, copies_grad, small,
    cross, ff_bias, ff_rows,
    kept, sent, source_grad,
    source, weight_in, weight_out, acc, x, dzb, out, djoined, sems,
):
    @pl.when(flags[0, 0] == 0)
    def _():
        start((rows.at[rows_at(0, T), :], source, sems.at[2]))

    @pl.when(flags[0, 0] != 0)
    def _():
        start((got, source, sems.at[2]))

    source = Landing(source, sems.at[2])
    weight_in, weight_out = fetch_self(0, flags, own_in, own_out, half, rest, weight_in, weight_out, sems)

    def first(at):
        unit, _ = normalized(source[at, :].astype(F32))
        x[at, :] = scaled(unit, small, 2).astype(BF)

    each_block(first)
    self_back(table, bias, flags, dz, x, joined, mixed, stats, weight_in, weight_out, cross, kept, sent, acc, dzb, out, djoined)

    def after(at):
        back = dz[at, :] + nt(djoined[at, :], weight_in[...])
        unit, scale = normalized(source[at, :].astype(F32))
        acc[1:2, :] += column_sum(back * unit)
        acc[2:3, :] += column_sum(back)
        source_grad[at, :] = (normalized_back(back * small[9:10, :], unit, scale) + copies_grad[at, :].astype(F32)).astype(BF)

    each_block(after)
    put_small(
        flags, kept, sent,
        [
            ff_rows[0:4, :], acc[0:1, :], ff_bias[3:4, :], ff_bias[0:1, :],
            ff_bias[4:5, :], ff_bias[1:2, :], acc[1:2, :],
            ff_bias[5:6, :], ff_bias[2:3, :], acc[2:3, :],
        ],
    )


def encoder_self_back(table, flags, bias, dz, rows, got, joined, mixed, stats, copies_grad, weights, small, cross, ff_bias, ff_rows, count, after=()):
    half = half_rows(count)
    outs = (shaped(half, D, BF), shaped(half, D, BF), shaped(T, D, BF))
    return kernel_call(
        encoder_self_back_kernel,
        outs,
        (table, flags, dz, Raw(rows), Raw(got), *map(Raw, weights), joined, bias, stats, mixed, copies_grad, small, cross, ff_bias, ff_rows),
        scalars=2,
        scratch=[
            pltpu.VMEM((T, D), BF), pltpu.VMEM((D, 3 * D), BF), pltpu.VMEM((D, D), BF),
            pltpu.VMEM((8, D), F32), pltpu.VMEM((T, D), BF), pltpu.VMEM((T, D), BF), pltpu.VMEM((T, D), BF),
            pltpu.VMEM((T, 3 * D), BF), pltpu.SemaphoreType.DMA((3,)),
        ],
        flops=18 * FLOP_UNIT,
        after=after,
    )


def start(*copies):
    for source, target, sem in copies:
        pltpu.make_async_copy(source, target, sem).start()


def fetch_self(layer, flags, own_in, own_out, half, rest, to_in, to_out, sems):
    own = flags[0, 0] == layer

    def other(low, high):
        start(
            (high.at[rows_at(D), :], to_out, sems.at[1]),
            (low.at[rows_at(0), :], to_in.at[:, rows_at(0)], sems.at[0]),
            (low.at[rows_at(D), :], to_in.at[:, rows_at(D)], sems.at[0]),
            (high.at[rows_at(0), :], to_in.at[:, rows_at(2 * D)], sems.at[0]),
        )

    pl.when(own)(lambda: start((own_out, to_out, sems.at[1]), (own_in, to_in, sems.at[0])))
    pl.when(jnp.logical_not(own) & (flags[0, 1] == 0))(lambda: other(half, rest))
    pl.when(jnp.logical_not(own) & (flags[0, 1] != 0))(lambda: other(rest, half))
    return Landing(to_in, sems.at[0]), Landing(to_out, sems.at[1])


def fetch_rest(layer, flags, own_cross, own_expand, own_contract, rest, half, last, cross, expand, contract, sems):
    own = flags[0, 0] == layer

    def other(low, high):
        start(
            *((rest.at[rows_at((2 + j) * D), :], expand.at[:, rows_at(j * D)], sems.at[1]) for j in range(2)),
            *((low.at[rows_at(j * D), :], expand.at[:, rows_at((2 + j) * D)], sems.at[1]) for j in range(2)),
            (low.at[rows_at(2 * D), :], contract.at[rows_at(0), :], sems.at[2]),
            (high, contract.at[rows_at(D, 3 * D), :], sems.at[2]),
            *((rest.at[rows_at(j * D), :], cross.at[:, rows_at(j * D)], sems.at[0]) for j in range(2)),
        )

    pl.when(own)(
        lambda: start((own_expand, expand, sems.at[1]), (own_contract, contract, sems.at[2]), (own_cross, cross, sems.at[0]))
    )
    pl.when(jnp.logical_not(own) & (flags[0, 1] == 0))(lambda: other(half, last))
    pl.when(jnp.logical_not(own) & (flags[0, 1] != 0))(lambda: other(last, half))
    return Landing(cross, sems.at[0]), Landing(expand, sems.at[1]), Landing(contract, sems.at[2])


def fetch_rows(flags, rows, got, source, target, sems):
    @pl.when(flags[0, 0] == 0)
    def _():
        start((rows.at[rows_at(0, T), :], source, sems.at[0]), (got, target, sems.at[1]))

    @pl.when(flags[0, 0] != 0)
    def _():
        start((got, source, sems.at[0]), (rows.at[rows_at(T, T), :], target, sems.at[1]))

    return Landing(source, sems.at[0]), Landing(target, sems.at[1])


def first_kernel(
    table, flags, rows, got, own_in, own_out, half, rest, bias, glance, places, small, small_other,
    e_small, d_small, e_joined, e_mixed, e_stats, e_z, x, d_joined, d_mixed, d_stats, d_z,
    source, target, e_in, e_out, d_in, d_out, wide, copied, sems,
):
    source, target = fetch_rows(flags, rows, got, source, target, sems.at[pl.ds(0, 2)])
    e_in, e_out = fetch_self(0, flags, own_in, own_out, half, rest, e_in, e_out, sems.at[pl.ds(2, 2)])
    d_in, d_out = fetch_self(1, flags, own_in, own_out, half, rest, d_in, d_out, sems.at[pl.ds(4, 2)])

    @pl.when(flags[0, 0] == 0)
    def _():
        e_small[0:13, :], d_small[0:13, :] = small[...], small_other[...]

    @pl.when(flags[0, 0] != 0)
    def _():
        e_small[0:13, :], d_small[0:13, :] = small_other[...], small[...]

    encoder_self_kernel(table, bias, source, e_in, e_out, e_small, e_joined, e_mixed, e_stats, e_z, wide)
    leave(e_z)
    decoder_self_kernel(
        table, bias, source, target, glance, places, d_in, d_out, d_small, x, d_joined, d_mixed, d_stats, d_z, copied
    )


def first(table, flags, bias, glance, places, rows, got, weights, small, small_other):
    layer = (shaped(T, 3 * D, BF), shaped(T, D, BF), STATS, shaped(T, D, F32))
    outs = (shaped(16, D, F32), shaped(16, D, F32), *layer, shaped(T, D, BF), *layer)
    return kernel_call(
        first_kernel,
        outs,
        (table, flags, Raw(rows), Raw(got), *map(Raw, weights), bias, glance, places, small, small_other),
        scalars=2,
        scratch=[
            pltpu.VMEM((T, D), BF), pltpu.VMEM((T, D), BF),
            pltpu.VMEM((D, 3 * D), BF), pltpu.VMEM((D, D), BF), pltpu.VMEM((D, 3 * D), BF), pltpu.VMEM((D, D), BF),
            pltpu.VMEM((T, D), F32), pltpu.VMEM((T, D), BF), pltpu.SemaphoreType.DMA((6,)),
        ],
        flops=24 * FLOP_UNIT,
    )


def middle_kernel(
    table, flags, e_z1, own_cross, own_expand, own_contract, rest, half, last, bias, d_z1, cotangent, e_small, d_small,
    hidden, e_z2, memory, decoded, kept, sent, ff_bias, ff_rows, cross_grads, cross_bias, dstates, dz1,
    e_cross, e_expand, e_contract, d_cross, d_expand, d_contract,
    active, states, queries, mixed, stats, d_z2, wide, inner, value_b, dzb, dz2, sems,
):
    own = (own_cross, own_expand, own_contract, rest, half, last)
    e_cross, e_expand, e_contract = fetch_rest(0, flags, *own, e_cross, e_expand, e_contract, sems.at[pl.ds(0, 3)])
    d_cross, d_expand, d_contract = fetch_rest(1, flags, *own, d_cross, d_expand, d_contract, sems.at[pl.ds(3, 3)])
    encoder_ff_kernel(e_z1, e_expand, e_contract, e_cross, e_small, hidden, e_z2, memory, states, active)
    decoder_cross_kernel(table, bias, d_z1, states, d_cross, d_small, queries, mixed, stats, d_z2, wide)
    decoder_ff_kernel(
        flags, d_z2, d_expand, d_contract, d_small, cotangent, decoded, kept, sent, ff_bias, ff_rows, dz2,
        active, inner, value_b, wide, dzb,
    )
    decoder_cross_back_kernel(
        table, bias, dz2, d_z1, queries, states, mixed, stats, d_cross, d_small, cross_grads, cross_bias, dstates, dz1,
        value_b, dzb, active.at[:, rows_at(0)], active.at[:, rows_at(D)],
    )


def middle(table, flags, bias, e_z1, d_z1, weights, cotangent, e_small, d_small):
    low, high = shaped(T, D, BF), shaped(T, D, F32)
    outs = (
        shaped(T, FF, BF), high, low, low, shaped(FF, D, BF), shaped(FF, D, BF),
        shaped(8, D, F32), shaped(8, D, F32), shaped(2 * D, D, BF), shaped(8, D, F32), shaped(T, 2 * D, BF), high,
    )
    weight_room = [pltpu.VMEM((D, 2 * D), BF), pltpu.VMEM((D, FF), BF), pltpu.VMEM((FF, D), BF)]
    return kernel_call(
        middle_kernel,
        outs,
        (table, flags, e_z1, *map(Raw, weights), bias, d_z1, cotangent, e_small, d_small),
        scalars=2,
        scratch=weight_room * 2
        + [
            pltpu.VMEM((T, FF), BF), pltpu.VMEM((T, 2 * D), BF), pltpu.VMEM((T, D), BF), pltpu.VMEM((T, D), BF),
            pltpu.VMEM(STATS.shape, F32), pltpu.VMEM((T, D), F32), pltpu.VMEM((T, D), F32), pltpu.VMEM((T, FF), BF),
            pltpu.VMEM((T, D), BF), pltpu.VMEM((T, D), BF), pltpu.VMEM((T, D), F32), pltpu.SemaphoreType.DMA((6,)),
        ],
        flops=54 * FLOP_UNIT,
    )


def swapped(value, axis, partner):
    count = lax.axis_size(axis)
    return lax.ppermute(value, axis, [(i, partner(i)) for i in range(count)])


def swapped_pipe(value):
    return swapped(value, "pipe", lambda i: 1 - i)


def added(first, second):
    return (first.astype(F32) + second.astype(F32)).astype(BF)


def gate(value, after):
    anywhere = pl.BlockSpec(memory_space=pl.ANY)
    return pl.pallas_call(
        lambda *refs: None,
        out_shape=jax.ShapeDtypeStruct(value.shape, value.dtype),
        in_specs=[anywhere] * (1 + len(after)),
        out_specs=anywhere,
        input_output_aliases={0: 0},
    )(value, *after)


def halve_kernel(step, pairs, flags, *refs):
    ins, (kept_out, sent_out) = refs[: 2 * pairs], refs[2 * pairs :]
    bit = flags[0, 1 + step]
    slot = 0
    for i in range(pairs):
        kept, got = ins[2 * i], ins[2 * i + 1]
        half = kept.shape[1] // 2
        for j in range(kept.shape[0]):
            for out, side in ((kept_out, bit), (sent_out, 1 - bit)):
                at = pl.ds(pl.multiple_of(side * half, 16), half)
                out[slot] = added(kept[j, at, :], got[j, at, :])
            slot += 1


def double_kernel(step, flags, own, got, out):
    half = own.shape[0]
    bit = flags[0, 1 + step]
    out[pl.ds(pl.multiple_of(bit * half, 16), half), :] = own[...]
    out[pl.ds(pl.multiple_of((1 - bit) * half, 16), half), :] = got[...]


def across_kernel(pairs, flags, *refs):
    ins, (keep, send) = refs[: 2 * pairs], refs[2 * pairs :]
    sums = [added(ins[2 * i][j], ins[2 * i + 1][j]) for i in range(pairs) for j in range(ins[2 * i].shape[0])]

    @pl.when(flags[0, 0] == 0)
    def _():
        keep[...], send[...] = sums[0], sums[1]

    @pl.when(flags[0, 0] != 0)
    def _():
        keep[...], send[...] = sums[1], sums[0]


class Steps:
    def __init__(self):
        count = lax.axis_size("dp")
        bits = list(range(1, (count - 1).bit_length()))
        cut = max(1, len(bits) // 3)
        orders = (bits, bits[cut:] + bits[:cut])
        index = lax.axis_index("dp")
        core = index & 1
        self.partners = [lambda i: i ^ 1]
        self.bits = [core]
        for pair in zip(*orders):
            self.partners.append(lambda i, pair=pair: i ^ (1 << pair[i & 1]))
            self.bits.append((index >> jnp.where(core == 0, *pair)) & 1)
        self.core, self.count, self.last = core, count, len(bits)
        self.place = 0
        for bit in self.bits:
            self.place = self.place * 2 + bit
        self.flags = jnp.stack([lax.axis_index("pipe")] + self.bits).astype(jnp.int32).reshape(1, -1)

    def swap(self, value, step):
        return swapped(value, "dp", self.partners[step])

    def halve(self, step, *pairs, after=()):
        many = sum(kept.shape[0] for kept, _ in pairs)
        shape = jax.ShapeDtypeStruct((many, pairs[0][0].shape[1] // 2, D), BF)
        operands = [x for pair in pairs for x in pair]
        return kernel_call(
            functools.partial(halve_kernel, step + 1, len(pairs)), (shape, shape), (self.flags, *operands), scalars=1, after=after, direct=True
        )

    def double(self, step, own, got, after=()):
        out = (shaped(2 * own.shape[0], D, BF),)
        return kernel_call(functools.partial(double_kernel, step), out, (self.flags, own, got), scalars=1, after=after, direct=True)[0]

    def half_gathered(self, value, after):
        parts = []
        for step in range(self.last, 0, -1):
            value = self.double(step, value, self.swap(value, step), after=after if step == 1 else ())
            parts.append(value)
        return parts

    def across(self, *pairs, after=()):
        shape = shaped(*pairs[0][0].shape[1:], BF)
        operands = [x for pair in pairs for x in pair]
        return kernel_call(
            functools.partial(across_kernel, len(pairs)), (shape, shape), (self.flags, *operands), scalars=1, after=after, direct=True
        )


def by_core(flags, first, second, body):
    pl.when(flags[0, 1] == 0)(lambda: body(first, second))
    pl.when(flags[0, 1] != 0)(lambda: body(second, first))


def spill_ff_kernel(flags, own, other, expand, contract):
    def fill(low, high):
        for j in range(FF // D):
            expand[:, rows_at(j * D)] = low[rows_at(j * D), :].astype(F32)
            contract[rows_at(j * D), :] = high[rows_at(j * D), :].astype(F32)

    by_core(flags, own, other, fill)


def spill_rest_kernel(flags, own, other, joined, out, cross, expand_bias, branch, gain, shift):
    def fill(low, high):
        spots = (
            (low, 0, cross, 0), (low, 1, joined, 0), (low, 2, joined, 1),
            (high, 0, cross, 1), (high, 1, joined, 2), (high, 2, out, 0),
        )
        for ref, block, to, column in spots:
            to[:, rows_at(column * D)] = ref[rows_at(block * D), :].astype(F32)
        value = low[rows_at(3 * D, 16), :].astype(F32)
        for j in range(FF // D):
            expand_bias[0:1, rows_at(j * D)] = value[j : j + 1, :]
        branch[...] = value[4:7, :]
        gain[...] = value[7:10, :]
        shift[...] = value[10:13, :]

    by_core(flags, own, other, fill)


def last_kernel(flags, expand, contract, out):
    @pl.when(flags[0, 1] == 0)
    def _():
        for j in range(2):
            out[rows_at(j * D), :] = expand[:, rows_at((2 + j) * D)]
        out[rows_at(2 * D), :] = contract[rows_at(0), :]

    @pl.when(flags[0, 1] != 0)
    def _():
        out[...] = contract[rows_at(D, 3 * D), :]


def per_device(
    embeddings, cotangent, lengths, copy_index, priority, hamming,
    self_in, self_out, cross_weight, expand, contract,
    expand_bias, branch_bias, norm_gain, norm_shift,
):
    pipe = lax.axis_index("pipe")
    leading = pipe == 0
    steps = Steps()
    flags, count = steps.flags, steps.count
    self_in, self_out, cross_weight, expand, contract = (w[0] for w in (self_in, self_out, cross_weight, expand, contract))

    rows = embeddings[0]
    small = jnp.concatenate([expand_bias.reshape(4, D), branch_bias[0], norm_gain[0], norm_shift[0]], 0)
    small_other = swapped_pipe(small)
    got = swapped_pipe(gate(lax.dynamic_slice_in_dim(rows, (1 - pipe) * T, T, 0), (small_other,)))
    size = 4 * D // count

    def piece(place, blocks_of):
        block, inside = place * size // D, place * size % D
        value = lax.dynamic_slice(blocks_of[0][0], (inside, blocks_of[0][1] * D), (size, D))
        for i in range(1, 4):
            matrix, column = blocks_of[i]
            value = jnp.where(block == i, lax.dynamic_slice(matrix, (inside, column * D), (size, D)), value)
        return value

    self_piece = piece(steps.place, [(self_in, 0), (self_in, 1), (self_in, 2), (self_out, 0)])
    rest_piece = piece(lax.axis_index("dp"), [(cross_weight, 0), (cross_weight, 1), (expand, 0), (expand, 1)])
    self_parts = steps.half_gathered(swapped_pipe(self_piece), (got,))
    self_half = self_parts[-1]
    (last_piece,) = kernel_call(last_kernel, (shaped(3 * D, D, BF),), (flags, expand, contract), scalars=1, after=(self_parts[-2],), direct=True)
    self_rest = steps.swap(self_half, 0)
    last_half = swapped_pipe(last_piece)
    rest = lax.all_gather(swapped_pipe(rest_piece), "dp").reshape(4 * D, D)

    table, bias, glance, places = row_layout(
        flags, lengths, hamming, priority.reshape(2 * T // WIN, WIN), copy_index.reshape(2 * T // WIN, WIN)
    )
    self_weights = (self_in, self_out, self_half, self_rest)
    (
        e_small, d_small, e_joined, e_mixed, e_stats, e_z1, x, d_joined, d_mixed, d_stats, d_z1,
    ) = first(table, flags, bias, glance, places, rows, got, self_weights, small, small_other)
    last_half = gate(last_half, (d_z1,))
    last_rest = steps.swap(last_half, 0)
    rest_weights = (cross_weight, expand, contract, rest, last_half, last_rest)
    (
        hidden, e_z2, memory, decoded, *dec_ff, d_ff_bias, d_ff_rows, d_cross, d_cross_bias, dstates, dz1,
    ) = middle(table, flags, bias, e_z1, d_z1, rest_weights, cotangent, e_small, d_small)

    def rows_swap(first, second):
        return swapped_pipe(jnp.where(leading, second, first).astype(BF))

    def rows_out(first, second, other):
        own, other = jnp.where(leading, first, second).astype(F32), other.astype(F32)
        return jnp.where(leading, jnp.concatenate([own, other], 0), jnp.concatenate([other, own], 0))[None]

    def opened(pair):
        return [part[None] for part in pair]

    layer_other = rows_swap(memory, decoded)
    dec_kept, dec_sent = opened(dec_ff)
    dec_got = steps.swap(dec_sent, 0)
    dec_kept, dec_sent = steps.halve(0, (dec_kept, dec_got))
    dec_got = steps.swap(dec_sent, 1)
    *dec_self, target_grad, copies_grad = decoder_self_back(
        table, flags, bias, dz1, x, d_joined, d_mixed, d_stats, glance, places, self_weights,
        d_cross, d_ff_bias, d_ff_rows, d_cross_bias, count, after=(dec_kept,),
    )
    dself_kept, dself_sent = opened(dec_self)
    dself_got = steps.swap(dself_sent, 0)
    dec_kept, dec_sent = steps.halve(1, (dec_kept, dec_got))
    dec_got = steps.swap(dec_sent, 2)
    e_cross, *enc_ff, e_ff_bias, e_ff_rows, e_dz1 = encoder_ff_back(
        flags, dstates, e_z1, e_z2, hidden, rest_weights, e_small, after=(dec_kept, target_grad)
    )
    enc_kept, enc_sent = opened(enc_ff)
    enc_got = steps.swap(enc_sent, 0)
    dself_kept, dself_sent = steps.halve(0, (dself_kept, dself_got))
    dself_got = steps.swap(dself_sent, 1)
    dec_kept, dec_sent = steps.halve(2, (dec_kept, dec_got))
    dec_got = steps.swap(dec_sent, 3)
    *enc_self, source_grad = encoder_self_back(
        table, flags, bias, e_dz1, rows, got, e_joined, e_mixed, e_stats, copies_grad, self_weights, e_small,
        e_cross, e_ff_bias, e_ff_rows, count, after=(dec_kept, dself_kept),
    )
    grad_other = rows_swap(source_grad, target_grad)
    self_kept, self_sent = opened(enc_self)
    self_got = steps.swap(self_sent, 0)
    enc_kept, enc_sent = steps.halve(0, (enc_kept, enc_got), after=(source_grad,))
    enc_got = steps.swap(enc_sent, 1)
    self_kept, self_sent = steps.halve(0, (self_kept, self_got))
    self_got = steps.swap(self_sent, 1)
    for step in range(3, steps.last):
        dec_kept, dec_sent = steps.halve(step, (dec_kept, dec_got))
        dec_got = steps.swap(dec_sent, step + 1)
    mark = (self_kept,)
    ff_step, self_step = 1, 1
    self_pairs = [(self_kept, self_got), (dself_kept, dself_got)]
    enc_pair = (enc_kept, enc_got)
    while ff_step < steps.last:
        kept, sent = steps.halve(ff_step, enc_pair, after=mark)
        ff_step += 1
        enc_pair = (kept, steps.swap(sent, ff_step))
        if self_step < steps.last:
            kept, sent = steps.halve(self_step, *self_pairs)
            self_step += 1
            self_pairs = [(kept, steps.swap(sent, self_step))]
            mark = (kept,)
    keep, send = steps.across(enc_pair, (dec_kept, dec_got), after=mark + (grad_other,))
    ff_got = swapped_pipe(send)
    keep_self, send_self = steps.across(*self_pairs)
    self_got = swapped_pipe(send_self)
    ff = added(keep, ff_got)
    ff_got = steps.swap(ff, steps.last)
    rest_sum = added(keep_self, self_got)
    self_got = steps.swap(rest_sum, steps.last)
    for step in range(steps.last, 0, -1):
        ff = steps.double(step, ff, ff_got, after=(rest_sum,))
        ff_got = steps.swap(ff, step - 1)
        rest_sum = steps.double(step, rest_sum, self_got)
        self_got = steps.swap(rest_sum, step - 1)

    layer_out = rows_out(memory, decoded, layer_other)
    embedding_grad = rows_out(source_grad, target_grad, grad_other)
    outs = (shaped(D, FF, F32), shaped(FF, D, F32))
    expand_grad, contract_grad = kernel_call(spill_ff_kernel, outs, (flags, ff, ff_got), scalars=1, direct=True)
    outs = (shaped(D, 3 * D, F32), shaped(D, D, F32), shaped(D, 2 * D, F32), shaped(1, FF, F32)) + (shaped(3, D, F32),) * 3
    in_grad, out_grad, cross_grad, *small_grads = kernel_call(spill_rest_kernel, outs, (flags, rest_sum, self_got), scalars=1, direct=True)
    return (
        layer_out,
        embedding_grad,
        in_grad[None],
        out_grad[None],
        cross_grad[None],
        expand_grad[None],
        contract_grad[None],
        small_grads[0],
        *(part[None] for part in small_grads[1:]),
    )


def solution(mesh):
    return jax.shard_map(
        per_device,
        mesh=mesh,
        in_specs=(
            P("pipe", "dp", None),
            P("dp", None),
            P("dp", None),
            P("dp"),
            P("dp"),
            P("dp", None),
            P("pipe", None, None),
            P("pipe", None, None),
            P("pipe", None, None),
            P("pipe", None, None),
            P("pipe", None, None),
            P("pipe", None),
            P("pipe", None, None),
            P("pipe", None, None),
            P("pipe", None, None),
        ),
        out_specs=(
            P("pipe", "dp", None),
            P("pipe", "dp", None),
            P("pipe", None, None),
            P("pipe", None, None),
            P("pipe", None, None),
            P("pipe", None, None),
            P("pipe", None, None),
            P("pipe", None),
            P("pipe", None, None),
            P("pipe", None, None),
            P("pipe", None, None),
        ),
        check_vma=False,
    )
```

```python
import functools
import math

import jax
import jax.numpy as jnp
from jax import lax
from jax.experimental import pallas as pl
from jax.experimental.pallas import tpu as pltpu
from jax.sharding import PartitionSpec as P

HEADS = 8
D = 512
FF = 2048
T = 1024
SENTS = 17
WIN = 128
EPSILON = 1e-05
NEG = -1e30
BF = jnp.bfloat16
F32 = jnp.float32
VMEM = pl.BlockSpec(memory_space=pltpu.VMEM)
SMEM = pl.BlockSpec(memory_space=pltpu.SMEM)
BLOCK = 512
STEPS = T // BLOCK


def nn(a, b):
    return jnp.dot(a, b, preferred_element_type=F32)


def nt(a, b):
    return lax.dot_general(a, b, (((1,), (1,)), ((), ())), preferred_element_type=F32)


def tn(a, b):
    return lax.dot_general(a, b, (((0,), (0,)), ((), ())), preferred_element_type=F32)


def normalized(value):
    center = jnp.mean(value, axis=-1, keepdims=True)
    centered = value - center
    spread = jnp.mean(centered * centered, axis=-1, keepdims=True)
    scale = lax.rsqrt(spread + EPSILON)
    return centered * scale, scale


def normalized_back(grad, unit, scale):
    first = jnp.mean(grad, axis=-1, keepdims=True)
    second = jnp.mean(grad * unit, axis=-1, keepdims=True)
    return scale * (grad - first - unit * second)


def folded(value):
    return jnp.sum(value.reshape(value.shape[0] // 8, 8, value.shape[1]), axis=0)


def column_sum(value):
    return jnp.sum(value, axis=0, keepdims=True)


def each_block(body):
    for index in range(STEPS):
        body(pl.ds(index * BLOCK, BLOCK))


def each_chunk(count, size, body):
    def step(index, carry):
        body(pl.multiple_of(index * size, size))
        return carry

    lax.fori_loop(0, count, step, 0)


class Held:
    def __init__(self, ref, copy):
        self.ref, self.copy = ref, copy

    def ready(self):
        if self.copy is not None:
            self.copy.wait()
            self.copy = None
        return self.ref

    def __getitem__(self, index):
        return self.ready()[index]

    @property
    def at(self):
        return self.ready().at

    @property
    def shape(self):
        return self.ref.shape


def ready(value):
    return value.ready() if isinstance(value, (Held, Landing)) else value


LEAVING = {}


def leave(*refs):
    for ref in refs:
        copy, started = LEAVING.get(id(ref), (None, True))
        if not started:
            copy.start()
            LEAVING[id(ref)] = (copy, True)


class Landing:
    def __init__(self, ref, sem):
        self.ref, self.sem = ref, sem

    def ready(self):
        if self.sem is not None:
            pltpu.make_async_copy(self.ref, self.ref, self.sem).wait()
            self.sem = None
        return self.ref

    def __getitem__(self, index):
        return self.ready()[index]

    @property
    def at(self):
        return self.ready().at

    @property
    def shape(self):
        return self.ref.shape


class Raw:
    def __init__(self, value):
        self.value, self.shape, self.dtype = value, value.shape, value.dtype


def bytes_of(x):
    return math.prod(x.shape) * jnp.dtype(x.dtype).itemsize


LARGE = 256 << 10


def kernel_call(body, outs, operands, scalars=0, scratch=(), out_specs=None, flops=0, after=(), direct=False, weight=20, room_for=52):
    size = sum(bytes_of(x) for x in (*operands, *outs))
    held = size + (sum(bytes_of(x) for x in scratch) if direct else 0)
    count, many, extra = len(operands), len(outs), len(scratch)
    raw = [isinstance(x, Raw) for x in operands]
    comes = [not (direct or r) and i >= scalars and bytes_of(x) >= LARGE for i, (x, r) in enumerate(zip(operands, raw))]
    goes = [not direct and bytes_of(x) >= LARGE for x in outs]
    anywhere = pl.BlockSpec(memory_space=pl.ANY)
    in_specs = [SMEM] * scalars + [anywhere if c or r else VMEM for c, r in zip(comes[scalars:], raw[scalars:])] + [anywhere] * len(after)
    specs = list(out_specs) if out_specs else [VMEM] * many
    specs = [anywhere if g else spec for g, spec in zip(goes, specs)]
    room = [pltpu.VMEM(x.shape, x.dtype) for x, c in zip((*operands, *outs), comes + goes) if c]
    sems = [pltpu.SemaphoreType.DMA((len(room),))] if room else []

    def run(*refs):
        ins, rest = list(refs[:count]), refs[count + len(after) :]
        results, rest = list(rest[:many]), rest[many:]
        own, rest = rest[:extra], rest[extra:]
        buffers, slot = rest[: len(room)], 0
        for i, c in enumerate(comes):
            if c:
                copy = pltpu.make_async_copy(ins[i], buffers[slot], rest[-1].at[slot])
                copy.start()
                ins[i] = Held(buffers[slot], copy)
                slot += 1
        LEAVING.clear()
        for i, g in enumerate(goes):
            if g:
                copy = pltpu.make_async_copy(buffers[slot], results[i], rest[-1].at[slot])
                results[i] = buffers[slot]
                LEAVING[id(results[i])] = (copy, False)
                slot += 1
        body(*ins, *results, *own)
        for value in ins:
            ready(value)
        for i, g in enumerate(goes):
            if g:
                leave(results[i])
        for i, g in enumerate(goes):
            if g:
                LEAVING[id(results[i])][0].wait()
        LEAVING.clear()

    return pl.pallas_call(
        run,
        out_shape=tuple(outs),
        in_specs=in_specs,
        out_specs=tuple(specs),
        scratch_shapes=list(scratch) + room + sems,
        compiler_params=pltpu.CompilerParams(vmem_limit_bytes=held + (3 << 20) if direct else room_for << 20),
        cost_estimate=pl.CostEstimate(flops=weight * (flops or 2 * FLOP_UNIT), bytes_accessed=weight * size, transcendentals=0),
    )(*(x.value if isinstance(x, Raw) else x for x in operands), *after)


def shaped(rows, columns, kind):
    return jax.ShapeDtypeStruct((rows, columns), kind)


def layout_kernel(flags, lengths, hamming, priority, copies, table, bias, glance, places):
    row = flags[0, 0]
    ends = []
    total = jnp.int32(0)
    for j in range(SENTS):
        total = total + lengths[row, j]
        ends.append(total)
    count = jnp.int32(0)
    first = jnp.int32(0)

    def origin(start):
        return jnp.minimum((start // 16) * 16, T - WIN)

    for j in range(SENTS):
        begin = jnp.int32(0) if j == 0 else ends[j - 1]
        opens = (ends[j] - origin(first)) > WIN
        if j == 0:
            opens = jnp.bool_(False)
        first = jnp.where(opens, begin, first)
        count = jnp.where(opens, count + 1, count)
        table[0, 1 + count] = origin(first)
        table[0, 32 + count] = first
        table[0, 64 + count] = ends[j]
    table[0, 0] = count + 1

    lanes = lax.broadcasted_iota(jnp.int32, (8, WIN), 1)
    rows = lax.broadcasted_iota(jnp.int32, (8, WIN), 0)
    place = rows * WIN + lanes
    quota = jnp.zeros((8, WIN), jnp.int32) + (hamming[row, 0] + 1) // 2
    for j in range(SENTS - 1):
        change = (hamming[row, j + 1] + 1) // 2 - (hamming[row, j] + 1) // 2
        quota = quota + jnp.where(place >= ends[j], change, 0)
    part = pl.ds(pl.multiple_of(row * (T // WIN), 8), T // WIN)
    chosen = jnp.where(priority[part, :] < quota, 1.0, 0.0)
    copy = copies[part, :].astype(F32)
    for i in range(T // WIN):
        part = pl.ds(i * WIN, WIN)
        glance[part, :] = jnp.broadcast_to(chosen[i : i + 1, :], (WIN, WIN)).T
        places[part, :] = jnp.broadcast_to(copy[i : i + 1, :], (WIN, WIN)).T.astype(jnp.int32)

    def window(w, carry):
        at = table[0, 1 + w]
        here = lanes + at
        segment = jnp.zeros((8, WIN), F32)
        for j in range(SENTS):
            segment = segment + jnp.where(here >= ends[j], 1.0, 0.0)
        inside = (here >= table[0, 32 + w]) & (here < table[0, 64 + w])
        segment = jnp.where(inside, segment, -1.0)
        across = jnp.broadcast_to(segment[0:1, :], (WIN, WIN))
        down = across.T
        bias[w] = jnp.where((across == down) & (across >= 0.0), 0.0, NEG)
        return carry

    lax.fori_loop(0, count + 1, window, 0)
    table[0, 2 + count] = 0
    bias[count + 1] = jnp.full((WIN, WIN), NEG, F32)


def row_layout(flags, lengths, hamming, priority, copies):
    outs = (
        shaped(1, 128, jnp.int32),
        jax.ShapeDtypeStruct((SENTS + 1, WIN, WIN), F32),
        shaped(T, WIN, F32),
        shaped(T, WIN, jnp.int32),
    )
    return kernel_call(
        layout_kernel,
        outs,
        (flags, lengths, hamming, priority, copies),
        scalars=3,
        out_specs=(SMEM, VMEM, VMEM, VMEM),
        direct=True,
        weight=0,
    )


def pair_halves(part):
    low = lax.broadcasted_iota(jnp.int32, (WIN, WIN), 1) < 64
    zero = jnp.zeros_like(part)
    return jnp.concatenate([jnp.where(low, part, zero), jnp.where(low, zero, part)], axis=0)


def pair_join(both):
    low = lax.broadcasted_iota(jnp.int32, (WIN, WIN), 1) < 64
    return jnp.where(low, both[:WIN], both[WIN:])


PAIRS = [slice(i * 128, i * 128 + 128) for i in range(HEADS // 2)]


PAIRS = [slice(i * 128, i * 128 + 128) for i in range(HEADS // 2)]
GROUP = 2


def grouped(table, body):
    def step(index, carry):
        body([index * GROUP + i for i in range(GROUP)])
        return carry

    lax.fori_loop(0, (table[0, 0] + GROUP - 1) // GROUP, step, 0)


def spread(table, windows):
    ats = [pl.ds(pl.multiple_of(table[0, 1 + w], 16), WIN) for w in windows]
    return [(w, pair, at, lanes) for w, at in zip(windows, ats) for pair, lanes in enumerate(PAIRS)]


def masks(bias, windows):
    out = []
    for w in windows:
        masked = bias[w]
        out += [jnp.concatenate([masked, masked], axis=1)] * len(PAIRS)
    return out


def attend(table, bias, queries, keys, values, mixed, stats):
    bias, queries, keys, values = map(ready, (bias, queries, keys, values))

    def body(windows):
        parts = spread(table, windows)
        masked = masks(bias, windows)
        query = [pair_halves(queries[at, lanes]) for _, _, at, lanes in parts]
        key = [keys[at, lanes] for _, _, at, lanes in parts]
        value = [values[at, lanes] for _, _, at, lanes in parts]
        scores = [nt(k, q) + mask for k, q, mask in zip(key, query, masked)]
        highest = [jnp.maximum(jnp.max(s, axis=0, keepdims=True), -1e29) for s in scores]
        raised = [jnp.exp(s - h) for s, h in zip(scores, highest)]
        inverse = [1.0 / jnp.maximum(jnp.sum(r, axis=0, keepdims=True), 1e-30) for r in raised]
        shares = [(r * i).astype(BF) for r, i in zip(raised, inverse)]
        out = [pair_join(tn(s, v)).astype(BF) for s, v in zip(shares, value)]
        for (w, pair, at, lanes), o, h, i in zip(parts, out, highest, inverse):
            mixed[at, lanes] = mixed[at, lanes] + o
            stats[w * 4 + pair, 0:1, :] = h
            stats[w * 4 + pair, 1:2, :] = i

    mixed[...] = jnp.zeros_like(mixed)
    grouped(table, body)


def attend_back(table, bias, queries, keys, values, stats, grad, grad_q, grad_k, grad_v):
    bias, queries, keys, values, stats = map(ready, (bias, queries, keys, values, stats))

    def body(windows):
        parts = spread(table, windows)
        masked = masks(bias, windows)
        query = [pair_halves(queries[at, lanes]) for _, _, at, lanes in parts]
        key = [keys[at, lanes] for _, _, at, lanes in parts]
        value = [values[at, lanes] for _, _, at, lanes in parts]
        out = [pair_halves(grad[at, lanes]) for _, _, at, lanes in parts]
        top = [stats[w * 4 + pair, 0:1, :] for w, pair, _, _ in parts]
        inverse = [stats[w * 4 + pair, 1:2, :] for w, pair, _, _ in parts]
        scores = [nt(k, q) + mask for k, q, mask in zip(key, query, masked)]
        back = [nt(v, o) for v, o in zip(value, out)]
        shares = [jnp.exp(s - h) * i for s, h, i in zip(scores, top, inverse)]
        got_v = [nn(s.astype(BF), o).astype(BF) for s, o in zip(shares, out)]
        total = [jnp.sum(s * b, axis=0, keepdims=True) for s, b in zip(shares, back)]
        scored = [(s * (b - t)).astype(BF) for s, b, t in zip(shares, back, total)]
        got_k = [nn(s, q).astype(BF) for s, q in zip(scored, query)]
        got_q = [(pair_join(tn(s, k)) * 0.125).astype(BF) for s, k in zip(scored, key)]
        for ref, got in zip((grad_q, grad_k, grad_v), (got_q, got_k, got_v)):
            for (_, _, at, lanes), value_got in zip(parts, got):
                ref[at, lanes] = ref[at, lanes] + value_got

    for ref in (grad_q, grad_k, grad_v):
        ref[...] = jnp.zeros_like(ref)
    grouped(table, body)


STATS = jax.ShapeDtypeStruct(((SENTS + 1) * 4, 2, 2 * WIN), F32)


def thirds(ref):
    return tuple(ref.at[:, i * D : (i + 1) * D] for i in range(ref.shape[1] // D))


def put(flags, half, kept, sent, rows, value):
    @pl.when(flags[0, 1] == half)
    def _():
        kept[rows, :] = value

    @pl.when(flags[0, 1] != half)
    def _():
        sent[rows, :] = value


def put_side(flags, side, mine, theirs, rows, value):
    @pl.when(flags[0, 0] == side)
    def _():
        mine[rows, :] = value

    @pl.when(flags[0, 0] != side)
    def _():
        theirs[rows, :] = value


def rows_at(start, count=D):
    return slice(start, start + count)


def scaled(unit, small, slot):
    return unit * small[7 + slot : 8 + slot, :] + small[10 + slot : 11 + slot, :]


def project(x, weight_in, joined, at):
    got = nn(x, weight_in[...])
    joined[at, :D] = (got[:, :D] * 0.125).astype(BF)
    joined[at, D:] = got[:, D:].astype(BF)


def encoder_self_kernel(table, bias, source, weight_in, weight_out, small, joined, mixed, stats, z, x):
    def before(at):
        unit, _ = normalized(source[at, :].astype(F32))
        value = scaled(unit, small, 2)
        x[at, :] = value
        project(value.astype(BF), weight_in, joined, at)

    each_block(before)
    leave(joined)
    attend(table, bias, *thirds(joined), mixed, stats)
    leave(mixed, stats)

    def after(at):
        z[at, :] = x[at, :] + nn(mixed[at, :], weight_out[...]) + small[4:5, :]

    each_block(after)


def copy_hits(bias, places, w, start):
    at = pl.ds(start, WIN)
    lanes = lax.broadcasted_iota(jnp.int32, (WIN, WIN), 1) + start
    inside = jnp.max(bias[w], axis=1, keepdims=True) == 0.0
    return at, jnp.where((places[at, :] == lanes) & inside, 1.0, 0.0).astype(BF)


def kept_rows(glance, at):
    return jnp.concatenate([glance[at, :]] * (D // WIN), axis=1) > 0.5


def decoder_self_kernel(
    table, bias, source, target, glance, places, weight_in, weight_out, small, x, joined, mixed, stats, z, copied
):
    copied[...] = jnp.zeros_like(copied)
    bias, places, source = map(ready, (bias, places, source))

    def gather(windows):
        parts = [copy_hits(bias, places, w, pl.multiple_of(table[0, 1 + w], 16)) for w in windows]
        got = [nn(hit, source[at, :]).astype(BF) for at, hit in parts]
        for (at, _), value in zip(parts, got):
            copied[at, :] = copied[at, :] + value

    grouped(table, gather)

    def before(at):
        value = jnp.where(kept_rows(glance, at), target[at, :].astype(F32), copied[at, :].astype(F32)).astype(BF)
        x[at, :] = value
        project(value, weight_in, joined, at)

    each_block(before)
    leave(joined)
    attend(table, bias, *thirds(joined), mixed, stats)
    leave(mixed, stats)

    def after(at):
        z[at, :] = x[at, :].astype(F32) + nn(mixed[at, :], weight_out[...]) + small[4:5, :]

    each_block(after)


FLOP_UNIT = 2 * T * D * D


ROOT = 0.7978845608028654
CUBE = 0.044715


def gelu_parts(u):
    square = u * u
    bent = jnp.tanh(u * (ROOT + ROOT * CUBE * square))
    half = 0.5 + 0.5 * bent
    slope = half + (u - u * (bent * bent)) * (0.5 * ROOT + 1.5 * ROOT * CUBE * square)
    return u * half, slope


def expand_block(value, expand, small, active, slope, at):
    for j in range(FF // D):
        cols = rows_at(j * D)
        hidden = (nn(value, expand[:, cols]) + small[j : j + 1, :]).astype(BF)
        active[at, cols], slope[at, cols] = gelu_parts(hidden)


def encoder_ff_kernel(flags, z1, expand, contract, cross, small, inner, z2, mine, theirs, states, active):
    def block(at):
        unit, _ = normalized(z1[at, :])
        value = scaled(unit, small, 0)
        for j in range(FF // D):
            cols = rows_at(j * D)
            hidden = (nn(value.astype(BF), expand[:, cols]) + small[j : j + 1, :]).astype(BF)
            inner[at, cols] = hidden
            active[at, cols], _ = gelu_parts(hidden)
        total = value + nn(active[at, :], contract[...]) + small[5:6, :]
        z2[at, :] = total
        unit, _ = normalized(total)
        out = scaled(unit, small, 1)
        put_side(flags, 0, mine, theirs, at, out.astype(BF))
        got = nn(out.astype(BF), cross[...])
        states[at, :D] = got[:, :D].astype(BF)
        states[at, D:] = (got[:, D:] + small[6:7, :]).astype(BF)

    each_block(block)
    leave(inner, z2)


def ff_back(flags, dzb, value_b, active, inner, contract, kept, sent, bias_rows):
    def block(at):
        for j in range(FF // D):
            cols = rows_at(j * D)
            back = nt(dzb[at, :], contract[cols, :])
            inner[at, cols] = (back * inner[at, cols].astype(F32)).astype(BF)

    each_block(block)
    for c in range(FF // D):
        cols = rows_at(c * D)
        put(flags, 1, kept, sent, cols, tn(active[:, cols], dzb[...]).astype(BF))
        put(flags, 0, kept, sent, cols, tn(value_b[...], inner[:, cols]).astype(BF))
        bias_rows[c : c + 1, :] = column_sum(inner[:, cols].astype(F32))


def decoder_ff_kernel(
    flags, z2, expand, contract, small, cotangent,
    mine, theirs, kept, sent, bias_grads, bias_rows, dz2,
    active, inner, value_b, dz, dzb,
):
    bias_grads[...] = jnp.zeros_like(bias_grads)
    offset = flags[0, 0] * T

    def block(at):
        unit, _ = normalized(z2[at, :])
        value = scaled(unit, small, 1)
        value_b[at, :] = value.astype(BF)
        expand_block(value.astype(BF), expand, small, active, inner, at)
        total = value + nn(active[at, :], contract[...]) + small[5:6, :]
        unit, scale = normalized(total)
        put_side(flags, 1, mine, theirs, at, scaled(unit, small, 2).astype(BF))
        wanted = cotangent[pl.ds(pl.multiple_of(offset + at.start, BLOCK), BLOCK), :].astype(F32)
        bias_grads[0:1, :] += column_sum(wanted * unit)
        bias_grads[1:2, :] += column_sum(wanted)
        back = normalized_back(wanted * small[9:10, :], unit, scale)
        bias_grads[2:3, :] += column_sum(back)
        dz[at, :] = back
        dzb[at, :] = back.astype(BF)

    each_block(block)
    leave(mine, theirs)
    ff_back(flags, dzb, value_b, active, inner, contract, kept, sent, bias_rows)

    def last(at):
        back = dz[at, :] + nt(inner[at, :], expand[...])
        unit, scale = normalized(z2[at, :])
        bias_grads[3:4, :] += column_sum(back * unit)
        bias_grads[4:5, :] += column_sum(back)
        dz2[at, :] = normalized_back(back * small[8:9, :], unit, scale)

    each_block(last)


def encoder_ff_back_kernel(
    flags, z2, dstates, z1, hidden, own_cross, own_expand, own_contract, rest, half, last_half, small,
    kept, sent, bias_grads, bias_rows, inner, dz,
    cross, contract, active, value_b, memory_b, dzb, sems,
):
    own = (own_cross, own_expand, own_contract, rest, half, last_half)
    cross, _, contract = fetch_rest(0, flags, *own, cross, None, contract, sems)
    bias_grads[...] = jnp.zeros_like(bias_grads)

    def block(at):
        unit, scale = normalized(z2[at, :])
        memory_b[at, :] = scaled(unit, small, 1).astype(BF)
        back = nt(dstates[at, :], cross[...])
        bias_grads[0:1, :] += column_sum(dstates[at, D:].astype(F32))
        bias_grads[1:2, :] += column_sum(back * unit)
        bias_grads[2:3, :] += column_sum(back)
        back = normalized_back(back * small[8:9, :], unit, scale)
        bias_grads[3:4, :] += column_sum(back)
        dz[at, :] = back
        dzb[at, :] = back.astype(BF)
        unit, _ = normalized(z1[at, :])
        value_b[at, :] = scaled(unit, small, 0).astype(BF)
        for j in range(FF // D):
            cols = rows_at(j * D)
            active[at, cols], inner[at, cols] = gelu_parts(hidden[at, cols])

    each_block(block)
    leave(dz)
    ff_back(flags, dzb, value_b, active, inner, contract, kept, sent, bias_rows)
    leave(inner)
    for c in range(2):
        put(flags, c, kept, sent, rows_at(FF), tn(memory_b[...], dstates[:, rows_at(c * D)]).astype(BF))


def encoder_ff_back(flags, dstates, z1, z2, hidden, weights, small, after=()):
    outs = (
        shaped(FF + D, D, BF), shaped(FF + D, D, BF),
        shaped(8, D, F32), shaped(8, D, F32), shaped(T, FF, BF), shaped(T, D, F32),
    )
    return kernel_call(
        encoder_ff_back_kernel,
        outs,
        (flags, z2, dstates, z1, hidden, *map(Raw, weights), small),
        scalars=1,
        scratch=[
            pltpu.VMEM((D, 2 * D), BF),
            pltpu.VMEM((FF, D), BF),
            pltpu.VMEM((T, FF), BF),
            pltpu.VMEM((T, D), BF),
            pltpu.VMEM((T, D), BF),
            pltpu.VMEM((T, D), BF),
            pltpu.SemaphoreType.DMA((3,)),
        ],
        flops=18 * FLOP_UNIT,
        after=after,
    )


def encoder_ff_last_kernel(
    flags, inner, dz, z1, own_cross, own_expand, own_contract, rest, half, last_half, small,
    bias_grads, dz1,
    expand, sems,
):
    own = (own_cross, own_expand, own_contract, rest, half, last_half)
    _, expand, _ = fetch_rest(0, flags, *own, None, expand, None, sems)
    bias_grads[...] = jnp.zeros_like(bias_grads)

    def last(at):
        back = dz[at, :] + nt(inner[at, :], expand[...])
        unit, scale = normalized(z1[at, :])
        bias_grads[4:5, :] += column_sum(back * unit)
        bias_grads[5:6, :] += column_sum(back)
        dz1[at, :] = normalized_back(back * small[7:8, :], unit, scale)

    each_block(last)


def encoder_ff_last(flags, inner, dz, z1, weights, small, after=()):
    return kernel_call(
        encoder_ff_last_kernel,
        (shaped(8, D, F32), shaped(T, D, F32)),
        (flags, inner, dz, z1, *map(Raw, weights), small),
        scalars=1,
        scratch=[pltpu.VMEM((D, FF), BF), pltpu.SemaphoreType.DMA((3,))],
        flops=4 * FLOP_UNIT,
        after=after,
    )


def decoder_cross_kernel(table, bias, z1, states, weight, small, queries, mixed, stats, z2, x):
    def before(at):
        unit, _ = normalized(z1[at, :])
        value = scaled(unit, small, 0)
        x[at, :] = value
        queries[at, :] = (nn(value.astype(BF), weight[:, :D]) * 0.125).astype(BF)

    each_block(before)
    attend(table, bias, queries, *thirds(states), mixed, stats)

    def after(at):
        z2[at, :] = x[at, :] + nn(mixed[at, :], weight[:, D:]) + small[6:7, :]

    each_block(after)


def decoder_cross_back_kernel(
    table, flags, bias, dz2, z1, queries, states, mixed, stats, weight, small,
    kept, sent, bias_grads, dstates, dz1,
    value_b, dzb, out, dq,
):
    bias_grads[...] = jnp.zeros_like(bias_grads)

    def before(at):
        bias_grads[0:1, :] += column_sum(dz2[at, :])
        low = dz2[at, :].astype(BF)
        dzb[at, :] = low
        out[at, :] = nt(low, weight[:, D:]).astype(BF)
        unit, _ = normalized(z1[at, :])
        value_b[at, :] = scaled(unit, small, 0).astype(BF)

    each_block(before)
    attend_back(table, bias, queries, *thirds(states), stats, out, dq, *thirds(dstates))
    leave(dstates)
    put(flags, 0, kept, sent, rows_at(FF), tn(value_b[...], dq[...]).astype(BF))
    put(flags, 1, kept, sent, rows_at(FF), tn(mixed[...], dzb[...]).astype(BF))
    leave(kept, sent)

    def after(at):
        back = dz2[at, :] + nt(dq[at, :], weight[:, :D])
        unit, scale = normalized(z1[at, :])
        bias_grads[1:2, :] += column_sum(back * unit)
        bias_grads[2:3, :] += column_sum(back)
        dz1[at, :] = normalized_back(back * small[7:8, :], unit, scale)

    each_block(after)


def self_back(table, bias, flags, dz, x, joined, mixed, stats, weight_in, weight_out, kept, sent, acc, dzb, out, djoined):
    acc[...] = jnp.zeros_like(acc)

    def before(at):
        acc[0:1, :] += column_sum(dz[at, :])
        low = dz[at, :].astype(BF)
        dzb[at, :] = low
        out[at, :] = nt(low, weight_out[...]).astype(BF)

    each_block(before)
    attend_back(table, bias, *thirds(joined), stats, out, *thirds(djoined))
    for c in range(3):
        value = tn(x[...], djoined[:, rows_at(c * D)]).astype(BF)
        put(flags, c // 2, kept, sent, rows_at(c % 2 * D), value)
    put(flags, 1, kept, sent, rows_at(D), tn(mixed[...], dzb[...]).astype(BF))


def put_small(flags, kept, sent, rows):
    count = kept.shape[0] - 2 * D
    at = rows_at(2 * D, count)
    filled = jnp.concatenate(rows + [jnp.zeros((count - 13, D), F32)], axis=0).astype(BF)
    put(flags, 0, kept, sent, at, filled)
    put(flags, 1, kept, sent, at, jnp.zeros((count, D), BF))


def decoder_self_back_kernel(
    table, flags, dz, own_in, own_out, half, rest, joined, bias, stats, x, mixed, glance, places,
    ff_bias, ff_rows, cross_bias,
    kept, sent, target_grad, source_grad,
    weight_in, weight_out, acc, dzb, out, djoined, dcopied, sems,
):
    weight_in, weight_out = fetch_self(1, flags, own_in, own_out, half, rest, weight_in, weight_out, sems)
    self_back(table, bias, flags, dz, x, joined, mixed, stats, weight_in, weight_out, kept, sent, acc, dzb, out, djoined)
    put_small(
        flags, kept, sent,
        [
            ff_rows[0:4, :], acc[0:1, :], ff_bias[2:3, :], cross_bias[0:1, :],
            cross_bias[1:2, :], ff_bias[3:4, :], ff_bias[0:1, :],
            cross_bias[2:3, :], ff_bias[4:5, :], ff_bias[1:2, :],
        ],
    )

    def after(at):
        back = dz[at, :] + nt(djoined[at, :], weight_in[...])
        kept_at = kept_rows(glance, at)
        target_grad[at, :] = jnp.where(kept_at, back, 0.0).astype(BF)
        dcopied[at, :] = jnp.where(kept_at, 0.0, back).astype(BF)

    each_block(after)
    leave(target_grad, kept, sent)
    source_grad[...] = jnp.zeros_like(source_grad)
    bias, places = ready(bias), ready(places)

    def scatter(windows):
        parts = [copy_hits(bias, places, w, pl.multiple_of(table[0, 1 + w], 16)) for w in windows]
        got = [tn(hit, dcopied[at, :]).astype(BF) for at, hit in parts]
        for (at, _), value in zip(parts, got):
            source_grad[at, :] = source_grad[at, :] + value

    grouped(table, scatter)


def half_rows(count):
    return 2 * D + 8 * count


def decoder_self_back(table, flags, bias, dz, x, joined, mixed, stats, glance, places, weights, ff_bias, ff_rows, cross_bias, count, after=()):
    half = half_rows(count)
    outs = (shaped(half, D, BF), shaped(half, D, BF), shaped(T, D, BF), shaped(T, D, BF))
    return kernel_call(
        decoder_self_back_kernel,
        outs,
        (table, flags, dz, *map(Raw, weights), joined, bias, stats, x, mixed, glance, places, ff_bias, ff_rows, cross_bias),
        scalars=2,
        scratch=[
            pltpu.VMEM((D, 3 * D), BF), pltpu.VMEM((D, D), BF),
            pltpu.VMEM((8, D), F32), pltpu.VMEM((T, D), BF), pltpu.VMEM((T, D), BF),
            pltpu.VMEM((T, 3 * D), BF), pltpu.VMEM((T, D), BF), pltpu.SemaphoreType.DMA((2,)),
        ],
        flops=18 * FLOP_UNIT,
        after=after,
    )


def encoder_self_back_kernel(
    table, flags, dz, rows, got_0, got_1, own_in, own_out, half, rest, joined, bias, stats, mixed, copies_grad, small,
    ff_bias, ff_rows, last_bias, target_grad,
    kept, sent, mine, theirs,
    source, weight_in, weight_out, acc, x, dzb, out, djoined, sems,
):
    @pl.when(flags[0, 0] == 0)
    def _():
        start((rows.at[rows_at(0, T), :], source, sems.at[2]))

    @pl.when(flags[0, 0] != 0)
    def _():
        start(*row_parts((got_0, got_1), source, sems.at[2]))

    source = Landing(source, sems.at[2])
    weight_in, weight_out = fetch_self(0, flags, own_in, own_out, half, rest, weight_in, weight_out, sems)

    def first(at):
        unit, _ = normalized(source[at, :].astype(F32))
        x[at, :] = scaled(unit, small, 2).astype(BF)

    each_block(first)
    self_back(table, bias, flags, dz, x, joined, mixed, stats, weight_in, weight_out, kept, sent, acc, dzb, out, djoined)

    def after(at):
        back = dz[at, :] + nt(djoined[at, :], weight_in[...])
        unit, scale = normalized(source[at, :].astype(F32))
        acc[1:2, :] += column_sum(back * unit)
        acc[2:3, :] += column_sum(back)
        value = normalized_back(back * small[9:10, :], unit, scale) + copies_grad[at, :].astype(F32)
        put_side(flags, 0, mine, theirs, at, value.astype(BF))
        put_side(flags, 1, mine, theirs, at, target_grad[at, :])

    each_block(after)
    put_small(
        flags, kept, sent,
        [
            ff_rows[0:4, :], acc[0:1, :], ff_bias[3:4, :], ff_bias[0:1, :],
            last_bias[4:5, :], ff_bias[1:2, :], acc[1:2, :],
            last_bias[5:6, :], ff_bias[2:3, :], acc[2:3, :],
        ],
    )


def encoder_self_back(table, flags, bias, dz, rows, got, joined, mixed, stats, copies_grad, weights, small, ff_bias, ff_rows, last_bias, target_grad, count, after=()):
    half = half_rows(count)
    outs = (shaped(half, D, BF), shaped(half, D, BF), shaped(T, D, BF), shaped(T, D, BF))
    return kernel_call(
        encoder_self_back_kernel,
        outs,
        (table, flags, dz, Raw(rows), *map(Raw, got), *map(Raw, weights), joined, bias, stats, mixed, copies_grad, small, ff_bias, ff_rows, last_bias, target_grad),
        scalars=2,
        scratch=[
            pltpu.VMEM((T, D), BF), pltpu.VMEM((D, 3 * D), BF), pltpu.VMEM((D, D), BF),
            pltpu.VMEM((8, D), F32), pltpu.VMEM((T, D), BF), pltpu.VMEM((T, D), BF), pltpu.VMEM((T, D), BF),
            pltpu.VMEM((T, 3 * D), BF), pltpu.SemaphoreType.DMA((3,)),
        ],
        flops=18 * FLOP_UNIT,
        after=after,
    )


def start(*copies):
    for source, target, sem in copies:
        pltpu.make_async_copy(source, target, sem).start()


def fetch_self(layer, flags, own_in, own_out, half, rest, to_in, to_out, sems):
    own = flags[0, 0] == layer

    def other(low, high):
        start(
            (high.at[rows_at(D), :], to_out, sems.at[1]),
            (low.at[rows_at(0), :], to_in.at[:, rows_at(0)], sems.at[0]),
            (low.at[rows_at(D), :], to_in.at[:, rows_at(D)], sems.at[0]),
            (high.at[rows_at(0), :], to_in.at[:, rows_at(2 * D)], sems.at[0]),
        )

    pl.when(own)(lambda: start((own_out, to_out, sems.at[1]), (own_in, to_in, sems.at[0])))
    pl.when(jnp.logical_not(own) & (flags[0, 1] == 0))(lambda: other(half, rest))
    pl.when(jnp.logical_not(own) & (flags[0, 1] != 0))(lambda: other(rest, half))
    return Landing(to_in, sems.at[0]), Landing(to_out, sems.at[1])


def fetch_rest(layer, flags, own_cross, own_expand, own_contract, rest, half, last, cross, expand, contract, sems):
    own = flags[0, 0] == layer

    def other(low, high):
        copies = [(rest.at[rows_at((2 + j) * D), :], expand.at[:, rows_at(j * D)], 1) for j in range(2)] if expand is not None else []
        copies += [(low.at[rows_at(j * D), :], expand.at[:, rows_at((2 + j) * D)], 1) for j in range(2)] if expand is not None else []
        if contract is not None:
            copies.append((low.at[rows_at(2 * D), :], contract.at[rows_at(0), :], 2))
            copies.append((high, contract.at[rows_at(D, 3 * D), :], 2))
        if cross is not None:
            copies += [(rest.at[rows_at(j * D), :], cross.at[:, rows_at(j * D)], 0) for j in range(2)]
        start(*((source, target, sems.at[i]) for source, target, i in copies))

    pairs = ((own_expand, expand, 1), (own_contract, contract, 2), (own_cross, cross, 0))
    pl.when(own)(lambda: start(*((source, target, sems.at[i]) for source, target, i in pairs if target is not None)))
    pl.when(jnp.logical_not(own) & (flags[0, 1] == 0))(lambda: other(half, last))
    pl.when(jnp.logical_not(own) & (flags[0, 1] != 0))(lambda: other(last, half))
    return tuple(ref if ref is None else Landing(ref, sems.at[i]) for i, ref in enumerate((cross, expand, contract)))


PARTS = ((0, 384), (384, 640))


def row_parts(parts, to, sem):
    return [(part, to.at[rows_at(at, size), :], sem) for part, (at, size) in zip(parts, PARTS)]


def fetch_rows(flags, rows, got, source, target, sems):
    @pl.when(flags[0, 0] == 0)
    def _():
        start((rows.at[rows_at(0, T), :], source, sems.at[0]), *row_parts(got, target, sems.at[1]))

    @pl.when(flags[0, 0] != 0)
    def _():
        start(*row_parts(got, source, sems.at[0]), (rows.at[rows_at(T, T), :], target, sems.at[1]))

    return Landing(source, sems.at[0]), Landing(target, sems.at[1])


def first_kernel(
    table, flags, rows, got_0, got_1, own_in, own_out, half, rest, bias, glance, places, small, small_other,
    e_small, d_small, e_joined, e_mixed, e_stats, e_z, x, d_joined, d_mixed, d_stats, d_z,
    source, target, e_in, e_out, d_in, d_out, wide, copied, sems,
):
    source, target = fetch_rows(flags, rows, (got_0, got_1), source, target, sems.at[pl.ds(0, 2)])
    e_in, e_out = fetch_self(0, flags, own_in, own_out, half, rest, e_in, e_out, sems.at[pl.ds(2, 2)])
    d_in, d_out = fetch_self(1, flags, own_in, own_out, half, rest, d_in, d_out, sems.at[pl.ds(4, 2)])

    @pl.when(flags[0, 0] == 0)
    def _():
        e_small[0:13, :], d_small[0:13, :] = small[...], small_other[...]

    @pl.when(flags[0, 0] != 0)
    def _():
        e_small[0:13, :], d_small[0:13, :] = small_other[...], small[...]

    encoder_self_kernel(table, bias, source, e_in, e_out, e_small, e_joined, e_mixed, e_stats, e_z, wide)
    leave(e_z)
    decoder_self_kernel(
        table, bias, source, target, glance, places, d_in, d_out, d_small, x, d_joined, d_mixed, d_stats, d_z, copied
    )


def first(table, flags, bias, glance, places, rows, got, weights, small, small_other):
    layer = (shaped(T, 3 * D, BF), shaped(T, D, BF), STATS, shaped(T, D, F32))
    outs = (shaped(16, D, F32), shaped(16, D, F32), *layer, shaped(T, D, BF), *layer)
    return kernel_call(
        first_kernel,
        outs,
        (table, flags, Raw(rows), *map(Raw, got), *map(Raw, weights), bias, glance, places, small, small_other),
        scalars=2,
        scratch=[
            pltpu.VMEM((T, D), BF), pltpu.VMEM((T, D), BF),
            pltpu.VMEM((D, 3 * D), BF), pltpu.VMEM((D, D), BF), pltpu.VMEM((D, 3 * D), BF), pltpu.VMEM((D, D), BF),
            pltpu.VMEM((T, D), F32), pltpu.VMEM((T, D), BF), pltpu.SemaphoreType.DMA((6,)),
        ],
        flops=24 * FLOP_UNIT,
        weight=0,
    )


def middle_kernel(
    table, flags, e_z1, own_cross, own_expand, own_contract, rest, half, last, bias, d_z1, cotangent, e_small, d_small,
    hidden, e_z2, mine, theirs, kept, sent, ff_bias, ff_rows, cross_bias, dstates, dz1,
    e_cross, e_expand, e_contract, d_cross, d_expand, d_contract,
    active, states, queries, mixed, stats, d_z2, wide, inner, value_b, dzb, dz2, sems,
):
    own = (own_cross, own_expand, own_contract, rest, half, last)
    e_cross, e_expand, e_contract = fetch_rest(0, flags, *own, e_cross, e_expand, e_contract, sems.at[pl.ds(0, 3)])
    d_cross, d_expand, d_contract = fetch_rest(1, flags, *own, d_cross, d_expand, d_contract, sems.at[pl.ds(3, 3)])
    encoder_ff_kernel(flags, e_z1, e_expand, e_contract, e_cross, e_small, hidden, e_z2, mine, theirs, states, active)
    decoder_cross_kernel(table, bias, d_z1, states, d_cross, d_small, queries, mixed, stats, d_z2, wide)
    decoder_ff_kernel(
        flags, d_z2, d_expand, d_contract, d_small, cotangent, mine, theirs, kept, sent, ff_bias, ff_rows, dz2,
        active, inner, value_b, wide, dzb,
    )
    decoder_cross_back_kernel(
        table, flags, bias, dz2, d_z1, queries, states, mixed, stats, d_cross, d_small, kept, sent, cross_bias, dstates, dz1,
        value_b, dzb, active.at[:, rows_at(0)], active.at[:, rows_at(D)],
    )


def middle(table, flags, bias, e_z1, d_z1, weights, cotangent, e_small, d_small):
    low, high = shaped(T, D, BF), shaped(T, D, F32)
    outs = (
        shaped(T, FF, BF), high, low, low, shaped(FF + D, D, BF), shaped(FF + D, D, BF),
        shaped(8, D, F32), shaped(8, D, F32), shaped(8, D, F32), shaped(T, 2 * D, BF), high,
    )
    weight_room = [pltpu.VMEM((D, 2 * D), BF), pltpu.VMEM((D, FF), BF), pltpu.VMEM((FF, D), BF)]
    return kernel_call(
        middle_kernel,
        outs,
        (table, flags, e_z1, *map(Raw, weights), bias, d_z1, cotangent, e_small, d_small),
        scalars=2,
        scratch=weight_room * 2
        + [
            pltpu.VMEM((T, FF), BF), pltpu.VMEM((T, 2 * D), BF), pltpu.VMEM((T, D), BF), pltpu.VMEM((T, D), BF),
            pltpu.VMEM(STATS.shape, F32), pltpu.VMEM((T, D), F32), pltpu.VMEM((T, D), F32), pltpu.VMEM((T, FF), BF),
            pltpu.VMEM((T, D), BF), pltpu.VMEM((T, D), BF), pltpu.VMEM((T, D), F32), pltpu.SemaphoreType.DMA((6,)),
        ],
        flops=54 * FLOP_UNIT,
        room_for=62,
    )


def swapped(value, axis, partner):
    count = lax.axis_size(axis)
    return lax.ppermute(value, axis, [(i, partner(i)) for i in range(count)])


def swapped_pipe(value):
    return swapped(value, "pipe", lambda i: 1 - i)


def added(first, second):
    return (first.astype(F32) + second.astype(F32)).astype(BF)


def gate(values, after):
    anywhere = pl.BlockSpec(memory_space=pl.ANY)
    return pl.pallas_call(
        lambda *refs: None,
        out_shape=tuple(jax.ShapeDtypeStruct(value.shape, value.dtype) for value in values),
        in_specs=[anywhere] * (len(values) + len(after)),
        out_specs=(anywhere,) * len(values),
        input_output_aliases={i: i for i in range(len(values))},
        cost_estimate=pl.CostEstimate(flops=0, bytes_accessed=0, transcendentals=0),
    )(*values, *after)


def halve_kernel(step, pairs, flags, *refs):
    ins, (kept_out, sent_out) = refs[: 2 * pairs], refs[2 * pairs :]
    bit = flags[0, 1 + step]
    slot = 0
    for i in range(pairs):
        kept, got = ins[2 * i], ins[2 * i + 1]
        half = kept.shape[1] // 2
        for j in range(kept.shape[0]):
            for out, side in ((kept_out, bit), (sent_out, 1 - bit)):
                at = pl.ds(pl.multiple_of(side * half, 16), half)
                out[slot] = added(kept[j, at, :], got[j, at, :])
            slot += 1


def double_kernel(step, flags, own, got, out):
    half = own.shape[0]
    bit = flags[0, 1 + step]
    out[pl.ds(pl.multiple_of(bit * half, 16), half), :] = own[...]
    out[pl.ds(pl.multiple_of((1 - bit) * half, 16), half), :] = got[...]


def across_kernel(pairs, flags, *refs):
    ins, (keep, send) = refs[: 2 * pairs], refs[2 * pairs :]
    sums = [added(ins[2 * i][j], ins[2 * i + 1][j]) for i in range(pairs) for j in range(ins[2 * i].shape[0])]

    @pl.when(flags[0, 0] == 0)
    def _():
        keep[...], send[...] = sums[0], sums[1]

    @pl.when(flags[0, 0] != 0)
    def _():
        keep[...], send[...] = sums[1], sums[0]


def add_kernel(first, second, out):
    out[...] = added(first[...], second[...])


class Steps:
    def __init__(self):
        count = lax.axis_size("dp")
        bits = list(range(1, (count - 1).bit_length()))
        cut = (len(bits) + 1) // 3
        orders = (bits, bits[cut : 2 * cut] + bits[:cut] + bits[2 * cut :])
        index = lax.axis_index("dp")
        core = index & 1
        self.partners = [lambda i: i ^ 1]
        self.bits = [core]
        for pair in zip(*orders):
            self.partners.append(lambda i, pair=pair: i ^ (1 << pair[i & 1]))
            self.bits.append((index >> jnp.where(core == 0, *pair)) & 1)
        self.core, self.count, self.last = core, count, len(bits)
        self.place = 0
        for bit in self.bits:
            self.place = self.place * 2 + bit
        self.flags = jnp.stack([lax.axis_index("pipe")] + self.bits).astype(jnp.int32).reshape(1, -1)

    def swap(self, value, step):
        return swapped(value, "dp", self.partners[step])

    def halve(self, step, *pairs, after=()):
        many = sum(kept.shape[0] for kept, _ in pairs)
        shape = jax.ShapeDtypeStruct((many, pairs[0][0].shape[1] // 2, D), BF)
        operands = [x for pair in pairs for x in pair]
        return kernel_call(
            functools.partial(halve_kernel, step + 1, len(pairs)), (shape, shape), (self.flags, *operands), scalars=1, after=after, direct=True
        )

    def double(self, step, own, got, after=(), weight=20):
        out = (shaped(2 * own.shape[0], D, BF),)
        return kernel_call(functools.partial(double_kernel, step), out, (self.flags, own, got), scalars=1, after=after, direct=True, weight=weight)[0]

    def half_gathered(self, value, afters):
        parts = []
        for step in range(self.last, 0, -1):
            after = afters[step - 1] if step <= len(afters) else ()
            value = self.double(step, value, self.swap(value, step), after=after, weight=0)
            parts.append(value)
        return parts

    def doubled(self, pairs, after, spill, outs):
        shape = shaped(*pairs[0][0].shape[1:], BF)
        operands = [x for pair in pairs for x in pair]
        kept, sent = kernel_call(
            functools.partial(across_kernel, len(pairs)), (shape, shape), (self.flags, *operands), scalars=1, after=after, direct=True
        )
        got = swapped_pipe(sent)
        after = yield kept
        (value,) = kernel_call(add_kernel, (shape,), (kept, got), after=after, direct=True)
        for step in range(self.last, 0, -1):
            got = self.swap(value, step)
            after = yield value
            value = self.double(step, value, got, after=after)
        got = self.swap(value, 0)
        after = yield value
        yield tuple(kernel_call(spill, outs, (self.flags, value, got), scalars=1, after=after, direct=True))


def by_core(flags, first, second, body):
    pl.when(flags[0, 1] == 0)(lambda: body(first, second))
    pl.when(flags[0, 1] != 0)(lambda: body(second, first))


def spill_ff_kernel(flags, own, other, expand, contract, cross):
    def fill(low, high):
        for j in range(FF // D):
            expand[:, rows_at(j * D)] = low[rows_at(j * D), :].astype(F32)
            contract[rows_at(j * D), :] = high[rows_at(j * D), :].astype(F32)
        cross[:, rows_at(0)] = low[rows_at(FF), :].astype(F32)
        cross[:, rows_at(D)] = high[rows_at(FF), :].astype(F32)

    by_core(flags, own, other, fill)


def spill_rest_kernel(flags, own, other, joined, out, expand_bias, branch, gain, shift):
    def fill(low, high):
        spots = ((low, 0, joined, 0), (low, 1, joined, 1), (high, 0, joined, 2), (high, 1, out, 0))
        for ref, block, to, column in spots:
            to[:, rows_at(column * D)] = ref[rows_at(block * D), :].astype(F32)
        value = low[rows_at(2 * D, 16), :].astype(F32)
        for j in range(FF // D):
            expand_bias[0:1, rows_at(j * D)] = value[j : j + 1, :]
        branch[...] = value[4:7, :]
        gain[...] = value[7:10, :]
        shift[...] = value[10:13, :]

    by_core(flags, own, other, fill)


def last_kernel(flags, expand, contract, out):
    @pl.when(flags[0, 1] == 0)
    def _():
        for j in range(2):
            out[rows_at(j * D), :] = expand[:, rows_at((2 + j) * D)]
        out[rows_at(2 * D), :] = contract[rows_at(0), :]

    @pl.when(flags[0, 1] != 0)
    def _():
        out[...] = contract[rows_at(D, 3 * D), :]


def per_device(
    embeddings, cotangent, lengths, copy_index, priority, hamming,
    self_in, self_out, cross_weight, expand, contract,
    expand_bias, branch_bias, norm_gain, norm_shift,
):
    pipe = lax.axis_index("pipe")
    leading = pipe == 0
    steps = Steps()
    flags, count = steps.flags, steps.count
    self_in, self_out, cross_weight, expand, contract = (w[0] for w in (self_in, self_out, cross_weight, expand, contract))

    rows = embeddings[0]
    small = jnp.concatenate([expand_bias.reshape(4, D), branch_bias[0], norm_gain[0], norm_shift[0]], 0)
    size = 4 * D // count

    def piece(place, blocks_of):
        block, inside = place * size // D, place * size % D
        value = lax.dynamic_slice(blocks_of[0][0], (inside, blocks_of[0][1] * D), (size, D))
        for i in range(1, 4):
            matrix, column = blocks_of[i]
            value = jnp.where(block == i, lax.dynamic_slice(matrix, (inside, column * D), (size, D)), value)
        return value

    self_piece = piece(steps.place, [(self_in, 0), (self_in, 1), (self_in, 2), (self_out, 0)])
    rest_piece = piece(lax.axis_index("dp"), [(cross_weight, 0), (cross_weight, 1), (expand, 0), (expand, 1)])
    table, bias, glance, places = row_layout(
        flags, lengths, hamming, priority.reshape(2 * T // WIN, WIN), copy_index.reshape(2 * T // WIN, WIN)
    )
    self_piece = swapped_pipe(self_piece)
    small_other = swapped_pipe(small)
    theirs = [lax.dynamic_slice_in_dim(rows, (1 - pipe) * T + at, size, 0) for at, size in PARTS]
    got = [swapped_pipe(part) for part in gate(theirs, (self_piece, small_other))]
    self_parts = steps.half_gathered(self_piece, ((bias,), (got[1],), (got[0],)))
    self_half = self_parts[-1]
    self_rest = steps.swap(self_half, 0)
    (last_piece,) = kernel_call(last_kernel, (shaped(3 * D, D, BF),), (flags, expand, contract), scalars=1, after=(self_parts[-2],), direct=True, weight=0)
    last_half = swapped_pipe(last_piece)
    (rest_piece,) = gate((swapped_pipe(rest_piece),), (self_parts[-2],))
    rest = lax.all_gather(rest_piece, "dp").reshape(4 * D, D)

    self_weights = (self_in, self_out, self_half, self_rest)
    (
        e_small, d_small, e_joined, e_mixed, e_stats, e_z1, x, d_joined, d_mixed, d_stats, d_z1,
    ) = first(table, flags, bias, glance, places, rows, got, self_weights, small, small_other)
    (last_half,) = gate((last_half,), (d_z1,))
    last_rest = steps.swap(last_half, 0)
    rest_weights = (cross_weight, expand, contract, rest, last_half, last_rest)
    (
        hidden, e_z2, layer_mine, layer_theirs, *dec_ff, d_ff_bias, d_ff_rows, d_cross_bias, dstates, dz1,
    ) = middle(table, flags, bias, e_z1, d_z1, rest_weights, cotangent, e_small, d_small)

    def rows_out(own, other):
        own, other = own.astype(F32), other.astype(F32)
        return jnp.where(leading, jnp.concatenate([own, other], 0), jnp.concatenate([other, own], 0))[None]

    def opened(pair):
        return [part[None] for part in pair]

    layer_other = swapped_pipe(layer_theirs)
    dec_kept, dec_sent = opened(dec_ff)
    dec_got = steps.swap(dec_sent, 0)
    *dec_self, target_grad, copies_grad = decoder_self_back(
        table, flags, bias, dz1, x, d_joined, d_mixed, d_stats, glance, places, self_weights,
        d_ff_bias, d_ff_rows, d_cross_bias, count,
    )
    dself_kept, dself_sent = opened(dec_self)
    dself_got = steps.swap(dself_sent, 0)
    (dec_got,) = gate((dec_got,), (target_grad,))
    dec_kept, dec_sent = steps.halve(0, (dec_kept, dec_got))
    dec_got = steps.swap(dec_sent, 1)
    *enc_ff, e_ff_bias, e_ff_rows, inner, dz = encoder_ff_back(
        flags, dstates, e_z1, e_z2, hidden, rest_weights, e_small, after=(dec_kept,)
    )
    enc_kept, enc_sent = opened(enc_ff)
    enc_got = steps.swap(enc_sent, 0)
    dec_got, dself_got = gate((dec_got, dself_got), (dz,))
    dec_kept, dec_sent = steps.halve(1, (dec_kept, dec_got))
    dec_got = steps.swap(dec_sent, 2)
    dself_kept, dself_sent = steps.halve(0, (dself_kept, dself_got))
    dself_got = steps.swap(dself_sent, 1)
    last_bias, e_dz1 = encoder_ff_last(flags, inner, dz, e_z1, rest_weights, e_small, after=(dec_kept, dself_kept))
    enc_got, dec_got = gate((enc_got, dec_got), (e_dz1,))
    dec_kept, dec_sent = steps.halve(2, (dec_kept, dec_got))
    dec_got = steps.swap(dec_sent, 3)
    enc_kept, enc_sent = steps.halve(0, (enc_kept, enc_got))
    enc_got = steps.swap(enc_sent, 1)
    *enc_self, grad_mine, grad_theirs = encoder_self_back(
        table, flags, bias, e_dz1, rows, got, e_joined, e_mixed, e_stats, copies_grad, self_weights, e_small,
        e_ff_bias, e_ff_rows, last_bias, target_grad, count, after=(enc_kept, dec_kept),
    )

    grad_other = swapped_pipe(grad_theirs)
    self_kept, self_sent = opened(enc_self)
    self_got = steps.swap(self_sent, 0)
    enc_got, dec_got, dself_got = gate((enc_got, dec_got, dself_got), (grad_mine,))

    def ff_sum():
        enc_pair, dec_pair = (enc_kept, enc_got), (dec_kept, dec_got)
        after = yield
        for step in range(1, steps.last):
            kept, sent = steps.halve(step, enc_pair, after=after)
            enc_pair = (kept, steps.swap(sent, step + 1))
            if step + 2 < steps.last:
                kept, sent = steps.halve(step + 2, dec_pair, after=(kept,))
                dec_pair = (kept, steps.swap(sent, step + 3))
            after = yield kept
        outs = (shaped(D, FF, F32), shaped(FF, D, F32), shaped(D, 2 * D, F32))
        yield from steps.doubled((enc_pair, dec_pair), after, spill_ff_kernel, outs)

    def self_sum():
        pairs = [(self_kept, self_got)]
        after = yield
        for step in range(steps.last):
            kept, sent = steps.halve(step, *pairs, after=after)
            pairs = [(kept, steps.swap(sent, step + 1))]
            if step == 0:
                pairs.append((dself_kept, dself_got))
            after = yield kept
        outs = (shaped(D, 3 * D, F32), shaped(D, D, F32), shaped(1, FF, F32)) + (shaped(3, D, F32),) * 3
        yield from steps.doubled(pairs, after, spill_rest_kernel, outs)

    chains = [ff_sum(), self_sum()]
    results = [None, None]
    mark = dself_got
    for chain in chains:
        next(chain)
    live = [0, 1]
    turn = 0
    while live:
        if turn == 5:
            layer = gate((layer_mine, layer_other), (mark,))
            layer_out, embedding_grad = rows_out(*layer), rows_out(*gate((grad_mine, grad_other), (mark,)))
        for i in list(live):
            extra = (layer_out, embedding_grad) if turn == 7 else ()
            value = chains[i].send((mark, *extra))
            if isinstance(value, tuple):
                results[i] = value
                live.remove(i)
                value = value[0]
            mark = value
        turn += 1
    expand_grad, contract_grad, cross_grad = results[0]
    in_grad, out_grad, *small_grads = results[1]
    return (
        layer_out,
        embedding_grad,
        in_grad[None],
        out_grad[None],
        cross_grad[None],
        expand_grad[None],
        contract_grad[None],
        small_grads[0],
        *(part[None] for part in small_grads[1:]),
    )


def solution(mesh):
    return jax.shard_map(
        per_device,
        mesh=mesh,
        in_specs=(
            P("pipe", "dp", None),
            P("dp", None),
            P("dp", None),
            P("dp"),
            P("dp"),
            P("dp", None),
            P("pipe", None, None),
            P("pipe", None, None),
            P("pipe", None, None),
            P("pipe", None, None),
            P("pipe", None, None),
            P("pipe", None),
            P("pipe", None, None),
            P("pipe", None, None),
            P("pipe", None, None),
        ),
        out_specs=(
            P("pipe", "dp", None),
            P("pipe", "dp", None),
            P("pipe", None, None),
            P("pipe", None, None),
            P("pipe", None, None),
            P("pipe", None, None),
            P("pipe", None, None),
            P("pipe", None),
            P("pipe", None, None),
            P("pipe", None, None),
            P("pipe", None, None),
        ),
        check_vma=False,
    )
```

```python
import functools
import math

import jax
import jax.numpy as jnp
from jax import lax
from jax.experimental import pallas as pl
from jax.experimental.pallas import tpu as pltpu
from jax.sharding import PartitionSpec as P

HEADS = 8
D = 512
FF = 2048
T = 1024
SENTS = 17
WIN = 128
EPSILON = 1e-05
NEG = -1e30
BF = jnp.bfloat16
F32 = jnp.float32
VMEM = pl.BlockSpec(memory_space=pltpu.VMEM)
SMEM = pl.BlockSpec(memory_space=pltpu.SMEM)
BLOCK = 512
STEPS = T // BLOCK


def nn(a, b):
    return jnp.dot(a, b, preferred_element_type=F32)


def nt(a, b):
    return lax.dot_general(a, b, (((1,), (1,)), ((), ())), preferred_element_type=F32)


def tn(a, b):
    return lax.dot_general(a, b, (((0,), (0,)), ((), ())), preferred_element_type=F32)


def normalized(value):
    center = jnp.mean(value, axis=-1, keepdims=True)
    centered = value - center
    spread = jnp.mean(centered * centered, axis=-1, keepdims=True)
    scale = lax.rsqrt(spread + EPSILON)
    return centered * scale, scale


def normalized_back(grad, unit, scale):
    first = jnp.mean(grad, axis=-1, keepdims=True)
    second = jnp.mean(grad * unit, axis=-1, keepdims=True)
    return scale * (grad - first - unit * second)


def folded(value):
    return jnp.sum(value.reshape(value.shape[0] // 8, 8, value.shape[1]), axis=0)


def column_sum(value):
    return jnp.sum(value, axis=0, keepdims=True)


def each_block(body):
    for index in range(STEPS):
        body(pl.ds(index * BLOCK, BLOCK))


def each_chunk(count, size, body):
    def step(index, carry):
        body(pl.multiple_of(index * size, size))
        return carry

    lax.fori_loop(0, count, step, 0)


class Held:
    def __init__(self, ref, copy):
        self.ref, self.copy = ref, copy

    def ready(self):
        if self.copy is not None:
            self.copy.wait()
            self.copy = None
        return self.ref

    def __getitem__(self, index):
        return self.ready()[index]

    @property
    def at(self):
        return self.ready().at

    @property
    def shape(self):
        return self.ref.shape


def ready(value):
    return value.ready() if isinstance(value, (Held, Landing)) else value


LEAVING = {}
WAITING = []


def arrive():
    for copy in WAITING:
        copy.start()
    WAITING.clear()


def leave(*refs):
    for ref in refs:
        copy, started = LEAVING.get(id(ref), (None, True))
        if not started:
            copy.start()
            LEAVING[id(ref)] = (copy, True)


class Landing:
    def __init__(self, ref, sem):
        self.ref, self.sem = ref, sem

    def ready(self):
        if self.sem is not None:
            pltpu.make_async_copy(self.ref, self.ref, self.sem).wait()
            self.sem = None
        return self.ref

    def __getitem__(self, index):
        return self.ready()[index]

    @property
    def at(self):
        return self.ready().at

    @property
    def shape(self):
        return self.ref.shape


class Raw:
    def __init__(self, value):
        self.value, self.shape, self.dtype = value, value.shape, value.dtype


def bytes_of(x):
    return math.prod(x.shape) * jnp.dtype(x.dtype).itemsize


LARGE = 256 << 10


def kernel_call(body, outs, operands, scalars=0, scratch=(), out_specs=None, flops=0, after=(), direct=False, weight=20, room_for=52, hold=False):
    size = sum(bytes_of(x) for x in (*operands, *outs))
    held = size + (sum(bytes_of(x) for x in scratch) if direct else 0)
    count, many, extra = len(operands), len(outs), len(scratch)
    raw = [isinstance(x, Raw) for x in operands]
    comes = [not (direct or r) and i >= scalars and bytes_of(x) >= LARGE for i, (x, r) in enumerate(zip(operands, raw))]
    goes = [not direct and bytes_of(x) >= LARGE for x in outs]
    anywhere = pl.BlockSpec(memory_space=pl.ANY)
    in_specs = [SMEM] * scalars + [anywhere if c or r else VMEM for c, r in zip(comes[scalars:], raw[scalars:])] + [anywhere] * len(after)
    specs = list(out_specs) if out_specs else [VMEM] * many
    specs = [anywhere if g else spec for g, spec in zip(goes, specs)]
    room = [pltpu.VMEM(x.shape, x.dtype) for x, c in zip((*operands, *outs), comes + goes) if c]
    sems = [pltpu.SemaphoreType.DMA((len(room),))] if room else []

    def run(*refs):
        ins, rest = list(refs[:count]), refs[count + len(after) :]
        results, rest = list(rest[:many]), rest[many:]
        own, rest = rest[:extra], rest[extra:]
        buffers, slot = rest[: len(room)], 0
        for i, c in enumerate(comes):
            if c:
                copy = pltpu.make_async_copy(ins[i], buffers[slot], rest[-1].at[slot])
                WAITING.append(copy)
                ins[i] = Held(buffers[slot], copy)
                slot += 1
        if not hold:
            arrive()
        LEAVING.clear()
        for i, g in enumerate(goes):
            if g:
                copy = pltpu.make_async_copy(buffers[slot], results[i], rest[-1].at[slot])
                results[i] = buffers[slot]
                LEAVING[id(results[i])] = (copy, False)
                slot += 1
        body(*ins, *results, *own)
        assert not WAITING
        for value in ins:
            ready(value)
        for i, g in enumerate(goes):
            if g:
                leave(results[i])
        for i, g in enumerate(goes):
            if g:
                LEAVING[id(results[i])][0].wait()
        LEAVING.clear()

    return pl.pallas_call(
        run,
        out_shape=tuple(outs),
        in_specs=in_specs,
        out_specs=tuple(specs),
        scratch_shapes=list(scratch) + room + sems,
        compiler_params=pltpu.CompilerParams(vmem_limit_bytes=held + (3 << 20) if direct else room_for << 20),
        cost_estimate=pl.CostEstimate(flops=weight * (flops or 2 * FLOP_UNIT), bytes_accessed=weight * size, transcendentals=0),
    )(*(x.value if isinstance(x, Raw) else x for x in operands), *after)


def shaped(rows, columns, kind):
    return jax.ShapeDtypeStruct((rows, columns), kind)


def layout_kernel(flags, lengths, hamming, priority, copies, table, bias, glance, places):
    row = flags[0, 0]
    ends = []
    total = jnp.int32(0)
    for j in range(SENTS):
        total = total + lengths[row, j]
        ends.append(total)
    count = jnp.int32(0)
    first = jnp.int32(0)

    def origin(start):
        return jnp.minimum((start // 16) * 16, T - WIN)

    for j in range(SENTS):
        begin = jnp.int32(0) if j == 0 else ends[j - 1]
        opens = (ends[j] - origin(first)) > WIN
        if j == 0:
            opens = jnp.bool_(False)
        first = jnp.where(opens, begin, first)
        count = jnp.where(opens, count + 1, count)
        table[0, 1 + count] = origin(first)
        table[0, 32 + count] = first
        table[0, 64 + count] = ends[j]
    table[0, 0] = count + 1

    lanes = lax.broadcasted_iota(jnp.int32, (8, WIN), 1)
    rows = lax.broadcasted_iota(jnp.int32, (8, WIN), 0)
    place = rows * WIN + lanes
    quota = jnp.zeros((8, WIN), jnp.int32) + (hamming[row, 0] + 1) // 2
    for j in range(SENTS - 1):
        change = (hamming[row, j + 1] + 1) // 2 - (hamming[row, j] + 1) // 2
        quota = quota + jnp.where(place >= ends[j], change, 0)
    part = pl.ds(pl.multiple_of(row * (T // WIN), 8), T // WIN)
    chosen = jnp.where(priority[part, :] < quota, 1.0, 0.0)
    copy = copies[part, :].astype(F32)
    for i in range(T // WIN):
        part = pl.ds(i * WIN, WIN)
        glance[part, :] = jnp.broadcast_to(chosen[i : i + 1, :], (WIN, WIN)).T
        places[part, :] = jnp.broadcast_to(copy[i : i + 1, :], (WIN, WIN)).T.astype(jnp.int32)

    def window(w, carry):
        at = table[0, 1 + w]
        here = lanes + at
        segment = jnp.zeros((8, WIN), F32)
        for j in range(SENTS):
            segment = segment + jnp.where(here >= ends[j], 1.0, 0.0)
        inside = (here >= table[0, 32 + w]) & (here < table[0, 64 + w])
        segment = jnp.where(inside, segment, -1.0)
        across = jnp.broadcast_to(segment[0:1, :], (WIN, WIN))
        down = across.T
        bias[w] = jnp.where((across == down) & (across >= 0.0), 0.0, NEG)
        return carry

    lax.fori_loop(0, count + 1, window, 0)
    for extra in range(1, WIDE_GROUP):
        table[0, 1 + count + extra] = 0
        bias[count + extra] = jnp.full((WIN, WIN), NEG, F32)


def row_layout(flags, lengths, hamming, priority, copies):
    outs = (
        shaped(1, 128, jnp.int32),
        jax.ShapeDtypeStruct((WINDOWS, WIN, WIN), F32),
        shaped(T, WIN, F32),
        shaped(T, WIN, jnp.int32),
    )
    return kernel_call(
        layout_kernel,
        outs,
        (flags, lengths, hamming, priority, copies),
        scalars=3,
        out_specs=(SMEM, VMEM, VMEM, VMEM),
        direct=True,
        weight=0,
    )


def pair_halves(part):
    low = lax.broadcasted_iota(jnp.int32, (WIN, WIN), 1) < 64
    zero = jnp.zeros_like(part)
    return jnp.concatenate([jnp.where(low, part, zero), jnp.where(low, zero, part)], axis=0)


def pair_join(both):
    low = lax.broadcasted_iota(jnp.int32, (WIN, WIN), 1) < 64
    return jnp.where(low, both[:WIN], both[WIN:])


PAIRS = [slice(i * 128, i * 128 + 128) for i in range(HEADS // 2)]


PAIRS = [slice(i * 128, i * 128 + 128) for i in range(HEADS // 2)]
GROUP = 2
WIDE_GROUP = 4
WINDOWS = SENTS + WIDE_GROUP - 1


def grouped(table, body, many=GROUP):
    def step(index, carry):
        body([index * many + i for i in range(many)])
        return carry

    lax.fori_loop(0, (table[0, 0] + many - 1) // many, step, 0)


def spread(table, windows):
    ats = [pl.ds(pl.multiple_of(table[0, 1 + w], 16), WIN) for w in windows]
    return [(w, pair, at, lanes) for w, at in zip(windows, ats) for pair, lanes in enumerate(PAIRS)]


def masks(bias, windows):
    out = []
    for w in windows:
        masked = bias[w]
        out += [jnp.concatenate([masked, masked], axis=1)] * len(PAIRS)
    return out


def attend(table, bias, queries, keys, values, mixed, stats):
    bias, queries, keys, values = map(ready, (bias, queries, keys, values))

    def body(windows):
        parts = spread(table, windows)
        masked = masks(bias, windows)
        query = [pair_halves(queries[at, lanes]) for _, _, at, lanes in parts]
        key = [keys[at, lanes] for _, _, at, lanes in parts]
        value = [values[at, lanes] for _, _, at, lanes in parts]
        scores = [nt(k, q) + mask for k, q, mask in zip(key, query, masked)]
        highest = [jnp.maximum(jnp.max(s, axis=0, keepdims=True), -1e29) for s in scores]
        raised = [jnp.exp(s - h) for s, h in zip(scores, highest)]
        inverse = [1.0 / jnp.maximum(jnp.sum(r, axis=0, keepdims=True), 1e-30) for r in raised]
        shares = [(r * i).astype(BF) for r, i in zip(raised, inverse)]
        out = [pair_join(tn(s, v)).astype(BF) for s, v in zip(shares, value)]
        for (w, pair, at, lanes), o, h, i in zip(parts, out, highest, inverse):
            mixed[at, lanes] = mixed[at, lanes] + o
            stats[w * 4 + pair, 0:1, :] = h
            stats[w * 4 + pair, 1:2, :] = i

    mixed[...] = jnp.zeros_like(mixed)
    grouped(table, body, WIDE_GROUP)


def attend_back(table, bias, queries, keys, values, stats, grad, grad_q, grad_k, grad_v):
    bias, queries, keys, values, stats = map(ready, (bias, queries, keys, values, stats))

    def body(windows):
        parts = spread(table, windows)
        masked = masks(bias, windows)
        query = [pair_halves(queries[at, lanes]) for _, _, at, lanes in parts]
        key = [keys[at, lanes] for _, _, at, lanes in parts]
        value = [values[at, lanes] for _, _, at, lanes in parts]
        out = [pair_halves(grad[at, lanes]) for _, _, at, lanes in parts]
        top = [stats[w * 4 + pair, 0:1, :] for w, pair, _, _ in parts]
        inverse = [stats[w * 4 + pair, 1:2, :] for w, pair, _, _ in parts]
        scores = [nt(k, q) + mask for k, q, mask in zip(key, query, masked)]
        back = [nt(v, o) for v, o in zip(value, out)]
        shares = [jnp.exp(s - h) * i for s, h, i in zip(scores, top, inverse)]
        got_v = [nn(s.astype(BF), o).astype(BF) for s, o in zip(shares, out)]
        total = [jnp.sum(s * b, axis=0, keepdims=True) for s, b in zip(shares, back)]
        scored = [(s * (b - t)).astype(BF) for s, b, t in zip(shares, back, total)]
        got_k = [nn(s, q).astype(BF) for s, q in zip(scored, query)]
        got_q = [(pair_join(tn(s, k)) * 0.125).astype(BF) for s, k in zip(scored, key)]
        for ref, got in zip((grad_q, grad_k, grad_v), (got_q, got_k, got_v)):
            for (_, _, at, lanes), value_got in zip(parts, got):
                ref[at, lanes] = ref[at, lanes] + value_got

    for ref in (grad_q, grad_k, grad_v):
        ref[...] = jnp.zeros_like(ref)
    grouped(table, body)


STATS = jax.ShapeDtypeStruct((WINDOWS * 4, 2, 2 * WIN), F32)


def thirds(ref):
    return tuple(ref.at[:, i * D : (i + 1) * D] for i in range(ref.shape[1] // D))


def put(flags, half, kept, sent, rows, value):
    @pl.when(flags[0, 1] == half)
    def _():
        kept[rows, :] = value

    @pl.when(flags[0, 1] != half)
    def _():
        sent[rows, :] = value


def put_side(flags, side, mine, theirs, rows, value):
    @pl.when(flags[0, 0] == side)
    def _():
        mine[rows, :] = value

    @pl.when(flags[0, 0] != side)
    def _():
        theirs[rows, :] = value


def rows_at(start, count=D):
    return slice(start, start + count)


def scaled(unit, small, slot):
    return unit * small[7 + slot : 8 + slot, :] + small[10 + slot : 11 + slot, :]


def project(x, weight_in, joined, at):
    got = nn(x, weight_in[...])
    joined[at, :D] = (got[:, :D] * 0.125).astype(BF)
    joined[at, D:] = got[:, D:].astype(BF)


def encoder_self_kernel(table, bias, source, weight_in, weight_out, small, joined, mixed, stats, z, x):
    def before(at):
        unit, _ = normalized(source[at, :].astype(F32))
        value = scaled(unit, small, 2)
        x[at, :] = value
        project(value.astype(BF), weight_in, joined, at)

    each_block(before)
    leave(joined)
    attend(table, bias, *thirds(joined), mixed, stats)
    leave(mixed, stats)

    def after(at):
        z[at, :] = x[at, :] + nn(mixed[at, :], weight_out[...]) + small[4:5, :]

    each_block(after)


def copy_hits(bias, places, w, start):
    at = pl.ds(start, WIN)
    lanes = lax.broadcasted_iota(jnp.int32, (WIN, WIN), 1) + start
    inside = jnp.max(bias[w], axis=1, keepdims=True) == 0.0
    return at, jnp.where((places[at, :] == lanes) & inside, 1.0, 0.0).astype(BF)


def kept_rows(glance, at):
    return jnp.concatenate([glance[at, :]] * (D // WIN), axis=1) > 0.5


def decoder_self_kernel(
    table, bias, source, target, glance, places, weight_in, weight_out, small, x, joined, mixed, stats, z, copied
):
    copied[...] = jnp.zeros_like(copied)
    bias, places, source = map(ready, (bias, places, source))

    def gather(windows):
        parts = [copy_hits(bias, places, w, pl.multiple_of(table[0, 1 + w], 16)) for w in windows]
        got = [nn(hit, source[at, :]).astype(BF) for at, hit in parts]
        for (at, _), value in zip(parts, got):
            copied[at, :] = copied[at, :] + value

    grouped(table, gather)

    def before(at):
        value = jnp.where(kept_rows(glance, at), target[at, :].astype(F32), copied[at, :].astype(F32)).astype(BF)
        x[at, :] = value
        project(value, weight_in, joined, at)

    each_block(before)
    leave(joined)
    attend(table, bias, *thirds(joined), mixed, stats)
    leave(mixed, stats)

    def after(at):
        z[at, :] = x[at, :].astype(F32) + nn(mixed[at, :], weight_out[...]) + small[4:5, :]

    each_block(after)


FLOP_UNIT = 2 * T * D * D


ROOT = 0.7978845608028654
CUBE = 0.044715


def gelu_parts(u):
    square = u * u
    bent = jnp.tanh(u * (ROOT + ROOT * CUBE * square))
    half = 0.5 + 0.5 * bent
    slope = half + (u - u * (bent * bent)) * (0.5 * ROOT + 1.5 * ROOT * CUBE * square)
    return u * half, slope


def expand_block(value, expand, small, active, slope, at):
    for j in range(FF // D):
        cols = rows_at(j * D)
        hidden = (nn(value, expand[:, cols]) + small[j : j + 1, :]).astype(BF)
        active[at, cols], slope[at, cols] = gelu_parts(hidden)


def encoder_ff_kernel(flags, z1, expand, contract, cross, small, inner, z2, mine, theirs, states, active):
    def block(at):
        unit, _ = normalized(z1[at, :])
        value = scaled(unit, small, 0)
        for j in range(FF // D):
            cols = rows_at(j * D)
            hidden = (nn(value.astype(BF), expand[:, cols]) + small[j : j + 1, :]).astype(BF)
            inner[at, cols] = hidden
            active[at, cols], _ = gelu_parts(hidden)
        total = value + nn(active[at, :], contract[...]) + small[5:6, :]
        z2[at, :] = total
        unit, _ = normalized(total)
        out = scaled(unit, small, 1)
        put_side(flags, 0, mine, theirs, at, out.astype(BF))
        got = nn(out.astype(BF), cross[...])
        states[at, :D] = got[:, :D].astype(BF)
        states[at, D:] = (got[:, D:] + small[6:7, :]).astype(BF)

    each_block(block)
    leave(inner, z2)


def ff_back(flags, dzb, value_b, active, inner, contract, kept, sent, bias_rows):
    def block(at):
        for j in range(FF // D):
            cols = rows_at(j * D)
            back = nt(dzb[at, :], contract[cols, :])
            inner[at, cols] = (back * inner[at, cols].astype(F32)).astype(BF)

    each_block(block)
    for c in range(FF // D):
        cols = rows_at(c * D)
        put(flags, 1, kept, sent, cols, tn(active[:, cols], dzb[...]).astype(BF))
        put(flags, 0, kept, sent, cols, tn(value_b[...], inner[:, cols]).astype(BF))
        bias_rows[c : c + 1, :] = column_sum(inner[:, cols].astype(F32))


def decoder_ff_kernel(
    flags, z2, expand, contract, small, cotangent,
    mine, theirs, kept, sent, bias_grads, bias_rows, dz2,
    active, inner, value_b, dz, dzb,
):
    bias_grads[...] = jnp.zeros_like(bias_grads)
    offset = flags[0, 0] * T

    def block(at):
        unit, _ = normalized(z2[at, :])
        value = scaled(unit, small, 1)
        value_b[at, :] = value.astype(BF)
        expand_block(value.astype(BF), expand, small, active, inner, at)
        total = value + nn(active[at, :], contract[...]) + small[5:6, :]
        unit, scale = normalized(total)
        put_side(flags, 1, mine, theirs, at, scaled(unit, small, 2).astype(BF))
        wanted = cotangent[pl.ds(pl.multiple_of(offset + at.start, BLOCK), BLOCK), :].astype(F32)
        bias_grads[0:1, :] += column_sum(wanted * unit)
        bias_grads[1:2, :] += column_sum(wanted)
        back = normalized_back(wanted * small[9:10, :], unit, scale)
        bias_grads[2:3, :] += column_sum(back)
        dz[at, :] = back
        dzb[at, :] = back.astype(BF)

    each_block(block)
    leave(mine, theirs)
    ff_back(flags, dzb, value_b, active, inner, contract, kept, sent, bias_rows)

    def last(at):
        back = dz[at, :] + nt(inner[at, :], expand[...])
        unit, scale = normalized(z2[at, :])
        bias_grads[3:4, :] += column_sum(back * unit)
        bias_grads[4:5, :] += column_sum(back)
        dz2[at, :] = normalized_back(back * small[8:9, :], unit, scale)

    each_block(last)


def encoder_ff_back_kernel(
    flags, z2, dstates, z1, hidden, own_cross, own_expand, own_contract, rest, half, last_half, small,
    kept, sent, bias_grads, bias_rows, inner, dz,
    cross, contract, active, value_b, memory_b, dzb, sems,
):
    own = (own_cross, own_expand, own_contract, rest, half, last_half)
    cross, _, contract = fetch_rest(0, flags, *own, cross, None, contract, sems)
    arrive()
    bias_grads[...] = jnp.zeros_like(bias_grads)

    def block(at):
        unit, scale = normalized(z2[at, :])
        memory_b[at, :] = scaled(unit, small, 1).astype(BF)
        back = nt(dstates[at, :], cross[...])
        bias_grads[0:1, :] += column_sum(dstates[at, D:].astype(F32))
        bias_grads[1:2, :] += column_sum(back * unit)
        bias_grads[2:3, :] += column_sum(back)
        back = normalized_back(back * small[8:9, :], unit, scale)
        bias_grads[3:4, :] += column_sum(back)
        dz[at, :] = back
        dzb[at, :] = back.astype(BF)
        unit, _ = normalized(z1[at, :])
        value_b[at, :] = scaled(unit, small, 0).astype(BF)
        for j in range(FF // D):
            cols = rows_at(j * D)
            active[at, cols], inner[at, cols] = gelu_parts(hidden[at, cols])

    each_block(block)
    leave(dz)
    ff_back(flags, dzb, value_b, active, inner, contract, kept, sent, bias_rows)
    leave(inner)
    for c in range(2):
        put(flags, c, kept, sent, rows_at(FF), tn(memory_b[...], dstates[:, rows_at(c * D)]).astype(BF))


def encoder_ff_back(flags, dstates, z1, z2, hidden, weights, small, after=()):
    outs = (
        shaped(FF + D, D, BF), shaped(FF + D, D, BF),
        shaped(8, D, F32), shaped(8, D, F32), shaped(T, FF, BF), shaped(T, D, F32),
    )
    return kernel_call(
        encoder_ff_back_kernel,
        outs,
        (flags, z2, dstates, z1, hidden, *map(Raw, weights), small),
        scalars=1,
        scratch=[
            pltpu.VMEM((D, 2 * D), BF),
            pltpu.VMEM((FF, D), BF),
            pltpu.VMEM((T, FF), BF),
            pltpu.VMEM((T, D), BF),
            pltpu.VMEM((T, D), BF),
            pltpu.VMEM((T, D), BF),
            pltpu.SemaphoreType.DMA((3,)),
        ],
        flops=18 * FLOP_UNIT,
        after=after,
        hold=True,
    )


def encoder_ff_last_kernel(
    flags, inner, dz, z1, own_cross, own_expand, own_contract, rest, half, last_half, small,
    bias_grads, dz1,
    expand, sems,
):
    own = (own_cross, own_expand, own_contract, rest, half, last_half)
    _, expand, _ = fetch_rest(0, flags, *own, None, expand, None, sems)
    arrive()
    bias_grads[...] = jnp.zeros_like(bias_grads)

    def last(at):
        back = dz[at, :] + nt(inner[at, :], expand[...])
        unit, scale = normalized(z1[at, :])
        bias_grads[4:5, :] += column_sum(back * unit)
        bias_grads[5:6, :] += column_sum(back)
        dz1[at, :] = normalized_back(back * small[7:8, :], unit, scale)

    each_block(last)


def encoder_ff_last(flags, inner, dz, z1, weights, small, after=()):
    return kernel_call(
        encoder_ff_last_kernel,
        (shaped(8, D, F32), shaped(T, D, F32)),
        (flags, inner, dz, z1, *map(Raw, weights), small),
        scalars=1,
        scratch=[pltpu.VMEM((D, FF), BF), pltpu.SemaphoreType.DMA((3,))],
        flops=4 * FLOP_UNIT,
        after=after,
        hold=True,
    )


def decoder_cross_kernel(table, bias, z1, states, weight, small, queries, mixed, stats, z2, x):
    def before(at):
        unit, _ = normalized(z1[at, :])
        value = scaled(unit, small, 0)
        x[at, :] = value
        queries[at, :] = (nn(value.astype(BF), weight[:, :D]) * 0.125).astype(BF)

    each_block(before)
    attend(table, bias, queries, *thirds(states), mixed, stats)

    def after(at):
        z2[at, :] = x[at, :] + nn(mixed[at, :], weight[:, D:]) + small[6:7, :]

    each_block(after)


def decoder_cross_back_kernel(
    table, flags, bias, dz2, z1, queries, states, mixed, stats, weight, small,
    kept, sent, bias_grads, dstates, dz1,
    value_b, dzb, out, dq,
):
    bias_grads[...] = jnp.zeros_like(bias_grads)

    def before(at):
        bias_grads[0:1, :] += column_sum(dz2[at, :])
        low = dz2[at, :].astype(BF)
        dzb[at, :] = low
        out[at, :] = nt(low, weight[:, D:]).astype(BF)
        unit, _ = normalized(z1[at, :])
        value_b[at, :] = scaled(unit, small, 0).astype(BF)

    each_block(before)
    attend_back(table, bias, queries, *thirds(states), stats, out, dq, *thirds(dstates))
    leave(dstates)
    put(flags, 0, kept, sent, rows_at(FF), tn(value_b[...], dq[...]).astype(BF))
    put(flags, 1, kept, sent, rows_at(FF), tn(mixed[...], dzb[...]).astype(BF))
    leave(kept, sent)

    def after(at):
        back = dz2[at, :] + nt(dq[at, :], weight[:, :D])
        unit, scale = normalized(z1[at, :])
        bias_grads[1:2, :] += column_sum(back * unit)
        bias_grads[2:3, :] += column_sum(back)
        dz1[at, :] = normalized_back(back * small[7:8, :], unit, scale)

    each_block(after)


def self_back(table, bias, flags, dz, x, joined, mixed, stats, weight_in, weight_out, kept, sent, acc, dzb, out, djoined):
    acc[...] = jnp.zeros_like(acc)

    def before(at):
        acc[0:1, :] += column_sum(dz[at, :])
        low = dz[at, :].astype(BF)
        dzb[at, :] = low
        out[at, :] = nt(low, weight_out[...]).astype(BF)

    each_block(before)
    attend_back(table, bias, *thirds(joined), stats, out, *thirds(djoined))
    for c in range(3):
        value = tn(x[...], djoined[:, rows_at(c * D)]).astype(BF)
        put(flags, c // 2, kept, sent, rows_at(c % 2 * D), value)
    put(flags, 1, kept, sent, rows_at(D), tn(mixed[...], dzb[...]).astype(BF))


def put_small(flags, kept, sent, rows):
    count = kept.shape[0] - 2 * D
    at = rows_at(2 * D, count)
    filled = jnp.concatenate(rows + [jnp.zeros((count - 13, D), F32)], axis=0).astype(BF)
    put(flags, 0, kept, sent, at, filled)
    put(flags, 1, kept, sent, at, jnp.zeros((count, D), BF))


def decoder_self_back_kernel(
    table, flags, dz, own_in, own_out, half, rest, joined, bias, stats, x, mixed, glance, places,
    ff_bias, ff_rows, cross_bias,
    kept, sent, target_grad, source_grad,
    weight_in, weight_out, acc, dzb, out, djoined, dcopied, sems,
):
    weight_in, weight_out = fetch_self(1, flags, own_in, own_out, half, rest, weight_in, weight_out, sems)
    arrive()
    self_back(table, bias, flags, dz, x, joined, mixed, stats, weight_in, weight_out, kept, sent, acc, dzb, out, djoined)
    put_small(
        flags, kept, sent,
        [
            ff_rows[0:4, :], acc[0:1, :], ff_bias[2:3, :], cross_bias[0:1, :],
            cross_bias[1:2, :], ff_bias[3:4, :], ff_bias[0:1, :],
            cross_bias[2:3, :], ff_bias[4:5, :], ff_bias[1:2, :],
        ],
    )

    def after(at):
        back = dz[at, :] + nt(djoined[at, :], weight_in[...])
        kept_at = kept_rows(glance, at)
        target_grad[at, :] = jnp.where(kept_at, back, 0.0).astype(BF)
        dcopied[at, :] = jnp.where(kept_at, 0.0, back).astype(BF)

    each_block(after)
    leave(target_grad, kept, sent)
    source_grad[...] = jnp.zeros_like(source_grad)
    bias, places = ready(bias), ready(places)

    def scatter(windows):
        parts = [copy_hits(bias, places, w, pl.multiple_of(table[0, 1 + w], 16)) for w in windows]
        got = [tn(hit, dcopied[at, :]).astype(BF) for at, hit in parts]
        for (at, _), value in zip(parts, got):
            source_grad[at, :] = source_grad[at, :] + value

    grouped(table, scatter)


def half_rows(count):
    return 2 * D + 8 * count


def decoder_self_back(table, flags, bias, dz, x, joined, mixed, stats, glance, places, weights, ff_bias, ff_rows, cross_bias, count, after=()):
    half = half_rows(count)
    outs = (shaped(half, D, BF), shaped(half, D, BF), shaped(T, D, BF), shaped(T, D, BF))
    return kernel_call(
        decoder_self_back_kernel,
        outs,
        (table, flags, dz, *map(Raw, weights), joined, bias, stats, x, mixed, glance, places, ff_bias, ff_rows, cross_bias),
        scalars=2,
        scratch=[
            pltpu.VMEM((D, 3 * D), BF), pltpu.VMEM((D, D), BF),
            pltpu.VMEM((8, D), F32), pltpu.VMEM((T, D), BF), pltpu.VMEM((T, D), BF),
            pltpu.VMEM((T, 3 * D), BF), pltpu.VMEM((T, D), BF), pltpu.SemaphoreType.DMA((2,)),
        ],
        flops=18 * FLOP_UNIT,
        after=after,
        hold=True,
    )


def encoder_self_back_kernel(
    table, flags, dz, rows, got_0, got_1, own_in, own_out, half, rest, joined, bias, stats, mixed, copies_grad, small,
    ff_bias, ff_rows, last_bias, target_grad,
    kept, sent, mine, theirs,
    source, weight_in, weight_out, acc, x, dzb, out, djoined, sems,
):
    @pl.when(flags[0, 0] == 0)
    def _():
        start((rows.at[rows_at(0, T), :], source, sems.at[2]))

    @pl.when(flags[0, 0] != 0)
    def _():
        start(*row_parts((got_0, got_1), source, sems.at[2]))

    source = Landing(source, sems.at[2])
    weight_in, weight_out = fetch_self(0, flags, own_in, own_out, half, rest, weight_in, weight_out, sems)
    arrive()

    def first(at):
        unit, _ = normalized(source[at, :].astype(F32))
        x[at, :] = scaled(unit, small, 2).astype(BF)

    each_block(first)
    self_back(table, bias, flags, dz, x, joined, mixed, stats, weight_in, weight_out, kept, sent, acc, dzb, out, djoined)

    def after(at):
        back = dz[at, :] + nt(djoined[at, :], weight_in[...])
        unit, scale = normalized(source[at, :].astype(F32))
        acc[1:2, :] += column_sum(back * unit)
        acc[2:3, :] += column_sum(back)
        value = normalized_back(back * small[9:10, :], unit, scale) + copies_grad[at, :].astype(F32)
        put_side(flags, 0, mine, theirs, at, value.astype(BF))
        put_side(flags, 1, mine, theirs, at, target_grad[at, :])

    each_block(after)
    put_small(
        flags, kept, sent,
        [
            ff_rows[0:4, :], acc[0:1, :], ff_bias[3:4, :], ff_bias[0:1, :],
            last_bias[4:5, :], ff_bias[1:2, :], acc[1:2, :],
            last_bias[5:6, :], ff_bias[2:3, :], acc[2:3, :],
        ],
    )


def encoder_self_back(table, flags, bias, dz, rows, got, joined, mixed, stats, copies_grad, weights, small, ff_bias, ff_rows, last_bias, target_grad, count, after=()):
    half = half_rows(count)
    outs = (shaped(half, D, BF), shaped(half, D, BF), shaped(T, D, BF), shaped(T, D, BF))
    return kernel_call(
        encoder_self_back_kernel,
        outs,
        (table, flags, dz, Raw(rows), *map(Raw, got), *map(Raw, weights), joined, bias, stats, mixed, copies_grad, small, ff_bias, ff_rows, last_bias, target_grad),
        scalars=2,
        scratch=[
            pltpu.VMEM((T, D), BF), pltpu.VMEM((D, 3 * D), BF), pltpu.VMEM((D, D), BF),
            pltpu.VMEM((8, D), F32), pltpu.VMEM((T, D), BF), pltpu.VMEM((T, D), BF), pltpu.VMEM((T, D), BF),
            pltpu.VMEM((T, 3 * D), BF), pltpu.SemaphoreType.DMA((3,)),
        ],
        flops=18 * FLOP_UNIT,
        after=after,
        hold=True,
    )


def start(*copies):
    for source, target, sem in copies:
        pltpu.make_async_copy(source, target, sem).start()


def fetch_self(layer, flags, own_in, own_out, half, rest, to_in, to_out, sems):
    own = flags[0, 0] == layer

    def other(low, high):
        start(
            (high.at[rows_at(D), :], to_out, sems.at[1]),
            (low.at[rows_at(0), :], to_in.at[:, rows_at(0)], sems.at[0]),
            (low.at[rows_at(D), :], to_in.at[:, rows_at(D)], sems.at[0]),
            (high.at[rows_at(0), :], to_in.at[:, rows_at(2 * D)], sems.at[0]),
        )

    pl.when(own)(lambda: start((own_out, to_out, sems.at[1]), (own_in, to_in, sems.at[0])))
    pl.when(jnp.logical_not(own) & (flags[0, 1] == 0))(lambda: other(half, rest))
    pl.when(jnp.logical_not(own) & (flags[0, 1] != 0))(lambda: other(rest, half))
    return Landing(to_in, sems.at[0]), Landing(to_out, sems.at[1])


def fetch_rest(layer, flags, own_cross, own_expand, own_contract, rest, half, last, cross, expand, contract, sems):
    own = flags[0, 0] == layer

    def other(low, high):
        copies = [(rest.at[rows_at((2 + j) * D), :], expand.at[:, rows_at(j * D)], 1) for j in range(2)] if expand is not None else []
        copies += [(low.at[rows_at(j * D), :], expand.at[:, rows_at((2 + j) * D)], 1) for j in range(2)] if expand is not None else []
        if contract is not None:
            copies.append((low.at[rows_at(2 * D), :], contract.at[rows_at(0), :], 2))
            copies.append((high, contract.at[rows_at(D, 3 * D), :], 2))
        if cross is not None:
            copies += [(rest.at[rows_at(j * D), :], cross.at[:, rows_at(j * D)], 0) for j in range(2)]
        start(*((source, target, sems.at[i]) for source, target, i in copies))

    pairs = ((own_cross, cross, 0), (own_expand, expand, 1), (own_contract, contract, 2))
    pl.when(own)(lambda: start(*((source, target, sems.at[i]) for source, target, i in pairs if target is not None)))
    pl.when(jnp.logical_not(own) & (flags[0, 1] == 0))(lambda: other(half, last))
    pl.when(jnp.logical_not(own) & (flags[0, 1] != 0))(lambda: other(last, half))
    return tuple(ref if ref is None else Landing(ref, sems.at[i]) for i, ref in enumerate((cross, expand, contract)))


PARTS = ((0, 384), (384, 640))


def row_parts(parts, to, sem):
    return [(part, to.at[rows_at(at, size), :], sem) for part, (at, size) in zip(parts, PARTS)]


def fetch_rows(flags, rows, got, source, target, sems):
    @pl.when(flags[0, 0] == 0)
    def _():
        start((rows.at[rows_at(0, T), :], source, sems.at[0]), *row_parts(got, target, sems.at[1]))

    @pl.when(flags[0, 0] != 0)
    def _():
        start(*row_parts(got, source, sems.at[0]), (rows.at[rows_at(T, T), :], target, sems.at[1]))

    return Landing(source, sems.at[0]), Landing(target, sems.at[1])


def first_kernel(
    table, flags, rows, got_0, got_1, own_in, own_out, half, rest, bias, glance, places, small, small_other,
    e_small, d_small, e_joined, e_mixed, e_stats, e_z, x, d_joined, d_mixed, d_stats, d_z,
    source, target, e_in, e_out, d_in, d_out, wide, copied, sems,
):
    source, target = fetch_rows(flags, rows, (got_0, got_1), source, target, sems.at[pl.ds(0, 2)])
    e_in, e_out = fetch_self(0, flags, own_in, own_out, half, rest, e_in, e_out, sems.at[pl.ds(2, 2)])
    arrive()
    d_in, d_out = fetch_self(1, flags, own_in, own_out, half, rest, d_in, d_out, sems.at[pl.ds(4, 2)])

    @pl.when(flags[0, 0] == 0)
    def _():
        e_small[0:13, :], d_small[0:13, :] = small[...], small_other[...]

    @pl.when(flags[0, 0] != 0)
    def _():
        e_small[0:13, :], d_small[0:13, :] = small_other[...], small[...]

    encoder_self_kernel(table, bias, source, e_in, e_out, e_small, e_joined, e_mixed, e_stats, e_z, wide)
    leave(e_z)
    decoder_self_kernel(
        table, bias, source, target, glance, places, d_in, d_out, d_small, x, d_joined, d_mixed, d_stats, d_z, copied
    )


def first(table, flags, bias, glance, places, rows, got, weights, small, small_other):
    layer = (shaped(T, 3 * D, BF), shaped(T, D, BF), STATS, shaped(T, D, F32))
    outs = (shaped(16, D, F32), shaped(16, D, F32), *layer, shaped(T, D, BF), *layer)
    return kernel_call(
        first_kernel,
        outs,
        (table, flags, Raw(rows), *map(Raw, got), *map(Raw, weights), bias, glance, places, small, small_other),
        scalars=2,
        scratch=[
            pltpu.VMEM((T, D), BF), pltpu.VMEM((T, D), BF),
            pltpu.VMEM((D, 3 * D), BF), pltpu.VMEM((D, D), BF), pltpu.VMEM((D, 3 * D), BF), pltpu.VMEM((D, D), BF),
            pltpu.VMEM((T, D), F32), pltpu.VMEM((T, D), BF), pltpu.SemaphoreType.DMA((6,)),
        ],
        flops=24 * FLOP_UNIT,
        weight=0,
        hold=True,
    )


def middle_kernel(
    table, flags, e_z1, own_cross, own_expand, own_contract, rest, half, last, bias, d_z1, cotangent, e_small, d_small,
    hidden, e_z2, mine, theirs, kept, sent, ff_bias, ff_rows, cross_bias, dstates, dz1,
    e_cross, e_expand, e_contract, d_cross, d_expand, d_contract,
    active, states, queries, mixed, stats, d_z2, wide, inner, value_b, dzb, dz2, sems,
):
    own = (own_cross, own_expand, own_contract, rest, half, last)
    e_cross, e_expand, e_contract = fetch_rest(0, flags, *own, e_cross, e_expand, e_contract, sems.at[pl.ds(0, 3)])
    arrive()
    d_cross, d_expand, d_contract = fetch_rest(1, flags, *own, d_cross, d_expand, d_contract, sems.at[pl.ds(3, 3)])
    encoder_ff_kernel(flags, e_z1, e_expand, e_contract, e_cross, e_small, hidden, e_z2, mine, theirs, states, active)
    decoder_cross_kernel(table, bias, d_z1, states, d_cross, d_small, queries, mixed, stats, d_z2, wide)
    decoder_ff_kernel(
        flags, d_z2, d_expand, d_contract, d_small, cotangent, mine, theirs, kept, sent, ff_bias, ff_rows, dz2,
        active, inner, value_b, wide, dzb,
    )
    decoder_cross_back_kernel(
        table, flags, bias, dz2, d_z1, queries, states, mixed, stats, d_cross, d_small, kept, sent, cross_bias, dstates, dz1,
        value_b, dzb, active.at[:, rows_at(0)], active.at[:, rows_at(D)],
    )


def middle(table, flags, bias, e_z1, d_z1, weights, cotangent, e_small, d_small):
    low, high = shaped(T, D, BF), shaped(T, D, F32)
    outs = (
        shaped(T, FF, BF), high, low, low, shaped(FF + D, D, BF), shaped(FF + D, D, BF),
        shaped(8, D, F32), shaped(8, D, F32), shaped(8, D, F32), shaped(T, 2 * D, BF), high,
    )
    weight_room = [pltpu.VMEM((D, 2 * D), BF), pltpu.VMEM((D, FF), BF), pltpu.VMEM((FF, D), BF)]
    return kernel_call(
        middle_kernel,
        outs,
        (table, flags, e_z1, *map(Raw, weights), bias, d_z1, cotangent, e_small, d_small),
        scalars=2,
        scratch=weight_room * 2
        + [
            pltpu.VMEM((T, FF), BF), pltpu.VMEM((T, 2 * D), BF), pltpu.VMEM((T, D), BF), pltpu.VMEM((T, D), BF),
            pltpu.VMEM(STATS.shape, F32), pltpu.VMEM((T, D), F32), pltpu.VMEM((T, D), F32), pltpu.VMEM((T, FF), BF),
            pltpu.VMEM((T, D), BF), pltpu.VMEM((T, D), BF), pltpu.VMEM((T, D), F32), pltpu.SemaphoreType.DMA((6,)),
        ],
        flops=54 * FLOP_UNIT,
        room_for=62,
        hold=True,
    )


def swapped(value, axis, partner):
    count = lax.axis_size(axis)
    return lax.ppermute(value, axis, [(i, partner(i)) for i in range(count)])


def swapped_pipe(value):
    return swapped(value, "pipe", lambda i: 1 - i)


def added(first, second):
    return (first.astype(F32) + second.astype(F32)).astype(BF)


def gate(values, after):
    anywhere = pl.BlockSpec(memory_space=pl.ANY)
    return pl.pallas_call(
        lambda *refs: None,
        out_shape=tuple(jax.ShapeDtypeStruct(value.shape, value.dtype) for value in values),
        in_specs=[anywhere] * (len(values) + len(after)),
        out_specs=(anywhere,) * len(values),
        input_output_aliases={i: i for i in range(len(values))},
        cost_estimate=pl.CostEstimate(flops=0, bytes_accessed=0, transcendentals=0),
    )(*values, *after)


def halve_kernel(step, pairs, flags, *refs):
    ins, (kept_out, sent_out) = refs[: 2 * pairs], refs[2 * pairs :]
    bit = flags[0, 1 + step]
    slot = 0
    for i in range(pairs):
        kept, got = ins[2 * i], ins[2 * i + 1]
        half = kept.shape[1] // 2
        for j in range(kept.shape[0]):
            for out, side in ((kept_out, bit), (sent_out, 1 - bit)):
                at = pl.ds(pl.multiple_of(side * half, 16), half)
                out[slot] = added(kept[j, at, :], got[j, at, :])
            slot += 1


def double_kernel(step, flags, own, got, out):
    half = own.shape[0]
    bit = flags[0, 1 + step]
    out[pl.ds(pl.multiple_of(bit * half, 16), half), :] = own[...]
    out[pl.ds(pl.multiple_of((1 - bit) * half, 16), half), :] = got[...]


def across_kernel(pairs, flags, *refs):
    ins, (keep, send) = refs[: 2 * pairs], refs[2 * pairs :]
    sums = [added(ins[2 * i][j], ins[2 * i + 1][j]) for i in range(pairs) for j in range(ins[2 * i].shape[0])]

    @pl.when(flags[0, 0] == 0)
    def _():
        keep[...], send[...] = sums[0], sums[1]

    @pl.when(flags[0, 0] != 0)
    def _():
        keep[...], send[...] = sums[1], sums[0]


def add_kernel(*refs):
    total = refs[0][...].astype(F32)
    for ref in refs[1:-1]:
        total = total + ref[...].astype(F32)
    refs[-1][...] = total.astype(BF)


def corner_kernel(step, flags, kept, got, *outs):
    half = kept.shape[1] // 2
    side, bit = flags[0, 0], flags[0, 1 + step]
    quarters = ((side, bit), (side, 1 - bit), (1 - side, bit), (1 - side, 1 - bit))
    for out, (layer, part) in zip(outs, quarters):
        at = (pl.ds(layer, 1), pl.ds(pl.multiple_of(part * half, 16), half), slice(None))
        out[...] = added(kept[at], got[at])[0]


class Steps:
    def __init__(self):
        count = lax.axis_size("dp")
        bits = list(range(1, (count - 1).bit_length()))
        cut = (len(bits) + 1) // 3
        orders = (bits, bits[cut : 2 * cut] + bits[:cut] + bits[2 * cut :])
        index = lax.axis_index("dp")
        core = index & 1
        self.partners = [lambda i: i ^ 1]
        self.bits = [core]
        for pair in zip(*orders):
            self.partners.append(lambda i, pair=pair: i ^ (1 << pair[i & 1]))
            self.bits.append((index >> jnp.where(core == 0, *pair)) & 1)
        self.core, self.count, self.last = core, count, len(bits)
        self.place = 0
        for bit in self.bits:
            self.place = self.place * 2 + bit
        self.flags = jnp.stack([lax.axis_index("pipe")] + self.bits).astype(jnp.int32).reshape(1, -1)

    def swap(self, value, step):
        return swapped(value, "dp", self.partners[step])

    def halve(self, step, *pairs, after=()):
        many = sum(kept.shape[0] for kept, _ in pairs)
        shape = jax.ShapeDtypeStruct((many, pairs[0][0].shape[1] // 2, D), BF)
        operands = [x for pair in pairs for x in pair]
        return kernel_call(
            functools.partial(halve_kernel, step + 1, len(pairs)), (shape, shape), (self.flags, *operands), scalars=1, after=after, direct=True
        )

    def double(self, step, own, got, after=(), weight=20):
        out = (shaped(2 * own.shape[0], D, BF),)
        return kernel_call(functools.partial(double_kernel, step), out, (self.flags, own, got), scalars=1, after=after, direct=True, weight=weight)[0]

    def half_gathered(self, value, afters):
        parts = []
        for step in range(self.last, 0, -1):
            after = afters[step - 1] if step <= len(afters) else ()
            value = self.double(step, value, self.swap(value, step), after=after, weight=0)
            parts.append(value)
        return parts

    def crossed(self, pairs, after):
        shape = shaped(*pairs[0][0].shape[1:], BF)
        operands = [x for pair in pairs for x in pair]
        kept, sent = kernel_call(
            functools.partial(across_kernel, len(pairs)), (shape, shape), (self.flags, *operands), scalars=1, after=after, direct=True
        )
        return kept, swapped_pipe(sent)

    def cornered(self, kept, got, after):
        shape = shaped(kept.shape[1] // 2, D, BF)
        own, *sent = kernel_call(
            functools.partial(corner_kernel, self.last), (shape,) * 4, (self.flags, kept, got), scalars=1, after=after, direct=True
        )
        partner = self.partners[self.last]
        pairs = [(p * self.count + i, (1 - p) * self.count + partner(i)) for p in range(2) for i in range(self.count)]
        return own, self.swap(sent[0], self.last), swapped_pipe(sent[1]), lax.ppermute(sent[2], ("pipe", "dp"), pairs)

    def doubled(self, parts, spill, outs):
        after = yield parts[0]
        (value,) = kernel_call(add_kernel, (shaped(*parts[0].shape, BF),), parts, after=after, direct=True)
        for step in range(self.last, 0, -1):
            got = self.swap(value, step)
            after = yield value
            value = self.double(step, value, got, after=after)
        got = self.swap(value, 0)
        after = yield value
        yield tuple(kernel_call(spill, outs, (self.flags, value, got), scalars=1, after=after, direct=True))


def by_core(flags, first, second, body):
    pl.when(flags[0, 1] == 0)(lambda: body(first, second))
    pl.when(flags[0, 1] != 0)(lambda: body(second, first))


def spill_ff_kernel(flags, own, other, expand, contract, cross):
    def fill(low, high):
        for j in range(FF // D):
            expand[:, rows_at(j * D)] = low[rows_at(j * D), :].astype(F32)
            contract[rows_at(j * D), :] = high[rows_at(j * D), :].astype(F32)
        cross[:, rows_at(0)] = low[rows_at(FF), :].astype(F32)
        cross[:, rows_at(D)] = high[rows_at(FF), :].astype(F32)

    by_core(flags, own, other, fill)


def spill_rest_kernel(flags, own, other, joined, out, expand_bias, branch, gain, shift):
    def fill(low, high):
        spots = ((low, 0, joined, 0), (low, 1, joined, 1), (high, 0, joined, 2), (high, 1, out, 0))
        for ref, block, to, column in spots:
            to[:, rows_at(column * D)] = ref[rows_at(block * D), :].astype(F32)
        value = low[rows_at(2 * D, 16), :].astype(F32)
        for j in range(FF // D):
            expand_bias[0:1, rows_at(j * D)] = value[j : j + 1, :]
        branch[...] = value[4:7, :]
        gain[...] = value[7:10, :]
        shift[...] = value[10:13, :]

    by_core(flags, own, other, fill)


def last_kernel(flags, expand, contract, out):
    @pl.when(flags[0, 1] == 0)
    def _():
        for j in range(2):
            out[rows_at(j * D), :] = expand[:, rows_at((2 + j) * D)]
        out[rows_at(2 * D), :] = contract[rows_at(0), :]

    @pl.when(flags[0, 1] != 0)
    def _():
        out[...] = contract[rows_at(D, 3 * D), :]


def per_device(
    embeddings, cotangent, lengths, copy_index, priority, hamming,
    self_in, self_out, cross_weight, expand, contract,
    expand_bias, branch_bias, norm_gain, norm_shift,
):
    pipe = lax.axis_index("pipe")
    leading = pipe == 0
    steps = Steps()
    flags, count = steps.flags, steps.count
    self_in, self_out, cross_weight, expand, contract = (w[0] for w in (self_in, self_out, cross_weight, expand, contract))

    rows = embeddings[0]
    small = jnp.concatenate([expand_bias.reshape(4, D), branch_bias[0], norm_gain[0], norm_shift[0]], 0)
    size = 4 * D // count

    def piece(place, blocks_of):
        block, inside = place * size // D, place * size % D
        value = lax.dynamic_slice(blocks_of[0][0], (inside, blocks_of[0][1] * D), (size, D))
        for i in range(1, 4):
            matrix, column = blocks_of[i]
            value = jnp.where(block == i, lax.dynamic_slice(matrix, (inside, column * D), (size, D)), value)
        return value

    self_piece = piece(steps.place, [(self_in, 0), (self_in, 1), (self_in, 2), (self_out, 0)])
    rest_piece = piece(lax.axis_index("dp"), [(cross_weight, 0), (cross_weight, 1), (expand, 0), (expand, 1)])
    table, bias, glance, places = row_layout(
        flags, lengths, hamming, priority.reshape(2 * T // WIN, WIN), copy_index.reshape(2 * T // WIN, WIN)
    )
    self_piece = swapped_pipe(self_piece)
    small_other = swapped_pipe(small)
    theirs = [lax.dynamic_slice_in_dim(rows, (1 - pipe) * T + at, size, 0) for at, size in PARTS]
    got = [swapped_pipe(part) for part in gate(theirs, (self_piece,))]
    self_parts = steps.half_gathered(self_piece, ((), (got[1], bias), (got[0],)))
    self_half = self_parts[-1]
    self_rest = steps.swap(self_half, 0)
    (last_piece,) = kernel_call(last_kernel, (shaped(3 * D, D, BF),), (flags, expand, contract), scalars=1, after=(self_parts[-2], small_other), direct=True, weight=0)
    last_half = swapped_pipe(last_piece)
    (rest_piece,) = gate((swapped_pipe(rest_piece),), (self_parts[0],))
    rest = lax.all_gather(rest_piece, "dp").reshape(4 * D, D)

    self_weights = (self_in, self_out, self_half, self_rest)
    (
        e_small, d_small, e_joined, e_mixed, e_stats, e_z1, x, d_joined, d_mixed, d_stats, d_z1,
    ) = first(table, flags, bias, glance, places, rows, got, self_weights, small, small_other)
    (last_half,) = gate((last_half,), (d_z1,))
    last_rest = steps.swap(last_half, 0)
    rest_weights = (cross_weight, expand, contract, rest, last_half, last_rest)
    (
        hidden, e_z2, layer_mine, layer_theirs, *dec_ff, d_ff_bias, d_ff_rows, d_cross_bias, dstates, dz1,
    ) = middle(table, flags, bias, e_z1, d_z1, rest_weights, cotangent, e_small, d_small)

    def rows_out(own, other):
        own, other = own.astype(F32), other.astype(F32)
        return jnp.where(leading, jnp.concatenate([own, other], 0), jnp.concatenate([other, own], 0))[None]

    def opened(pair):
        return [part[None] for part in pair]

    layer_other = swapped_pipe(layer_theirs)
    dec_kept, dec_sent = opened(dec_ff)
    dec_got = steps.swap(dec_sent, 0)
    *dec_self, target_grad, copies_grad = decoder_self_back(
        table, flags, bias, dz1, x, d_joined, d_mixed, d_stats, glance, places, self_weights,
        d_ff_bias, d_ff_rows, d_cross_bias, count,
    )
    dself_kept, dself_sent = opened(dec_self)
    dself_got = steps.swap(dself_sent, 0)
    (dec_got,) = gate((dec_got,), (target_grad,))
    dec_kept, dec_sent = steps.halve(0, (dec_kept, dec_got))
    dec_got = steps.swap(dec_sent, 1)
    *enc_ff, e_ff_bias, e_ff_rows, inner, dz = encoder_ff_back(
        flags, dstates, e_z1, e_z2, hidden, rest_weights, e_small, after=(dec_kept,)
    )
    enc_kept, enc_sent = opened(enc_ff)
    enc_got = steps.swap(enc_sent, 0)
    dec_got, dself_got = gate((dec_got, dself_got), (dz,))
    dec_kept, dec_sent = steps.halve(1, (dec_kept, dec_got))
    dec_got = steps.swap(dec_sent, 2)
    dself_kept, dself_sent = steps.halve(0, (dself_kept, dself_got))
    dself_got = steps.swap(dself_sent, 1)
    last_bias, e_dz1 = encoder_ff_last(flags, inner, dz, e_z1, rest_weights, e_small, after=(dec_kept, dself_kept))
    enc_got, dec_got = gate((enc_got, dec_got), (e_dz1,))
    dec_kept, dec_sent = steps.halve(2, (dec_kept, dec_got))
    dec_got = steps.swap(dec_sent, 3)
    enc_kept, enc_sent = steps.halve(0, (enc_kept, enc_got))
    enc_got = steps.swap(enc_sent, 1)
    *enc_self, grad_mine, grad_theirs = encoder_self_back(
        table, flags, bias, e_dz1, rows, got, e_joined, e_mixed, e_stats, copies_grad, self_weights, e_small,
        e_ff_bias, e_ff_rows, last_bias, target_grad, count, after=(enc_kept, dec_kept),
    )

    grad_other = swapped_pipe(grad_theirs)
    self_kept, self_sent = opened(enc_self)
    self_got = steps.swap(self_sent, 0)
    enc_got, dec_got, dself_got = gate((enc_got, dec_got, dself_got), (grad_mine,))

    def ff_sum():
        enc_pair, dec_pair = (enc_kept, enc_got), (dec_kept, dec_got)
        after = yield
        for step in range(1, steps.last):
            kept, sent = steps.halve(step, enc_pair, after=after)
            enc_pair = (kept, steps.swap(sent, step + 1))
            if step + 2 < steps.last:
                kept, sent = steps.halve(step + 2, dec_pair, after=(kept,))
                dec_pair = (kept, steps.swap(sent, step + 3))
            after = yield kept
        outs = (shaped(D, FF, F32), shaped(FF, D, F32), shaped(D, 2 * D, F32))
        yield from steps.doubled(steps.crossed((enc_pair, dec_pair), after), spill_ff_kernel, outs)

    def self_sum():
        pairs = [(self_kept, self_got)]
        after = yield
        for step in range(steps.last - 1):
            kept, sent = steps.halve(step, *pairs, after=after)
            pairs = [(kept, steps.swap(sent, step + 1))]
            if step == 0:
                pairs.append((dself_kept, dself_got))
            after = yield kept
        outs = (shaped(D, 3 * D, F32), shaped(D, D, F32), shaped(1, FF, F32)) + (shaped(3, D, F32),) * 3
        yield from steps.doubled(steps.cornered(*pairs[0], after), spill_rest_kernel, outs)

    chains = [ff_sum(), self_sum()]
    results = [None, None]
    mark = dself_got
    for chain in chains:
        next(chain)
    live = [0, 1]
    turn = 0
    while live:
        if turn == 5:
            layer = gate((layer_mine, layer_other), (mark,))
            layer_out, embedding_grad = rows_out(*layer), rows_out(*gate((grad_mine, grad_other), (mark,)))
        for i in list(live):
            extra = (layer_out, embedding_grad) if turn == 7 else ()
            value = chains[i].send((mark, *extra))
            if isinstance(value, tuple):
                results[i] = value
                live.remove(i)
                value = value[0]
            mark = value
        turn += 1
    expand_grad, contract_grad, cross_grad = results[0]
    in_grad, out_grad, *small_grads = results[1]
    return (
        layer_out,
        embedding_grad,
        in_grad[None],
        out_grad[None],
        cross_grad[None],
        expand_grad[None],
        contract_grad[None],
        small_grads[0],
        *(part[None] for part in small_grads[1:]),
    )


def solution(mesh):
    return jax.shard_map(
        per_device,
        mesh=mesh,
        in_specs=(
            P("pipe", "dp", None),
            P("dp", None),
            P("dp", None),
            P("dp"),
            P("dp"),
            P("dp", None),
            P("pipe", None, None),
            P("pipe", None, None),
            P("pipe", None, None),
            P("pipe", None, None),
            P("pipe", None, None),
            P("pipe", None),
            P("pipe", None, None),
            P("pipe", None, None),
            P("pipe", None, None),
        ),
        out_specs=(
            P("pipe", "dp", None),
            P("pipe", "dp", None),
            P("pipe", None, None),
            P("pipe", None, None),
            P("pipe", None, None),
            P("pipe", None, None),
            P("pipe", None, None),
            P("pipe", None),
            P("pipe", None, None),
            P("pipe", None, None),
            P("pipe", None, None),
        ),
        check_vma=False,
    )
```

```python
import functools
import math

import jax
import jax.numpy as jnp
from jax import lax
from jax.experimental import pallas as pl
from jax.experimental.pallas import tpu as pltpu
from jax.sharding import PartitionSpec as P

HEADS = 8
D = 512
FF = 2048
T = 1024
SENTS = 17
WIN = 128
EPSILON = 1e-05
NEG = -1e30
BF = jnp.bfloat16
F32 = jnp.float32
VMEM = pl.BlockSpec(memory_space=pltpu.VMEM)
SMEM = pl.BlockSpec(memory_space=pltpu.SMEM)
BLOCK = 512
STEPS = T // BLOCK


def nn(a, b):
    return jnp.dot(a, b, preferred_element_type=F32)


def nt(a, b):
    return lax.dot_general(a, b, (((1,), (1,)), ((), ())), preferred_element_type=F32)


def tn(a, b):
    return lax.dot_general(a, b, (((0,), (0,)), ((), ())), preferred_element_type=F32)


def normalized(value):
    center = jnp.mean(value, axis=-1, keepdims=True)
    centered = value - center
    spread = jnp.mean(centered * centered, axis=-1, keepdims=True)
    scale = lax.rsqrt(spread + EPSILON)
    return centered * scale, scale


def normalized_back(grad, unit, scale):
    first = jnp.mean(grad, axis=-1, keepdims=True)
    second = jnp.mean(grad * unit, axis=-1, keepdims=True)
    return scale * (grad - first - unit * second)


def folded(value):
    return jnp.sum(value.reshape(value.shape[0] // 8, 8, value.shape[1]), axis=0)


def column_sum(value):
    return jnp.sum(value, axis=0, keepdims=True)


def each_block(body):
    for index in range(STEPS):
        body(pl.ds(index * BLOCK, BLOCK))


def each_chunk(count, size, body):
    def step(index, carry):
        body(pl.multiple_of(index * size, size))
        return carry

    lax.fori_loop(0, count, step, 0)


class Held:
    def __init__(self, ref, copy):
        self.ref, self.copy = ref, copy

    def ready(self):
        if self.copy is not None:
            self.copy.wait()
            self.copy = None
        return self.ref

    def __getitem__(self, index):
        return self.ready()[index]

    @property
    def at(self):
        return self.ready().at

    @property
    def shape(self):
        return self.ref.shape


def ready(value):
    return value.ready() if isinstance(value, (Held, Landing)) else value


LEAVING = {}
WAITING = []


def arrive():
    for copy in WAITING:
        copy.start()
    WAITING.clear()


def leave(*refs):
    for ref in refs:
        copy, started = LEAVING.get(id(ref), (None, True))
        if not started:
            copy.start()
            LEAVING[id(ref)] = (copy, True)


class Landing:
    def __init__(self, ref, sem):
        self.ref, self.sem = ref, sem

    def ready(self):
        if self.sem is not None:
            pltpu.make_async_copy(self.ref, self.ref, self.sem).wait()
            self.sem = None
        return self.ref

    def __getitem__(self, index):
        return self.ready()[index]

    @property
    def at(self):
        return self.ready().at

    @property
    def shape(self):
        return self.ref.shape


class Raw:
    def __init__(self, value):
        self.value, self.shape, self.dtype = value, value.shape, value.dtype


def bytes_of(x):
    return math.prod(x.shape) * jnp.dtype(x.dtype).itemsize


LARGE = 256 << 10


def kernel_call(body, outs, operands, scalars=0, scratch=(), out_specs=None, flops=0, after=(), direct=False, weight=20, room_for=52, hold=False, stay=False):
    size = sum(bytes_of(x) for x in (*operands, *outs))
    held = size + (sum(bytes_of(x) for x in scratch) if direct else 0)
    count, many, extra = len(operands), len(outs), len(scratch)
    raw = [isinstance(x, Raw) for x in operands]
    comes = [not (direct or stay or r) and i >= scalars and bytes_of(x) >= LARGE for i, (x, r) in enumerate(zip(operands, raw))]
    goes = [not direct and bytes_of(x) >= LARGE for x in outs]
    anywhere = pl.BlockSpec(memory_space=pl.ANY)
    in_specs = [SMEM] * scalars + [anywhere if c or r else VMEM for c, r in zip(comes[scalars:], raw[scalars:])] + [anywhere] * len(after)
    specs = list(out_specs) if out_specs else [VMEM] * many
    specs = [anywhere if g else spec for g, spec in zip(goes, specs)]
    room = [pltpu.VMEM(x.shape, x.dtype) for x, c in zip((*operands, *outs), comes + goes) if c]
    sems = [pltpu.SemaphoreType.DMA((len(room),))] if room else []

    def run(*refs):
        ins, rest = list(refs[:count]), refs[count + len(after) :]
        results, rest = list(rest[:many]), rest[many:]
        own, rest = rest[:extra], rest[extra:]
        buffers, slot = rest[: len(room)], 0
        for i, c in enumerate(comes):
            if c:
                copy = pltpu.make_async_copy(ins[i], buffers[slot], rest[-1].at[slot])
                WAITING.append(copy)
                ins[i] = Held(buffers[slot], copy)
                slot += 1
        if not hold:
            arrive()
        LEAVING.clear()
        for i, g in enumerate(goes):
            if g:
                copy = pltpu.make_async_copy(buffers[slot], results[i], rest[-1].at[slot])
                results[i] = buffers[slot]
                LEAVING[id(results[i])] = (copy, False)
                slot += 1
        body(*ins, *results, *own)
        assert not WAITING
        for value in ins:
            ready(value)
        for i, g in enumerate(goes):
            if g:
                leave(results[i])
        for i, g in enumerate(goes):
            if g:
                LEAVING[id(results[i])][0].wait()
        LEAVING.clear()

    return pl.pallas_call(
        run,
        out_shape=tuple(outs),
        in_specs=in_specs,
        out_specs=tuple(specs),
        scratch_shapes=list(scratch) + room + sems,
        compiler_params=pltpu.CompilerParams(vmem_limit_bytes=held + (3 << 20) if direct else room_for << 20),
        cost_estimate=pl.CostEstimate(flops=weight * (flops or 2 * FLOP_UNIT), bytes_accessed=weight * size, transcendentals=0),
    )(*(x.value if isinstance(x, Raw) else x for x in operands), *after)


def shaped(rows, columns, kind):
    return jax.ShapeDtypeStruct((rows, columns), kind)


def layout_kernel(flags, lengths, hamming, priority, copies, table, bias, glance, places):
    row = flags[0, 0]
    ends = []
    total = jnp.int32(0)
    for j in range(SENTS):
        total = total + lengths[row, j]
        ends.append(total)
    count = jnp.int32(0)
    first = jnp.int32(0)

    def origin(start):
        return jnp.minimum((start // 16) * 16, T - WIN)

    for j in range(SENTS):
        begin = jnp.int32(0) if j == 0 else ends[j - 1]
        opens = (ends[j] - origin(first)) > WIN
        if j == 0:
            opens = jnp.bool_(False)
        first = jnp.where(opens, begin, first)
        count = jnp.where(opens, count + 1, count)
        table[0, 1 + count] = origin(first)
        table[0, 32 + count] = first
        table[0, 64 + count] = ends[j]
    table[0, 0] = count + 1

    lanes = lax.broadcasted_iota(jnp.int32, (8, WIN), 1)
    rows = lax.broadcasted_iota(jnp.int32, (8, WIN), 0)
    place = rows * WIN + lanes
    quota = jnp.zeros((8, WIN), jnp.int32) + (hamming[row, 0] + 1) // 2
    for j in range(SENTS - 1):
        change = (hamming[row, j + 1] + 1) // 2 - (hamming[row, j] + 1) // 2
        quota = quota + jnp.where(place >= ends[j], change, 0)
    part = pl.ds(pl.multiple_of(row * (T // WIN), 8), T // WIN)
    chosen = jnp.where(priority[part, :] < quota, 1.0, 0.0)
    copy = copies[part, :].astype(F32)
    for i in range(T // WIN):
        part = pl.ds(i * WIN, WIN)
        glance[part, :] = jnp.broadcast_to(chosen[i : i + 1, :], (WIN, WIN)).T
        places[part, :] = jnp.broadcast_to(copy[i : i + 1, :], (WIN, WIN)).T.astype(jnp.int32)

    def window(w, carry):
        at = table[0, 1 + w]
        here = lanes + at
        segment = jnp.zeros((8, WIN), F32)
        for j in range(SENTS):
            segment = segment + jnp.where(here >= ends[j], 1.0, 0.0)
        inside = (here >= table[0, 32 + w]) & (here < table[0, 64 + w])
        segment = jnp.where(inside, segment, -1.0)
        across = jnp.broadcast_to(segment[0:1, :], (WIN, WIN))
        down = across.T
        bias[w] = jnp.where((across == down) & (across >= 0.0), 0.0, NEG)
        return carry

    lax.fori_loop(0, count + 1, window, 0)
    for extra in range(1, WIDE_GROUP):
        table[0, 1 + count + extra] = 0
        bias[count + extra] = jnp.full((WIN, WIN), NEG, F32)


def row_layout(flags, lengths, hamming, priority, copies):
    outs = (
        shaped(1, 128, jnp.int32),
        jax.ShapeDtypeStruct((WINDOWS, WIN, WIN), F32),
        shaped(T, WIN, F32),
        shaped(T, WIN, jnp.int32),
    )
    return kernel_call(
        layout_kernel,
        outs,
        (flags, lengths, hamming, priority, copies),
        scalars=3,
        out_specs=(SMEM, VMEM, VMEM, VMEM),
        direct=True,
        weight=0,
    )


def pair_halves(part):
    low = lax.broadcasted_iota(jnp.int32, (WIN, WIN), 1) < 64
    zero = jnp.zeros_like(part)
    return jnp.concatenate([jnp.where(low, part, zero), jnp.where(low, zero, part)], axis=0)


def pair_join(both):
    low = lax.broadcasted_iota(jnp.int32, (WIN, WIN), 1) < 64
    return jnp.where(low, both[:WIN], both[WIN:])


PAIRS = [slice(i * 128, i * 128 + 128) for i in range(HEADS // 2)]


PAIRS = [slice(i * 128, i * 128 + 128) for i in range(HEADS // 2)]
GROUP = 2
WIDE_GROUP = 4
WINDOWS = SENTS + WIDE_GROUP - 1


def grouped(table, body, many=GROUP):
    def step(index, carry):
        body([index * many + i for i in range(many)])
        return carry

    lax.fori_loop(0, (table[0, 0] + many - 1) // many, step, 0)


def spread(table, windows):
    ats = [pl.ds(pl.multiple_of(table[0, 1 + w], 16), WIN) for w in windows]
    return [(w, pair, at, lanes) for w, at in zip(windows, ats) for pair, lanes in enumerate(PAIRS)]


def masks(bias, windows):
    out = []
    for w in windows:
        masked = bias[w]
        out += [jnp.concatenate([masked, masked], axis=1)] * len(PAIRS)
    return out


def attend(table, bias, queries, keys, values, mixed, stats):
    bias, queries, keys, values = map(ready, (bias, queries, keys, values))

    def body(windows):
        parts = spread(table, windows)
        masked = masks(bias, windows)
        query = [pair_halves(queries[at, lanes]) for _, _, at, lanes in parts]
        key = [keys[at, lanes] for _, _, at, lanes in parts]
        value = [values[at, lanes] for _, _, at, lanes in parts]
        scores = [nt(k, q) + mask for k, q, mask in zip(key, query, masked)]
        highest = [jnp.maximum(jnp.max(s, axis=0, keepdims=True), -1e29) for s in scores]
        raised = [jnp.exp(s - h) for s, h in zip(scores, highest)]
        inverse = [1.0 / jnp.maximum(jnp.sum(r, axis=0, keepdims=True), 1e-30) for r in raised]
        shares = [(r * i).astype(BF) for r, i in zip(raised, inverse)]
        out = [pair_join(tn(s, v)).astype(BF) for s, v in zip(shares, value)]
        for (w, pair, at, lanes), o, h, i in zip(parts, out, highest, inverse):
            mixed[at, lanes] = mixed[at, lanes] + o
            stats[w * 4 + pair, 0:1, :] = h
            stats[w * 4 + pair, 1:2, :] = i

    mixed[...] = jnp.zeros_like(mixed)
    grouped(table, body, WIDE_GROUP)


def attend_back(table, bias, queries, keys, values, stats, grad, grad_q, grad_k, grad_v):
    bias, queries, keys, values, stats = map(ready, (bias, queries, keys, values, stats))

    def body(windows):
        parts = spread(table, windows)
        masked = masks(bias, windows)
        query = [pair_halves(queries[at, lanes]) for _, _, at, lanes in parts]
        key = [keys[at, lanes] for _, _, at, lanes in parts]
        value = [values[at, lanes] for _, _, at, lanes in parts]
        out = [pair_halves(grad[at, lanes]) for _, _, at, lanes in parts]
        top = [stats[w * 4 + pair, 0:1, :] for w, pair, _, _ in parts]
        inverse = [stats[w * 4 + pair, 1:2, :] for w, pair, _, _ in parts]
        scores = [nt(k, q) + mask for k, q, mask in zip(key, query, masked)]
        back = [nt(v, o) for v, o in zip(value, out)]
        shares = [jnp.exp(s - h) * i for s, h, i in zip(scores, top, inverse)]
        got_v = [nn(s.astype(BF), o).astype(BF) for s, o in zip(shares, out)]
        total = [jnp.sum(s * b, axis=0, keepdims=True) for s, b in zip(shares, back)]
        scored = [(s * (b - t)).astype(BF) for s, b, t in zip(shares, back, total)]
        got_k = [nn(s, q).astype(BF) for s, q in zip(scored, query)]
        got_q = [(pair_join(tn(s, k)) * 0.125).astype(BF) for s, k in zip(scored, key)]
        for ref, got in zip((grad_q, grad_k, grad_v), (got_q, got_k, got_v)):
            for (_, _, at, lanes), value_got in zip(parts, got):
                ref[at, lanes] = ref[at, lanes] + value_got

    for ref in (grad_q, grad_k, grad_v):
        ref[...] = jnp.zeros_like(ref)
    grouped(table, body)


STATS = jax.ShapeDtypeStruct((WINDOWS * 4, 2, 2 * WIN), F32)


def thirds(ref):
    return tuple(ref.at[:, i * D : (i + 1) * D] for i in range(ref.shape[1] // D))


def put(flags, half, kept, sent, rows, value):
    @pl.when(flags[0, 1] == half)
    def _():
        kept[rows, :] = value

    @pl.when(flags[0, 1] != half)
    def _():
        sent[rows, :] = value


def put_side(flags, side, mine, theirs, rows, value):
    @pl.when(flags[0, 0] == side)
    def _():
        mine[rows, :] = value

    @pl.when(flags[0, 0] != side)
    def _():
        theirs[rows, :] = value


def rows_at(start, count=D):
    return slice(start, start + count)


def scaled(unit, small, slot):
    return unit * small[7 + slot : 8 + slot, :] + small[10 + slot : 11 + slot, :]


def project(x, weight_in, joined, at):
    got = nn(x, weight_in[...])
    joined[at, :D] = (got[:, :D] * 0.125).astype(BF)
    joined[at, D:] = got[:, D:].astype(BF)


def encoder_self_kernel(table, bias, source, weight_in, weight_out, small, joined, mixed, stats, z, x):
    def before(at):
        unit, _ = normalized(source[at, :].astype(F32))
        value = scaled(unit, small, 2)
        x[at, :] = value
        project(value.astype(BF), weight_in, joined, at)

    each_block(before)
    leave(joined)
    attend(table, bias, *thirds(joined), mixed, stats)
    leave(mixed, stats)

    def after(at):
        z[at, :] = x[at, :] + nn(mixed[at, :], weight_out[...]) + small[4:5, :]

    each_block(after)


def copy_hits(bias, places, w, start):
    at = pl.ds(start, WIN)
    lanes = lax.broadcasted_iota(jnp.int32, (WIN, WIN), 1) + start
    inside = jnp.max(bias[w], axis=1, keepdims=True) == 0.0
    return at, jnp.where((places[at, :] == lanes) & inside, 1.0, 0.0).astype(BF)


def kept_rows(glance, at):
    return jnp.concatenate([glance[at, :]] * (D // WIN), axis=1) > 0.5


def decoder_self_kernel(
    table, bias, source, target, glance, places, weight_in, weight_out, small, x, joined, mixed, stats, z, copied
):
    copied[...] = jnp.zeros_like(copied)
    bias, places, source = map(ready, (bias, places, source))

    def gather(windows):
        parts = [copy_hits(bias, places, w, pl.multiple_of(table[0, 1 + w], 16)) for w in windows]
        got = [nn(hit, source[at, :]).astype(BF) for at, hit in parts]
        for (at, _), value in zip(parts, got):
            copied[at, :] = copied[at, :] + value

    grouped(table, gather)

    def before(at):
        value = jnp.where(kept_rows(glance, at), target[at, :].astype(F32), copied[at, :].astype(F32)).astype(BF)
        x[at, :] = value
        project(value, weight_in, joined, at)

    each_block(before)
    leave(joined)
    attend(table, bias, *thirds(joined), mixed, stats)
    leave(mixed, stats)

    def after(at):
        z[at, :] = x[at, :].astype(F32) + nn(mixed[at, :], weight_out[...]) + small[4:5, :]

    each_block(after)


FLOP_UNIT = 2 * T * D * D


ROOT = 0.7978845608028654
CUBE = 0.044715


def gelu_parts(u):
    square = u * u
    bent = jnp.tanh(u * (ROOT + ROOT * CUBE * square))
    half = 0.5 + 0.5 * bent
    slope = half + (u - u * (bent * bent)) * (0.5 * ROOT + 1.5 * ROOT * CUBE * square)
    return u * half, slope


def expand_block(value, expand, small, active, slope, at):
    for j in range(FF // D):
        cols = rows_at(j * D)
        hidden = (nn(value, expand[:, cols]) + small[j : j + 1, :]).astype(BF)
        active[at, cols], slope[at, cols] = gelu_parts(hidden)


def encoder_ff_kernel(flags, z1, expand, contract, cross, small, inner, z2, mine, theirs, states, active):
    def block(at):
        unit, _ = normalized(z1[at, :])
        value = scaled(unit, small, 0)
        for j in range(FF // D):
            cols = rows_at(j * D)
            hidden = (nn(value.astype(BF), expand[:, cols]) + small[j : j + 1, :]).astype(BF)
            inner[at, cols] = hidden
            active[at, cols], _ = gelu_parts(hidden)
        total = value + nn(active[at, :], contract[...]) + small[5:6, :]
        z2[at, :] = total
        unit, _ = normalized(total)
        out = scaled(unit, small, 1)
        put_side(flags, 0, mine, theirs, at, out.astype(BF))
        got = nn(out.astype(BF), cross[...])
        states[at, :D] = got[:, :D].astype(BF)
        states[at, D:] = (got[:, D:] + small[6:7, :]).astype(BF)

    each_block(block)
    leave(inner, z2)


def ff_back(flags, dzb, value_b, active, inner, contract, kept, sent, bias_rows):
    def block(at):
        for j in range(FF // D):
            cols = rows_at(j * D)
            back = nt(dzb[at, :], contract[cols, :])
            inner[at, cols] = (back * inner[at, cols].astype(F32)).astype(BF)

    each_block(block)
    for c in range(FF // D):
        cols = rows_at(c * D)
        put(flags, 1, kept, sent, cols, tn(active[:, cols], dzb[...]).astype(BF))
        put(flags, 0, kept, sent, cols, tn(value_b[...], inner[:, cols]).astype(BF))
        bias_rows[c : c + 1, :] = column_sum(inner[:, cols].astype(F32))


def decoder_ff_kernel(
    flags, z2, expand, contract, small, cotangent,
    mine, theirs, kept, sent, bias_grads, bias_rows, dz2,
    active, inner, value_b, dz, dzb,
):
    bias_grads[...] = jnp.zeros_like(bias_grads)
    offset = flags[0, 0] * T

    def block(at):
        unit, _ = normalized(z2[at, :])
        value = scaled(unit, small, 1)
        value_b[at, :] = value.astype(BF)
        expand_block(value.astype(BF), expand, small, active, inner, at)
        total = value + nn(active[at, :], contract[...]) + small[5:6, :]
        unit, scale = normalized(total)
        put_side(flags, 1, mine, theirs, at, scaled(unit, small, 2).astype(BF))
        wanted = cotangent[pl.ds(pl.multiple_of(offset + at.start, BLOCK), BLOCK), :].astype(F32)
        bias_grads[0:1, :] += column_sum(wanted * unit)
        bias_grads[1:2, :] += column_sum(wanted)
        back = normalized_back(wanted * small[9:10, :], unit, scale)
        bias_grads[2:3, :] += column_sum(back)
        dz[at, :] = back
        dzb[at, :] = back.astype(BF)

    each_block(block)
    leave(mine, theirs)
    ff_back(flags, dzb, value_b, active, inner, contract, kept, sent, bias_rows)

    def last(at):
        back = dz[at, :] + nt(inner[at, :], expand[...])
        unit, scale = normalized(z2[at, :])
        bias_grads[3:4, :] += column_sum(back * unit)
        bias_grads[4:5, :] += column_sum(back)
        dz2[at, :] = normalized_back(back * small[8:9, :], unit, scale)

    each_block(last)


def encoder_ff_back_kernel(
    flags, z2, dstates, z1, hidden, own_cross, own_expand, own_contract, rest, half, last_half, small,
    kept, sent, bias_grads, bias_rows, inner, dz,
    cross, contract, active, value_b, memory_b, dzb, sems,
):
    own = (own_cross, own_expand, own_contract, rest, half, last_half)
    cross, _, contract = fetch_rest(0, flags, *own, cross, None, contract, sems)
    arrive()
    bias_grads[...] = jnp.zeros_like(bias_grads)

    def block(at):
        unit, scale = normalized(z2[at, :])
        memory_b[at, :] = scaled(unit, small, 1).astype(BF)
        back = nt(dstates[at, :], cross[...])
        bias_grads[0:1, :] += column_sum(dstates[at, D:].astype(F32))
        bias_grads[1:2, :] += column_sum(back * unit)
        bias_grads[2:3, :] += column_sum(back)
        back = normalized_back(back * small[8:9, :], unit, scale)
        bias_grads[3:4, :] += column_sum(back)
        dz[at, :] = back
        dzb[at, :] = back.astype(BF)
        unit, _ = normalized(z1[at, :])
        value_b[at, :] = scaled(unit, small, 0).astype(BF)
        for j in range(FF // D):
            cols = rows_at(j * D)
            active[at, cols], inner[at, cols] = gelu_parts(hidden[at, cols])

    each_block(block)
    leave(dz)
    ff_back(flags, dzb, value_b, active, inner, contract, kept, sent, bias_rows)
    leave(inner)
    for c in range(2):
        put(flags, c, kept, sent, rows_at(FF), tn(memory_b[...], dstates[:, rows_at(c * D)]).astype(BF))


def encoder_ff_back(flags, dstates, z1, z2, hidden, weights, small, after=()):
    outs = (
        shaped(FF + D, D, BF), shaped(FF + D, D, BF),
        shaped(8, D, F32), shaped(8, D, F32), shaped(T, FF, BF), shaped(T, D, F32),
    )
    return kernel_call(
        encoder_ff_back_kernel,
        outs,
        (flags, z2, dstates, z1, hidden, *map(Raw, weights), small),
        scalars=1,
        scratch=[
            pltpu.VMEM((D, 2 * D), BF),
            pltpu.VMEM((FF, D), BF),
            pltpu.VMEM((T, FF), BF),
            pltpu.VMEM((T, D), BF),
            pltpu.VMEM((T, D), BF),
            pltpu.VMEM((T, D), BF),
            pltpu.SemaphoreType.DMA((3,)),
        ],
        flops=18 * FLOP_UNIT,
        after=after,
        hold=True,
    )


def encoder_ff_last_kernel(
    flags, inner, dz, z1, own_cross, own_expand, own_contract, rest, half, last_half, small,
    bias_grads, dz1,
    expand, sems,
):
    own = (own_cross, own_expand, own_contract, rest, half, last_half)
    _, expand, _ = fetch_rest(0, flags, *own, None, expand, None, sems)
    arrive()
    bias_grads[...] = jnp.zeros_like(bias_grads)

    def last(at):
        back = dz[at, :] + nt(inner[at, :], expand[...])
        unit, scale = normalized(z1[at, :])
        bias_grads[4:5, :] += column_sum(back * unit)
        bias_grads[5:6, :] += column_sum(back)
        dz1[at, :] = normalized_back(back * small[7:8, :], unit, scale)

    each_block(last)


def encoder_ff_last(flags, inner, dz, z1, weights, small, after=()):
    return kernel_call(
        encoder_ff_last_kernel,
        (shaped(8, D, F32), shaped(T, D, F32)),
        (flags, inner, dz, z1, *map(Raw, weights), small),
        scalars=1,
        scratch=[pltpu.VMEM((D, FF), BF), pltpu.SemaphoreType.DMA((3,))],
        flops=4 * FLOP_UNIT,
        after=after,
        hold=True,
    )


def decoder_cross_kernel(table, bias, z1, states, weight, small, queries, mixed, stats, z2, x):
    def before(at):
        unit, _ = normalized(z1[at, :])
        value = scaled(unit, small, 0)
        x[at, :] = value
        queries[at, :] = (nn(value.astype(BF), weight[:, :D]) * 0.125).astype(BF)

    each_block(before)
    attend(table, bias, queries, *thirds(states), mixed, stats)

    def after(at):
        z2[at, :] = x[at, :] + nn(mixed[at, :], weight[:, D:]) + small[6:7, :]

    each_block(after)


def decoder_cross_back_kernel(
    table, flags, bias, dz2, z1, queries, states, mixed, stats, weight, small,
    kept, sent, bias_grads, dstates, dz1,
    value_b, dzb, out, dq,
):
    bias_grads[...] = jnp.zeros_like(bias_grads)

    def before(at):
        bias_grads[0:1, :] += column_sum(dz2[at, :])
        low = dz2[at, :].astype(BF)
        dzb[at, :] = low
        out[at, :] = nt(low, weight[:, D:]).astype(BF)
        unit, _ = normalized(z1[at, :])
        value_b[at, :] = scaled(unit, small, 0).astype(BF)

    each_block(before)
    attend_back(table, bias, queries, *thirds(states), stats, out, dq, *thirds(dstates))
    leave(dstates)
    put(flags, 0, kept, sent, rows_at(FF), tn(value_b[...], dq[...]).astype(BF))
    put(flags, 1, kept, sent, rows_at(FF), tn(mixed[...], dzb[...]).astype(BF))
    leave(kept, sent)

    def after(at):
        back = dz2[at, :] + nt(dq[at, :], weight[:, :D])
        unit, scale = normalized(z1[at, :])
        bias_grads[1:2, :] += column_sum(back * unit)
        bias_grads[2:3, :] += column_sum(back)
        dz1[at, :] = normalized_back(back * small[7:8, :], unit, scale)

    each_block(after)


def self_back(table, bias, flags, dz, x, joined, mixed, stats, weight_in, weight_out, kept, sent, acc, dzb, out, djoined):
    acc[...] = jnp.zeros_like(acc)

    def before(at):
        acc[0:1, :] += column_sum(dz[at, :])
        low = dz[at, :].astype(BF)
        dzb[at, :] = low
        out[at, :] = nt(low, weight_out[...]).astype(BF)

    each_block(before)
    attend_back(table, bias, *thirds(joined), stats, out, *thirds(djoined))
    for c in range(3):
        value = tn(x[...], djoined[:, rows_at(c * D)]).astype(BF)
        put(flags, c // 2, kept, sent, rows_at(c % 2 * D), value)
    put(flags, 1, kept, sent, rows_at(D), tn(mixed[...], dzb[...]).astype(BF))


def put_small(flags, kept, sent, rows):
    count = kept.shape[0] - 2 * D
    at = rows_at(2 * D, count)
    filled = jnp.concatenate(rows + [jnp.zeros((count - 13, D), F32)], axis=0).astype(BF)
    put(flags, 0, kept, sent, at, filled)
    put(flags, 1, kept, sent, at, jnp.zeros((count, D), BF))


def decoder_self_back_kernel(
    table, flags, dz, own_in, own_out, half, rest, joined, bias, stats, x, mixed, glance, places,
    ff_bias, ff_rows, cross_bias,
    kept, sent, target_grad, source_grad,
    weight_in, weight_out, acc, dzb, out, djoined, dcopied, sems,
):
    weight_in, weight_out = fetch_self(1, flags, own_in, own_out, half, rest, weight_in, weight_out, sems)
    arrive()
    self_back(table, bias, flags, dz, x, joined, mixed, stats, weight_in, weight_out, kept, sent, acc, dzb, out, djoined)
    put_small(
        flags, kept, sent,
        [
            ff_rows[0:4, :], acc[0:1, :], ff_bias[2:3, :], cross_bias[0:1, :],
            cross_bias[1:2, :], ff_bias[3:4, :], ff_bias[0:1, :],
            cross_bias[2:3, :], ff_bias[4:5, :], ff_bias[1:2, :],
        ],
    )

    def after(at):
        back = dz[at, :] + nt(djoined[at, :], weight_in[...])
        kept_at = kept_rows(glance, at)
        target_grad[at, :] = jnp.where(kept_at, back, 0.0).astype(BF)
        dcopied[at, :] = jnp.where(kept_at, 0.0, back).astype(BF)

    each_block(after)
    leave(target_grad, kept, sent)
    source_grad[...] = jnp.zeros_like(source_grad)
    bias, places = ready(bias), ready(places)

    def scatter(windows):
        parts = [copy_hits(bias, places, w, pl.multiple_of(table[0, 1 + w], 16)) for w in windows]
        got = [tn(hit, dcopied[at, :]).astype(BF) for at, hit in parts]
        for (at, _), value in zip(parts, got):
            source_grad[at, :] = source_grad[at, :] + value

    grouped(table, scatter)


def half_rows(count):
    return 2 * D + 8 * count


def decoder_self_back(table, flags, bias, dz, x, joined, mixed, stats, glance, places, weights, ff_bias, ff_rows, cross_bias, count, after=()):
    half = half_rows(count)
    outs = (shaped(half, D, BF), shaped(half, D, BF), shaped(T, D, BF), shaped(T, D, BF))
    return kernel_call(
        decoder_self_back_kernel,
        outs,
        (table, flags, dz, *map(Raw, weights), joined, bias, stats, x, mixed, glance, places, ff_bias, ff_rows, cross_bias),
        scalars=2,
        scratch=[
            pltpu.VMEM((D, 3 * D), BF), pltpu.VMEM((D, D), BF),
            pltpu.VMEM((8, D), F32), pltpu.VMEM((T, D), BF), pltpu.VMEM((T, D), BF),
            pltpu.VMEM((T, 3 * D), BF), pltpu.VMEM((T, D), BF), pltpu.SemaphoreType.DMA((2,)),
        ],
        flops=18 * FLOP_UNIT,
        after=after,
        hold=True,
    )


def encoder_self_back_kernel(
    table, flags, dz, rows, got_0, got_1, own_in, own_out, half, rest, joined, bias, stats, mixed, copies_grad, small,
    ff_bias, ff_rows, last_bias, target_grad,
    kept, sent, mine, theirs,
    source, weight_in, weight_out, acc, x, dzb, out, djoined, sems,
):
    @pl.when(flags[0, 0] == 0)
    def _():
        start((rows.at[rows_at(0, T), :], source, sems.at[2]))

    @pl.when(flags[0, 0] != 0)
    def _():
        start(*row_parts((got_0, got_1), source, sems.at[2]))

    source = Landing(source, sems.at[2])
    weight_in, weight_out = fetch_self(0, flags, own_in, own_out, half, rest, weight_in, weight_out, sems)
    arrive()

    def first(at):
        unit, _ = normalized(source[at, :].astype(F32))
        x[at, :] = scaled(unit, small, 2).astype(BF)

    each_block(first)
    self_back(table, bias, flags, dz, x, joined, mixed, stats, weight_in, weight_out, kept, sent, acc, dzb, out, djoined)

    def after(at):
        back = dz[at, :] + nt(djoined[at, :], weight_in[...])
        unit, scale = normalized(source[at, :].astype(F32))
        acc[1:2, :] += column_sum(back * unit)
        acc[2:3, :] += column_sum(back)
        value = normalized_back(back * small[9:10, :], unit, scale) + copies_grad[at, :].astype(F32)
        put_side(flags, 0, mine, theirs, at, value.astype(BF))
        put_side(flags, 1, mine, theirs, at, target_grad[at, :])

    each_block(after)
    put_small(
        flags, kept, sent,
        [
            ff_rows[0:4, :], acc[0:1, :], ff_bias[3:4, :], ff_bias[0:1, :],
            last_bias[4:5, :], ff_bias[1:2, :], acc[1:2, :],
            last_bias[5:6, :], ff_bias[2:3, :], acc[2:3, :],
        ],
    )


def encoder_self_back(table, flags, bias, dz, rows, got, joined, mixed, stats, copies_grad, weights, small, ff_bias, ff_rows, last_bias, target_grad, count, after=()):
    half = half_rows(count)
    outs = (shaped(half, D, BF), shaped(half, D, BF), shaped(T, D, BF), shaped(T, D, BF))
    return kernel_call(
        encoder_self_back_kernel,
        outs,
        (table, flags, dz, Raw(rows), *map(Raw, got), *map(Raw, weights), joined, bias, stats, mixed, copies_grad, small, ff_bias, ff_rows, last_bias, target_grad),
        scalars=2,
        scratch=[
            pltpu.VMEM((T, D), BF), pltpu.VMEM((D, 3 * D), BF), pltpu.VMEM((D, D), BF),
            pltpu.VMEM((8, D), F32), pltpu.VMEM((T, D), BF), pltpu.VMEM((T, D), BF), pltpu.VMEM((T, D), BF),
            pltpu.VMEM((T, 3 * D), BF), pltpu.SemaphoreType.DMA((3,)),
        ],
        flops=18 * FLOP_UNIT,
        after=after,
        hold=True,
    )


def start(*copies):
    for source, target, sem in copies:
        pltpu.make_async_copy(source, target, sem).start()


def fetch_self(layer, flags, own_in, own_out, half, rest, to_in, to_out, sems):
    own = flags[0, 0] == layer

    def other(low, high):
        start(
            (high.at[rows_at(D), :], to_out, sems.at[1]),
            (low.at[rows_at(0), :], to_in.at[:, rows_at(0)], sems.at[0]),
            (low.at[rows_at(D), :], to_in.at[:, rows_at(D)], sems.at[0]),
            (high.at[rows_at(0), :], to_in.at[:, rows_at(2 * D)], sems.at[0]),
        )

    pl.when(own)(lambda: start((own_out, to_out, sems.at[1]), (own_in, to_in, sems.at[0])))
    pl.when(jnp.logical_not(own) & (flags[0, 1] == 0))(lambda: other(half, rest))
    pl.when(jnp.logical_not(own) & (flags[0, 1] != 0))(lambda: other(rest, half))
    return Landing(to_in, sems.at[0]), Landing(to_out, sems.at[1])


def fetch_rest(layer, flags, own_cross, own_expand, own_contract, rest, half, last, cross, expand, contract, sems):
    own = flags[0, 0] == layer

    def other(low, high):
        copies = [(rest.at[rows_at((2 + j) * D), :], expand.at[:, rows_at(j * D)], 1) for j in range(2)] if expand is not None else []
        copies += [(low.at[rows_at(j * D), :], expand.at[:, rows_at((2 + j) * D)], 1) for j in range(2)] if expand is not None else []
        if contract is not None:
            copies.append((low.at[rows_at(2 * D), :], contract.at[rows_at(0), :], 2))
            copies.append((high, contract.at[rows_at(D, 3 * D), :], 2))
        if cross is not None:
            copies += [(rest.at[rows_at(j * D), :], cross.at[:, rows_at(j * D)], 0) for j in range(2)]
        start(*((source, target, sems.at[i]) for source, target, i in copies))

    pairs = ((own_cross, cross, 0), (own_expand, expand, 1), (own_contract, contract, 2))
    pl.when(own)(lambda: start(*((source, target, sems.at[i]) for source, target, i in pairs if target is not None)))
    pl.when(jnp.logical_not(own) & (flags[0, 1] == 0))(lambda: other(half, last))
    pl.when(jnp.logical_not(own) & (flags[0, 1] != 0))(lambda: other(last, half))
    return tuple(ref if ref is None else Landing(ref, sems.at[i]) for i, ref in enumerate((cross, expand, contract)))


PARTS = ((0, 384), (384, 640))


def row_parts(parts, to, sem):
    return [(part, to.at[rows_at(at, size), :], sem) for part, (at, size) in zip(parts, PARTS)]


def fetch_rows(flags, rows, got, source, target, sems):
    @pl.when(flags[0, 0] == 0)
    def _():
        start((rows.at[rows_at(0, T), :], source, sems.at[0]), *row_parts(got, target, sems.at[1]))

    @pl.when(flags[0, 0] != 0)
    def _():
        start(*row_parts(got, source, sems.at[0]), (rows.at[rows_at(T, T), :], target, sems.at[1]))

    return Landing(source, sems.at[0]), Landing(target, sems.at[1])


def first_kernel(
    table, flags, rows, got_0, got_1, own_in, own_out, half, rest, bias, glance, places, small, small_other,
    e_small, d_small, e_joined, e_mixed, e_stats, e_z, x, d_joined, d_mixed, d_stats, d_z,
    source, target, e_in, e_out, d_in, d_out, wide, copied, sems,
):
    source, target = fetch_rows(flags, rows, (got_0, got_1), source, target, sems.at[pl.ds(0, 2)])
    e_in, e_out = fetch_self(0, flags, own_in, own_out, half, rest, e_in, e_out, sems.at[pl.ds(2, 2)])
    arrive()
    d_in, d_out = fetch_self(1, flags, own_in, own_out, half, rest, d_in, d_out, sems.at[pl.ds(4, 2)])

    @pl.when(flags[0, 0] == 0)
    def _():
        e_small[0:13, :], d_small[0:13, :] = small[...], small_other[...]

    @pl.when(flags[0, 0] != 0)
    def _():
        e_small[0:13, :], d_small[0:13, :] = small_other[...], small[...]

    encoder_self_kernel(table, bias, source, e_in, e_out, e_small, e_joined, e_mixed, e_stats, e_z, wide)
    leave(e_z)
    decoder_self_kernel(
        table, bias, source, target, glance, places, d_in, d_out, d_small, x, d_joined, d_mixed, d_stats, d_z, copied
    )


def first(table, flags, bias, glance, places, rows, got, weights, small, small_other):
    layer = (shaped(T, 3 * D, BF), shaped(T, D, BF), STATS, shaped(T, D, F32))
    outs = (shaped(16, D, F32), shaped(16, D, F32), *layer, shaped(T, D, BF), *layer)
    return kernel_call(
        first_kernel,
        outs,
        (table, flags, Raw(rows), *map(Raw, got), *map(Raw, weights), bias, glance, places, small, small_other),
        scalars=2,
        scratch=[
            pltpu.VMEM((T, D), BF), pltpu.VMEM((T, D), BF),
            pltpu.VMEM((D, 3 * D), BF), pltpu.VMEM((D, D), BF), pltpu.VMEM((D, 3 * D), BF), pltpu.VMEM((D, D), BF),
            pltpu.VMEM((T, D), F32), pltpu.VMEM((T, D), BF), pltpu.SemaphoreType.DMA((6,)),
        ],
        flops=24 * FLOP_UNIT,
        weight=0,
        hold=True,
    )


def middle_kernel(
    table, flags, e_z1, own_cross, own_expand, own_contract, rest, half, last, bias, d_z1, cotangent, e_small, d_small,
    hidden, e_z2, mine, theirs, kept, sent, ff_bias, ff_rows, cross_bias, dstates, dz1,
    e_cross, e_expand, e_contract, d_cross, d_expand, d_contract,
    active, states, queries, mixed, stats, d_z2, wide, inner, value_b, dzb, dz2, sems,
):
    own = (own_cross, own_expand, own_contract, rest, half, last)
    e_cross, e_expand, e_contract = fetch_rest(0, flags, *own, e_cross, e_expand, e_contract, sems.at[pl.ds(0, 3)])
    arrive()
    d_cross, d_expand, d_contract = fetch_rest(1, flags, *own, d_cross, d_expand, d_contract, sems.at[pl.ds(3, 3)])
    encoder_ff_kernel(flags, e_z1, e_expand, e_contract, e_cross, e_small, hidden, e_z2, mine, theirs, states, active)
    decoder_cross_kernel(table, bias, d_z1, states, d_cross, d_small, queries, mixed, stats, d_z2, wide)
    decoder_ff_kernel(
        flags, d_z2, d_expand, d_contract, d_small, cotangent, mine, theirs, kept, sent, ff_bias, ff_rows, dz2,
        active, inner, value_b, wide, dzb,
    )
    decoder_cross_back_kernel(
        table, flags, bias, dz2, d_z1, queries, states, mixed, stats, d_cross, d_small, kept, sent, cross_bias, dstates, dz1,
        value_b, dzb, active.at[:, rows_at(0)], active.at[:, rows_at(D)],
    )


def middle(table, flags, bias, e_z1, d_z1, weights, cotangent, e_small, d_small):
    low, high = shaped(T, D, BF), shaped(T, D, F32)
    outs = (
        shaped(T, FF, BF), high, low, low, shaped(FF + D, D, BF), shaped(FF + D, D, BF),
        shaped(8, D, F32), shaped(8, D, F32), shaped(8, D, F32), shaped(T, 2 * D, BF), high,
    )
    weight_room = [pltpu.VMEM((D, 2 * D), BF), pltpu.VMEM((D, FF), BF), pltpu.VMEM((FF, D), BF)]
    return kernel_call(
        middle_kernel,
        outs,
        (table, flags, e_z1, *map(Raw, weights), bias, d_z1, cotangent, e_small, d_small),
        scalars=2,
        scratch=weight_room * 2
        + [
            pltpu.VMEM((T, FF), BF), pltpu.VMEM((T, 2 * D), BF), pltpu.VMEM((T, D), BF), pltpu.VMEM((T, D), BF),
            pltpu.VMEM(STATS.shape, F32), pltpu.VMEM((T, D), F32), pltpu.VMEM((T, D), F32), pltpu.VMEM((T, FF), BF),
            pltpu.VMEM((T, D), BF), pltpu.VMEM((T, D), BF), pltpu.VMEM((T, D), F32), pltpu.SemaphoreType.DMA((6,)),
        ],
        flops=54 * FLOP_UNIT,
        room_for=62,
        hold=True,
    )


def swapped(value, axis, partner):
    count = lax.axis_size(axis)
    return lax.ppermute(value, axis, [(i, partner(i)) for i in range(count)])


def swapped_pipe(value):
    return swapped(value, "pipe", lambda i: 1 - i)


def added(first, second):
    return (first.astype(F32) + second.astype(F32)).astype(BF)


def gate(values, after):
    anywhere = pl.BlockSpec(memory_space=pl.ANY)
    return pl.pallas_call(
        lambda *refs: None,
        out_shape=tuple(jax.ShapeDtypeStruct(value.shape, value.dtype) for value in values),
        in_specs=[anywhere] * (len(values) + len(after)),
        out_specs=(anywhere,) * len(values),
        input_output_aliases={i: i for i in range(len(values))},
        cost_estimate=pl.CostEstimate(flops=0, bytes_accessed=0, transcendentals=0),
    )(*values, *after)


def halve_kernel(step, pairs, flags, *refs):
    ins, (kept_out, sent_out) = refs[: 2 * pairs], refs[2 * pairs :]
    bit = flags[0, 1 + step]
    slot = 0
    for i in range(pairs):
        kept, got = ins[2 * i], ins[2 * i + 1]
        half = kept.shape[1] // 2
        for j in range(kept.shape[0]):
            for out, side in ((kept_out, bit), (sent_out, 1 - bit)):
                at = pl.ds(pl.multiple_of(side * half, 16), half)
                out[slot] = added(kept[j, at, :], got[j, at, :])
            slot += 1


def double_kernel(step, flags, own, got, out):
    half = own.shape[0]
    bit = flags[0, 1 + step]
    out[pl.ds(pl.multiple_of(bit * half, 16), half), :] = own[...]
    out[pl.ds(pl.multiple_of((1 - bit) * half, 16), half), :] = got[...]


def across_kernel(pairs, flags, *refs):
    ins, (keep, send) = refs[: 2 * pairs], refs[2 * pairs :]
    sums = [added(ins[2 * i][j], ins[2 * i + 1][j]) for i in range(pairs) for j in range(ins[2 * i].shape[0])]

    @pl.when(flags[0, 0] == 0)
    def _():
        keep[...], send[...] = sums[0], sums[1]

    @pl.when(flags[0, 0] != 0)
    def _():
        keep[...], send[...] = sums[1], sums[0]


def add_kernel(*refs):
    total = refs[0][...].astype(F32)
    for ref in refs[1:-1]:
        total = total + ref[...].astype(F32)
    refs[-1][...] = total.astype(BF)


def corner_kernel(step, flags, kept, got, *outs):
    half = kept.shape[1] // 2
    side, bit = flags[0, 0], flags[0, 1 + step]
    quarters = ((side, bit), (side, 1 - bit), (1 - side, bit), (1 - side, 1 - bit))
    for out, (layer, part) in zip(outs, quarters):
        at = (pl.ds(layer, 1), pl.ds(pl.multiple_of(part * half, 16), half), slice(None))
        out[...] = added(kept[at], got[at])[0]


class Steps:
    def __init__(self):
        count = lax.axis_size("dp")
        bits = list(range(1, (count - 1).bit_length()))
        cut = (len(bits) + 1) // 3
        orders = (bits, bits[cut : 2 * cut] + bits[:cut] + bits[2 * cut :])
        index = lax.axis_index("dp")
        core = index & 1
        self.partners = [lambda i: i ^ 1]
        self.bits = [core]
        for pair in zip(*orders):
            self.partners.append(lambda i, pair=pair: i ^ (1 << pair[i & 1]))
            self.bits.append((index >> jnp.where(core == 0, *pair)) & 1)
        self.core, self.count, self.last = core, count, len(bits)
        self.place = 0
        for bit in self.bits:
            self.place = self.place * 2 + bit
        self.flags = jnp.stack([lax.axis_index("pipe")] + self.bits).astype(jnp.int32).reshape(1, -1)

    def swap(self, value, step):
        return swapped(value, "dp", self.partners[step])

    def halve(self, step, *pairs, after=()):
        many = sum(kept.shape[0] for kept, _ in pairs)
        shape = jax.ShapeDtypeStruct((many, pairs[0][0].shape[1] // 2, D), BF)
        operands = [x for pair in pairs for x in pair]
        return kernel_call(
            functools.partial(halve_kernel, step + 1, len(pairs)), (shape, shape), (self.flags, *operands), scalars=1, after=after, direct=True
        )

    def double(self, step, own, got, after=(), weight=20):
        out = (shaped(2 * own.shape[0], D, BF),)
        return kernel_call(functools.partial(double_kernel, step), out, (self.flags, own, got), scalars=1, after=after, direct=True, weight=weight)[0]

    def half_gathered(self, value, afters):
        parts = []
        for step in range(self.last, 0, -1):
            after = afters[step - 1] if step <= len(afters) else ()
            value = self.double(step, value, self.swap(value, step), after=after, weight=0)
            parts.append(value)
        return parts

    def crossed(self, pairs, after):
        shape = shaped(*pairs[0][0].shape[1:], BF)
        operands = [x for pair in pairs for x in pair]
        kept, sent = kernel_call(
            functools.partial(across_kernel, len(pairs)), (shape, shape), (self.flags, *operands), scalars=1, after=after, direct=True
        )
        return kept, swapped_pipe(sent)

    def cornered(self, kept, got, after):
        shape = shaped(kept.shape[1] // 2, D, BF)
        own, *sent = kernel_call(
            functools.partial(corner_kernel, self.last), (shape,) * 4, (self.flags, kept, got), scalars=1, after=after, direct=True
        )
        partner = self.partners[self.last]
        pairs = [(p * self.count + i, (1 - p) * self.count + partner(i)) for p in range(2) for i in range(self.count)]
        return own, self.swap(sent[0], self.last), swapped_pipe(sent[1]), lax.ppermute(sent[2], ("pipe", "dp"), pairs)

    def doubled(self, parts, spill, outs):
        after = yield parts[0]
        (value,) = kernel_call(add_kernel, (shaped(*parts[0].shape, BF),), parts, after=after, direct=True)
        for step in range(self.last, 0, -1):
            got = self.swap(value, step)
            after = yield value
            value = self.double(step, value, got, after=after)
        got = self.swap(value, 0)
        after = yield value
        yield tuple(kernel_call(spill, outs, (self.flags, value, got), scalars=1, after=after, stay=True, room_for=28))


def by_core(flags, first, second, body):
    pl.when(flags[0, 1] == 0)(lambda: body(first, second))
    pl.when(flags[0, 1] != 0)(lambda: body(second, first))


def spill_ff_kernel(flags, own, other, expand, contract, cross):
    def columns(low, high):
        for j in range(FF // D):
            expand[:, rows_at(j * D)] = low[rows_at(j * D), :].astype(F32)

    def rows(low, high):
        for j in range(FF // D):
            contract[rows_at(j * D), :] = high[rows_at(j * D), :].astype(F32)

    def pair(low, high):
        cross[:, rows_at(0)] = low[rows_at(FF), :].astype(F32)
        cross[:, rows_at(D)] = high[rows_at(FF), :].astype(F32)

    for ref, fill in ((expand, columns), (contract, rows), (cross, pair)):
        by_core(flags, own, other, fill)
        leave(ref)


def spill_rest_kernel(flags, own, other, joined, out, expand_bias, branch, gain, shift):
    def columns(low, high):
        for column, (ref, block) in enumerate(((low, 0), (low, 1), (high, 0))):
            joined[:, rows_at(column * D)] = ref[rows_at(block * D), :].astype(F32)

    def fill(low, high):
        out[...] = high[rows_at(D), :].astype(F32)
        value = low[rows_at(2 * D, 16), :].astype(F32)
        for j in range(FF // D):
            expand_bias[0:1, rows_at(j * D)] = value[j : j + 1, :]
        for j in range(3):
            for ref, row in ((branch, 4), (gain, 7), (shift, 10)):
                ref[j] = value[row + j : row + j + 1, :]

    by_core(flags, own, other, columns)
    leave(joined)
    by_core(flags, own, other, fill)


def last_kernel(flags, expand, contract, out):
    @pl.when(flags[0, 1] == 0)
    def _():
        for j in range(2):
            out[rows_at(j * D), :] = expand[:, rows_at((2 + j) * D)]
        out[rows_at(2 * D), :] = contract[rows_at(0), :]

    @pl.when(flags[0, 1] != 0)
    def _():
        out[...] = contract[rows_at(D, 3 * D), :]


def per_device(
    embeddings, cotangent, lengths, copy_index, priority, hamming,
    self_in, self_out, cross_weight, expand, contract,
    expand_bias, branch_bias, norm_gain, norm_shift,
):
    pipe = lax.axis_index("pipe")
    leading = pipe == 0
    steps = Steps()
    flags, count = steps.flags, steps.count
    self_in, self_out, cross_weight, expand, contract = (w[0] for w in (self_in, self_out, cross_weight, expand, contract))

    rows = embeddings[0]
    small = jnp.concatenate([expand_bias.reshape(4, D), branch_bias[0], norm_gain[0], norm_shift[0]], 0)
    size = 4 * D // count

    def piece(place, blocks_of):
        block, inside = place * size // D, place * size % D
        value = lax.dynamic_slice(blocks_of[0][0], (inside, blocks_of[0][1] * D), (size, D))
        for i in range(1, 4):
            matrix, column = blocks_of[i]
            value = jnp.where(block == i, lax.dynamic_slice(matrix, (inside, column * D), (size, D)), value)
        return value

    self_piece = piece(steps.place, [(self_in, 0), (self_in, 1), (self_in, 2), (self_out, 0)])
    rest_piece = piece(lax.axis_index("dp"), [(cross_weight, 0), (cross_weight, 1), (expand, 0), (expand, 1)])
    table, bias, glance, places = row_layout(
        flags, lengths, hamming, priority.reshape(2 * T // WIN, WIN), copy_index.reshape(2 * T // WIN, WIN)
    )
    self_piece = swapped_pipe(self_piece)
    small_other = swapped_pipe(small)
    theirs = [lax.dynamic_slice_in_dim(rows, (1 - pipe) * T + at, size, 0) for at, size in PARTS]
    got = [swapped_pipe(part) for part in gate(theirs, (self_piece,))]
    self_parts = steps.half_gathered(self_piece, ((), (got[1], bias), (got[0],)))
    self_half = self_parts[-1]
    self_rest = steps.swap(self_half, 0)
    (last_piece,) = kernel_call(last_kernel, (shaped(3 * D, D, BF),), (flags, expand, contract), scalars=1, after=(self_parts[-2], small_other), direct=True, weight=0)
    last_half = swapped_pipe(last_piece)
    (rest_piece,) = gate((swapped_pipe(rest_piece),), (self_parts[0],))
    rest = lax.all_gather(rest_piece, "dp").reshape(4 * D, D)

    self_weights = (self_in, self_out, self_half, self_rest)
    (
        e_small, d_small, e_joined, e_mixed, e_stats, e_z1, x, d_joined, d_mixed, d_stats, d_z1,
    ) = first(table, flags, bias, glance, places, rows, got, self_weights, small, small_other)
    (last_half,) = gate((last_half,), (d_z1,))
    last_rest = steps.swap(last_half, 0)
    rest_weights = (cross_weight, expand, contract, rest, last_half, last_rest)
    (
        hidden, e_z2, layer_mine, layer_theirs, *dec_ff, d_ff_bias, d_ff_rows, d_cross_bias, dstates, dz1,
    ) = middle(table, flags, bias, e_z1, d_z1, rest_weights, cotangent, e_small, d_small)

    def rows_out(own, other):
        own, other = own.astype(F32), other.astype(F32)
        return jnp.where(leading, jnp.concatenate([own, other], 0), jnp.concatenate([other, own], 0))[None]

    def opened(pair):
        return [part[None] for part in pair]

    layer_other = swapped_pipe(layer_theirs)
    dec_kept, dec_sent = opened(dec_ff)
    dec_got = steps.swap(dec_sent, 0)
    *dec_self, target_grad, copies_grad = decoder_self_back(
        table, flags, bias, dz1, x, d_joined, d_mixed, d_stats, glance, places, self_weights,
        d_ff_bias, d_ff_rows, d_cross_bias, count,
    )
    dself_kept, dself_sent = opened(dec_self)
    dself_got = steps.swap(dself_sent, 0)
    (dec_got,) = gate((dec_got,), (target_grad,))
    dec_kept, dec_sent = steps.halve(0, (dec_kept, dec_got))
    dec_got = steps.swap(dec_sent, 1)
    *enc_ff, e_ff_bias, e_ff_rows, inner, dz = encoder_ff_back(
        flags, dstates, e_z1, e_z2, hidden, rest_weights, e_small, after=(dec_kept,)
    )
    enc_kept, enc_sent = opened(enc_ff)
    enc_got = steps.swap(enc_sent, 0)
    dec_got, dself_got = gate((dec_got, dself_got), (dz,))
    dec_kept, dec_sent = steps.halve(1, (dec_kept, dec_got))
    dec_got = steps.swap(dec_sent, 2)
    dself_kept, dself_sent = steps.halve(0, (dself_kept, dself_got))
    dself_got = steps.swap(dself_sent, 1)
    last_bias, e_dz1 = encoder_ff_last(flags, inner, dz, e_z1, rest_weights, e_small, after=(dec_kept, dself_kept))
    enc_got, dec_got = gate((enc_got, dec_got), (e_dz1,))
    dec_kept, dec_sent = steps.halve(2, (dec_kept, dec_got))
    dec_got = steps.swap(dec_sent, 3)
    enc_kept, enc_sent = steps.halve(0, (enc_kept, enc_got))
    enc_got = steps.swap(enc_sent, 1)
    *enc_self, grad_mine, grad_theirs = encoder_self_back(
        table, flags, bias, e_dz1, rows, got, e_joined, e_mixed, e_stats, copies_grad, self_weights, e_small,
        e_ff_bias, e_ff_rows, last_bias, target_grad, count, after=(enc_kept, dec_kept),
    )

    self_kept, self_sent = opened(enc_self)
    self_got = steps.swap(self_sent, 0)
    enc_got, dec_got, dself_got = gate((enc_got, dec_got, dself_got), (grad_mine,))

    def ff_sum():
        enc_pair, dec_pair = (enc_kept, enc_got), (dec_kept, dec_got)
        after = yield
        for step in range(1, steps.last):
            kept, sent = steps.halve(step, enc_pair, after=after)
            enc_pair = (kept, steps.swap(sent, step + 1))
            if step + 2 < steps.last:
                kept, sent = steps.halve(step + 2, dec_pair, after=(kept,))
                dec_pair = (kept, steps.swap(sent, step + 3))
            after = yield kept
        outs = (shaped(D, FF, F32), shaped(FF, D, F32), shaped(D, 2 * D, F32))
        yield from steps.doubled(steps.crossed((enc_pair, dec_pair), after), spill_ff_kernel, outs)

    def self_sum():
        pairs = [(self_kept, self_got)]
        after = yield
        for step in range(steps.last - 1):
            kept, sent = steps.halve(step, *pairs, after=after)
            pairs = [(kept, steps.swap(sent, step + 1))]
            if step == 0:
                pairs.append((dself_kept, dself_got))
            after = yield kept
        outs = (shaped(D, 3 * D, F32), shaped(D, D, F32), shaped(1, FF, F32)) + (jax.ShapeDtypeStruct((3, 1, D), F32),) * 3
        yield from steps.doubled(steps.cornered(*pairs[0], after), spill_rest_kernel, outs)

    chains = [ff_sum(), self_sum()]
    results = [None, None]
    mark = dself_got
    for chain in chains:
        next(chain)
    live = [0, 1]
    turn = 0
    while live:
        if turn == 5:
            layer = gate((layer_mine, layer_other), (mark,))
            layer_out, embedding_grad = rows_out(*layer), rows_out(*gate((grad_mine, grad_other), (mark,)))
        for i in list(live):
            extra = (layer_out, embedding_grad) if turn == 7 else ()
            value = chains[i].send((mark, *extra))
            if isinstance(value, tuple):
                results[i] = value
                live.remove(i)
                value = value[0]
            mark = value
            if turn == 0 and i == 0:
                grad_other = swapped_pipe(*gate((grad_theirs,), (mark,)))
        turn += 1
    expand_grad, contract_grad, cross_grad = results[0]
    in_grad, out_grad, *small_grads = results[1]
    return (
        layer_out,
        embedding_grad,
        in_grad[None],
        out_grad[None],
        cross_grad[None],
        expand_grad[None],
        contract_grad[None],
        small_grads[0],
        *(part.transpose(1, 0, 2) for part in small_grads[1:]),
    )


def solution(mesh):
    return jax.shard_map(
        per_device,
        mesh=mesh,
        in_specs=(
            P("pipe", "dp", None),
            P("dp", None),
            P("dp", None),
            P("dp"),
            P("dp"),
            P("dp", None),
            P("pipe", None, None),
            P("pipe", None, None),
            P("pipe", None, None),
            P("pipe", None, None),
            P("pipe", None, None),
            P("pipe", None),
            P("pipe", None, None),
            P("pipe", None, None),
            P("pipe", None, None),
        ),
        out_specs=(
            P("pipe", "dp", None),
            P("pipe", "dp", None),
            P("pipe", None, None),
            P("pipe", None, None),
            P("pipe", None, None),
            P("pipe", None, None),
            P("pipe", None, None),
            P("pipe", None),
            P("pipe", None, None),
            P("pipe", None, None),
            P("pipe", None, None),
        ),
        check_vma=False,
    )
```
